256 devices in a mesh: dp: 4 (over x_hi, core), label: 64 (over x_lo, z, y).
Axes of the slice: x: 4 (x_hi: 2, x_lo: 2; x = x_hi * 2 + x_lo), y: 4, z: 8, core: 2. Of those that a mesh axis runs over, the one named last changes fastest.
Arguments:
- embeddings: bfloat16 [2048, 768], P(('dp', 'label')), may hold values from -16 to 16
- classifier: bfloat16 [262144, 768], P('label'), may hold values from -1 to 1
- positives: int32 [2048, 5], P(('dp', 'label')), may hold values from 0 to 262143
- counts: int32 [2048], P(('dp', 'label')), may hold values from 1 to 5
Outputs:
- loss: float32 [2048], P(('dp', 'label'))
- query_grad: bfloat16 [2048, 768], P(('dp', 'label'))
- class_grad: bfloat16 [262144, 768], P('label')
The draws below stay inside these ranges and needn't reach their ends.
All inputs are finite; a program needn't handle non-finite values.
Results may differ from the reference program's by a relative error of at most 0.0095.
Values may be sent and summed in bfloat16 or wider, within the bound.
No kernel may reach another device: no remote copies, remote signals or barrier semaphores. Data moves between devices by JAX's collectives and lax.ppermute only.
A program may use at most 64 MiB of HBM per device.

```python
import jax
import jax.numpy as jnp
from jax import lax

D = 768
LAB_DEV = 4096
POS = 5
LABELS = 262144
GROUPQ = 512
QUERIES = 2048
N_DP = 4
N_LABEL = 64


def special_rows(key):
    inner = jax.random.fold_in(key, 5)
    first = jax.random.uniform(inner, (8, D), jnp.float32, -0.95, 0.95)
    noise = jax.random.uniform(jax.random.fold_in(inner, 1), (8, D), jnp.float32, -0.004, 0.004)
    paired = jnp.stack([first, 0.99 * first + noise], axis=1)
    return paired.reshape(16, D)


def drawn_rows(special):
    targets = jnp.array([120.0, 200.0, 300.0, 120.0, 200.0, 300.0], jnp.float32)
    factor = targets / (0.3008 * D)
    return special[0:12:2] * factor[:, None]


def draw_classifier(key, part):
    special = special_rows(key)
    key = jax.random.fold_in(key, 11)
    base = jnp.clip(jax.random.normal(key, (LABELS, D), jnp.float32), -6.0, 6.0) * 0.11
    return base.at[:16].set(special).astype(jnp.bfloat16)


def draw_embeddings(key, part):
    special = special_rows(key)
    aligned = drawn_rows(special)
    key = jax.random.fold_in(key, 23)
    values = jnp.clip(jax.random.normal(key, (QUERIES, D), jnp.float32), -6.0, 6.0)
    values = values.at[:6].set(aligned)
    return values.astype(jnp.bfloat16)


def place_ends(result, key, low, largest):
    longest = result.shape.index(max(result.shape))
    spots = []
    for shift in (0, 1):
        where = [jax.random.randint(jax.random.fold_in(key, axis), (), 0, length) for axis, length in enumerate(result.shape)]
        where[longest] = (where[longest] + shift) % result.shape[longest]
        spots.append(tuple(where))
    return result.at[spots[0]].set(low).at[spots[1]].set(largest)


def setup_inputs(seed: int = 0) -> dict:
    splits = jax.random.split(jax.random.key(seed), 5)
    embeddings = draw_embeddings(jax.random.fold_in(splits[4], 71), 0)
    classifier = draw_classifier(jax.random.fold_in(splits[4], 71), 0)
    positives = place_ends(jax.random.randint(splits[2], (QUERIES, POS), 0, LABELS), jax.random.fold_in(splits[2], 1), 0, LABELS - 1).astype(jnp.int32)
    counts = place_ends(jax.random.randint(splits[3], (QUERIES,), 1, POS + 1), jax.random.fold_in(splits[3], 1), 1, POS).astype(jnp.int32)
    return {"embeddings": embeddings, "classifier": classifier, "positives": positives, "counts": counts}


def group_pass(group, ids, cnt, blocks):
    fcnt = cnt.astype(jnp.float32)
    slots = jnp.arange(ids.shape[1])[None, :] < cnt[:, None]
    rows = group.shape[0]

    def stats_step(carry, item):
        top, total, possum = carry
        wblock, index = item
        scores = lax.dot_general(group, wblock, (((1,), (1,)), ((), ())), preferred_element_type=jnp.float32)
        local = ids - index * LAB_DEV
        valid = (local >= 0) & (local < LAB_DEV) & slots
        picked = jnp.take_along_axis(scores, jnp.clip(local, 0, LAB_DEV - 1).astype(jnp.int32), 1)
        possum = possum + jnp.sum(jnp.where(valid, picked, 0.0), 1)
        newtop = jnp.maximum(top, jnp.max(scores, 1))
        total = total * jnp.exp(top - newtop) + jnp.sum(jnp.exp(scores - newtop[:, None]), 1)
        return (newtop, total, possum), None

    indices = jnp.arange(N_LABEL, dtype=jnp.int32)
    init = (jnp.full((rows,), -1e30, jnp.float32), jnp.zeros((rows,), jnp.float32), jnp.zeros((rows,), jnp.float32))
    (top, total, possum), _ = lax.scan(stats_step, init, (blocks, indices))
    lse = top + jnp.log(total)
    loss = lse - possum / fcnt

    def grad_step(qgrad, item):
        wblock, index = item
        scores = lax.dot_general(group, wblock, (((1,), (1,)), ((), ())), preferred_element_type=jnp.float32)
        local = ids - index * LAB_DEV
        valid = (local >= 0) & (local < LAB_DEV) & slots
        cols = jnp.arange(LAB_DEV, dtype=jnp.int32)[None, :]
        target = jnp.zeros_like(scores)
        for slot in range(ids.shape[1]):
            hit = (cols == local[:, slot:slot + 1]) & valid[:, slot:slot + 1]
            target = target + jnp.where(hit, 1.0 / fcnt[:, None], 0.0)
        grad = (jnp.exp(scores - lse[:, None]) - target).astype(jnp.bfloat16)
        qgrad = qgrad + jnp.dot(grad, wblock, preferred_element_type=jnp.float32)
        part = lax.dot_general(grad, group, (((0,), (0,)), ((), ())), preferred_element_type=jnp.float32).astype(jnp.bfloat16)
        return qgrad, part

    qgrad, parts = lax.scan(grad_step, jnp.zeros((rows, D), jnp.float32), (blocks, indices))
    return loss, qgrad.astype(jnp.bfloat16), parts


def reference(embeddings, classifier, positives, counts):
    blocks = classifier.reshape(N_LABEL, LAB_DEV, D)
    losses = []
    qgrads = []
    summed = jnp.zeros((N_LABEL, LAB_DEV, D), jnp.float32)
    for index in range(N_DP):
        first = index * GROUPQ
        loss, qgrad, parts = group_pass(embeddings[first:first + GROUPQ], positives[first:first + GROUPQ], counts[first:first + GROUPQ], blocks)
        losses.append(loss)
        qgrads.append(qgrad)
        summed = summed + parts.astype(jnp.float32)
    class_grad = summed.reshape(LABELS, D).astype(jnp.bfloat16)
    return jnp.concatenate(losses), jnp.concatenate(qgrads), class_grad
```

```python
import functools

import jax
import jax.numpy as jnp
from jax import lax
from jax.experimental import pallas as pl
from jax.experimental.pallas import tpu as pltpu
from jax.sharding import Mesh, PartitionSpec as P

AXES = ("xh", "core", "xl", "z", "y")
SIZES = {"xh": 2, "core": 2, "xl": 2, "z": 8, "y": 4}
EXTRA = 128
POS = 5
LO, MID, HI, CNT = 0, 8, 16, 24
VMEM = pl.BlockSpec(memory_space=pltpu.VMEM)
SMEM = pl.BlockSpec(memory_space=pltpu.SMEM)
NT = (((1,), (1,)), ((), ()))
TN = (((0,), (0,)), ((), ()))
LCH = 256


def shift(x, axis, step):
    n = SIZES[axis]
    return lax.ppermute(x, axis, [(i, (i + step) % n) for i in range(n)])


def scores_kernel(own_ref, oth_ref, w_ref, e_ref, m_ref, l_ref, s_ref):
    labels, width = w_ref.shape
    for part, q_ref in enumerate((own_ref, oth_ref)):
        rows = q_ref.shape[0]
        q = q_ref[:, :width]

        def product(i, top):
            at = pl.multiple_of(i * LCH, LCH)
            s = lax.dot_general(w_ref[pl.ds(at, LCH), :], q, NT, preferred_element_type=jnp.float32)
            s_ref[pl.ds(at, LCH), :] = s
            return jnp.maximum(top, jnp.max(s.reshape(LCH // 8, 8, rows), 0))

        top = lax.fori_loop(0, labels // LCH, product, jnp.full((8, rows), -1e30, jnp.float32))
        top = jnp.max(top, 0, keepdims=True)

        def expo(i, total):
            at = pl.multiple_of(i * LCH, LCH)
            e = jnp.exp(s_ref[pl.ds(at, LCH), :] - top)
            e_ref[pl.ds(at, LCH), part * rows:(part + 1) * rows] = e.astype(jnp.bfloat16)
            return total + jnp.sum(e.reshape(LCH // 8, 8, rows), 0)

        total = lax.fori_loop(0, labels // LCH, expo, jnp.zeros((8, rows), jnp.float32))
        m_ref[part:part + 1, :] = top
        l_ref[part:part + 1, :] = top + jnp.log(jnp.sum(total, 0, keepdims=True))


def scores_call(own, oth, w):
    rows = own.shape[0]
    labels = w.shape[0]
    return pl.pallas_call(
        scores_kernel,
        out_shape=(
            jax.ShapeDtypeStruct((labels, 2 * rows), jnp.bfloat16),
            jax.ShapeDtypeStruct((2, rows), jnp.float32),
            jax.ShapeDtypeStruct((2, rows), jnp.float32),
        ),
        in_specs=[VMEM] * 3,
        out_specs=(VMEM,) * 3,
        scratch_shapes=[pltpu.VMEM((labels, rows), jnp.float32)],
        compiler_params=pltpu.CompilerParams(vmem_limit_bytes=24 * 2**20),
        cost_estimate=pl.CostEstimate(flops=4 * rows * labels * w.shape[1], bytes_accessed=labels * rows * 4, transcendentals=2 * rows * labels),
        name="scores",
    )(own, oth, w)


def hits_kernel(base_ref, *refs):
    blocks = refs[:8]
    w_ref, n_ref, key_ref, s_ref, t_ref = refs[8:]
    labels, width = w_ref.shape
    base = base_ref[0].astype(jnp.float32)
    row = lax.broadcasted_iota(jnp.int32, (8, EXTRA), 0)
    col = lax.broadcasted_iota(jnp.int32, (8, EXTRA), 1)
    digits = jnp.where(col == row + LO, 1.0, jnp.where(col == row + MID, 128.0, jnp.where(col == row + HI, 16384.0, 0.0)))
    digits = jnp.where(row < POS, digits, 0.0).astype(jnp.bfloat16)
    counting = jnp.where(col == CNT, 1.0, 0.0).astype(jnp.bfloat16)
    big = 1e9
    for b, q_ref in enumerate(blocks):
        rows = q_ref.shape[0]
        extra = q_ref[:, width:]
        ids = lax.dot_general(digits, extra, NT, preferred_element_type=jnp.float32)
        cnt = lax.dot_general(counting, extra, NT, preferred_element_type=jnp.float32)
        slot = lax.broadcasted_iota(jnp.int32, (8, rows), 0)
        lane = lax.broadcasted_iota(jnp.int32, (8, rows), 1)
        valid = (slot.astype(jnp.float32) < cnt) & (slot < POS)
        ids = jnp.where(valid, ids, -1.0)
        same = jnp.zeros((8, rows), jnp.float32)
        again = jnp.zeros((8, rows), jnp.float32)
        for j in range(POS):
            eq = jnp.where(ids == ids[j:j + 1, :], 1.0, 0.0)
            same = same + eq
            again = again + jnp.where(slot > j, eq, 0.0)
        local = ids - base
        hit = valid & (local >= 0.0) & (local < float(labels)) & (again == 0.0)
        weight = same / cnt
        keys = jnp.where(hit, (lane * 8 + slot).astype(jnp.float32) * float(labels) + local, big)
        n = jnp.sum(jnp.where(hit, 1.0, 0.0)).astype(jnp.int32)
        n_ref[b] = n

        def step(i, keys):
            kf = jnp.min(keys)
            this = keys == kf
            k = kf.astype(jnp.int32)
            label = lax.rem(k, labels)
            query = lax.div(k, labels * 8)
            qat = pl.multiple_of(lax.div(query, 16) * 16, 16)
            lat = pl.multiple_of(lax.div(label, 16) * 16, 16)
            s16 = lax.dot_general(q_ref[pl.ds(qat, 16), :width], w_ref[pl.ds(lat, 16), :], NT, preferred_element_type=jnp.float32)
            r16 = lax.broadcasted_iota(jnp.int32, (16, 16), 0)
            c16 = lax.broadcasted_iota(jnp.int32, (16, 16), 1)
            at = b * rows * POS + i
            key_ref[at] = k
            s_ref[at] = jnp.sum(jnp.where((r16 == query - qat) & (c16 == label - lat), s16, 0.0))
            t_ref[at] = jnp.sum(jnp.where(this, weight, 0.0))
            return jnp.where(this, big, keys)

        lax.fori_loop(0, n, step, keys)


def hits_call(base, blocks, w):
    total = 8 * blocks[0].shape[0] * POS
    return pl.pallas_call(
        hits_kernel,
        out_shape=(
            jax.ShapeDtypeStruct((8,), jnp.int32),
            jax.ShapeDtypeStruct((total,), jnp.int32),
            jax.ShapeDtypeStruct((total,), jnp.float32),
            jax.ShapeDtypeStruct((total,), jnp.float32),
        ),
        in_specs=[SMEM] + [VMEM] * 9,
        out_specs=(SMEM,) * 4,
        compiler_params=pltpu.CompilerParams(vmem_limit_bytes=16 * 2**20),
        cost_estimate=pl.CostEstimate(flops=10**9, bytes_accessed=2**23, transcendentals=0),
        name="hits",
    )(base, *blocks, w)


def query_kernel(xh_ref, n_ref, key_ref, s_ref, t_ref, lse_ref, m_ref, e0, e1, e2, e3, w_ref, p0, p1, p2, p3, own_ref, oth_ref, pos_ref):
    labels, width = w_ref.shape
    rows = e0.shape[1] // 2
    xh = xh_ref[0]
    half = rows // 2
    pos_ref[...] = jnp.zeros_like(pos_ref)
    for d, (e_ref, p_ref) in enumerate(((e0, p0), (e1, p1), (e2, p2), (e3, p3))):
        scale = [jnp.exp(m_ref[2 * d + k:2 * d + k + 1, :] - lse_ref[2 * d + k:2 * d + k + 1, :]) for k in range(2)]

        def scaled(i, carry):
            at = pl.multiple_of(i * LCH, LCH)
            for k in range(2):
                cols = slice(k * rows, (k + 1) * rows)
                p_ref[pl.ds(at, LCH), cols] = (e_ref[pl.ds(at, LCH), cols].astype(jnp.float32) * scale[k]).astype(jnp.bfloat16)
            return carry

        lax.fori_loop(0, labels // LCH, scaled, 0)
        for k in range(2):
            b = 2 * d + k

            def patch(i, carry):
                at = b * rows * POS + i
                key = key_ref[at]
                s = s_ref[at]
                label = lax.rem(key, labels)
                rest = lax.div(key, labels)
                slot = lax.rem(rest, 8)
                query = lax.div(rest, 8)
                lat = pl.multiple_of(lax.div(label, 16) * 16, 16)
                qhi = lax.div(query, half)
                qlo = lax.rem(query, half)
                qat = pl.multiple_of(qhi * half, half)
                spot = (pl.ds(lat, 16), pl.ds(pl.multiple_of(k * rows + qhi * half, half), half))
                value = jnp.exp(s - lse_ref[b:b + 1, pl.ds(qat, half)]) - t_ref[at]
                r = lax.broadcasted_iota(jnp.int32, (16, half), 0)
                c = lax.broadcasted_iota(jnp.int32, (16, half), 1)
                old = p_ref[spot].astype(jnp.float32)
                p_ref[spot] = jnp.where((r == label - lat) & (c == qlo), value, old).astype(jnp.bfloat16)

                @pl.when(qhi == xh)
                def _():
                    c1 = lax.broadcasted_iota(jnp.int32, (1, EXTRA), 1)
                    times = t_ref[at] * 1.0
                    full = jnp.full((1, EXTRA), s * times, jnp.float32)
                    high = full.astype(jnp.bfloat16).astype(jnp.float32)
                    mid = (full - high).astype(jnp.bfloat16).astype(jnp.float32)
                    low = full - high - mid
                    put = jnp.where(c1 == slot, high, jnp.where(c1 == slot + 8, mid, jnp.where(c1 == slot + 16, low, 0.0)))
                    into = (k, pl.ds(d * half + qlo, 1), slice(None))
                    pos_ref[into] = pos_ref[into] + put

                return carry

            lax.fori_loop(0, n_ref[b], patch, 0)
        mine = pl.multiple_of(xh * half, half)
        both = jnp.concatenate([p_ref[:, pl.ds(mine, half)], p_ref[:, pl.ds(pl.multiple_of(rows + xh * half, half), half)]], 1)
        u = lax.dot_general(both, w_ref[...], TN, preferred_element_type=jnp.float32)
        for k, out in enumerate((own_ref, oth_ref)):
            out[d * half:(d + 1) * half, :width] = u[k * half:(k + 1) * half].astype(jnp.bfloat16)
            out[d * half:(d + 1) * half, width:] = pos_ref[k, d * half:(d + 1) * half, :].astype(jnp.bfloat16)


def query_call(xh, hits, lse, m, es, w):
    labels, width = w.shape
    rows = es[0].shape[1] // 2
    out = jax.ShapeDtypeStruct((4 * rows // 2, width + EXTRA), jnp.bfloat16)
    res = pl.pallas_call(
        query_kernel,
        out_shape=tuple(jax.ShapeDtypeStruct(e.shape, e.dtype) for e in es) + (out, out),
        in_specs=[SMEM] * 5 + [VMEM] * 7,
        out_specs=(VMEM,) * 6,
        scratch_shapes=[pltpu.VMEM((2, 4 * rows // 2, EXTRA), jnp.float32)],
        compiler_params=pltpu.CompilerParams(vmem_limit_bytes=40 * 2**20),
        cost_estimate=pl.CostEstimate(flops=8 * rows * labels * width, bytes_accessed=2**24, transcendentals=0),
        name="query_part",
    )(xh, *hits, lse, m, *es, w)
    return res[:4], res[4], res[5]


def class_kernel(core_ref, p0, p1, p2, p3, *refs):
    blocks = refs[:8]
    out_ref = refs[8]
    rows = blocks[0].shape[0]
    width = out_ref.shape[1]
    acc = None
    for d, p_ref in enumerate((p0, p1, p2, p3)):
        for k in range(2):
            term = jnp.dot(p_ref[:, k * rows:(k + 1) * rows], blocks[2 * d + k][:, :width], preferred_element_type=jnp.float32)
            acc = term if acc is None else acc + term
    out_ref[...] = acc.astype(jnp.bfloat16)


def class_call(core, ps, blocks, width):
    labels = ps[0].shape[0]
    steps = labels // LCH
    rows = blocks[0].shape[0]
    whole = lambda i, c: (0, 0)
    return pl.pallas_call(
        class_kernel,
        out_shape=jax.ShapeDtypeStruct((2 * labels, width), jnp.bfloat16),
        grid_spec=pltpu.PrefetchScalarGridSpec(
            num_scalar_prefetch=1,
            grid=(steps,),
            in_specs=[pl.BlockSpec((LCH, 2 * rows), lambda i, c: (i, 0))] * 4 + [pl.BlockSpec(blocks[0].shape, whole)] * 8,
            out_specs=pl.BlockSpec((LCH, width), lambda i, c: (c[0] * steps + i, 0)),
        ),
        compiler_params=pltpu.CompilerParams(vmem_limit_bytes=32 * 2**20),
        cost_estimate=pl.CostEstimate(flops=16 * rows * labels * width, bytes_accessed=2**24, transcendentals=0),
        name="class_part",
    )(core, *ps, *blocks)


def lse_of(parts, axis=None):
    if axis is None:
        top = functools.reduce(jnp.maximum, parts)
        return top + jnp.log(functools.reduce(jnp.add, [jnp.exp(p - top) for p in parts]))
    top = jnp.max(parts, axis)
    return top + jnp.log(jnp.sum(jnp.exp(parts - jnp.expand_dims(top, axis)), axis))


def body(embeddings, classifier, positives, counts):
    q_dev, width = embeddings.shape
    labels = classifier.shape[0] // 2
    xh, core, xl, z, y = (lax.axis_index(a) for a in AXES)
    rank = (xl * 8 + z) * 4 + y
    base = (rank * 2 + core) * labels

    blank = jnp.zeros((q_dev, 8 - POS), jnp.int32)
    extra = jnp.concatenate(
        [positives & 127, blank, (positives >> 7) & 127, blank, positives >> 14, blank, counts[:, None], jnp.zeros((q_dev, EXTRA - CNT - 1), jnp.int32)],
        1,
    ).astype(jnp.bfloat16)
    sent = jnp.concatenate([embeddings, extra], 1)
    copies = jnp.broadcast_to(sent[None], (32, q_dev, width + EXTRA)).reshape(32 * q_dev, width + EXTRA)
    mine = lax.all_to_all(copies, ("xh", "xl", "z"), 0, 0, tiled=True)
    own = [mine] + [shift(mine, "y", -d) for d in range(1, 4)]
    oth = [shift(b, "core", 1) for b in own]
    w = lax.dynamic_slice_in_dim(classifier, core * labels, labels)
    rows = mine.shape[0]

    es, ms, ls = zip(*[scores_call(a, b, w) for a, b in zip(own, oth)])
    blocks = [b for pair in zip(own, oth) for b in pair]
    hits = hits_call(base[None], blocks, w)
    m = jnp.concatenate(ms, 0)
    stat = jnp.concatenate(ls, 0)
    swapped = shift(stat, "core", 1).reshape(4, 2, rows)[:, ::-1].reshape(8, rows)
    stat = lse_of([stat, swapped])
    stat = lse_of([stat] + [jnp.roll(shift(stat, "y", -d), 2 * d, 0) for d in range(1, 4)])
    lse = lse_of(lax.all_to_all(jnp.broadcast_to(stat[None], (16, 8, rows)), ("xl", "z"), 0, 0, tiled=True), 0)

    ps, u_own, u_oth = query_call(xh[None], hits, lse, m, es, w)
    f32 = lambda a: a.astype(jnp.float32)
    u = (f32(u_own) + f32(shift(u_oth, "core", 1))).astype(jnp.bfloat16)
    part = u.shape[0] // 4
    u = [u[d * part:(d + 1) * part] for d in range(4)]
    total = f32(u[0])
    for d in range(1, 4):
        total = total + f32(shift(u[d], "y", d))
    got = lax.all_to_all(total.astype(jnp.bfloat16), ("xl", "z"), 0, 0, tiled=True)
    final = jnp.sum(f32(got).reshape(16, q_dev, width + EXTRA), 0)
    query_grad = final[:, :width].astype(jnp.bfloat16)
    pos_mean = jnp.sum(final[:, width:width + 24], 1)
    at = ((xh * 2 + xl) * 8 + z) * q_dev
    loss = lax.dynamic_slice(lse, (0, at), (1, q_dev))[0] - pos_mean

    halves = class_call(core[None], ps, blocks, width)
    mine_half = lax.dynamic_slice_in_dim(halves, core * labels, labels)
    class_grad = lax.dynamic_update_slice_in_dim(halves, shift(mine_half, "core", 1), (1 - core) * labels, 0)
    return loss, query_grad, class_grad


def solution(mesh):
    fine = Mesh(mesh.devices.reshape(tuple(SIZES[a] for a in AXES)), AXES)
    split = P(AXES, None)
    lab = P(("xl", "z", "y"), None)
    return jax.shard_map(
        body,
        mesh=fine,
        in_specs=(split, lab, split, P(AXES)),
        out_specs=(P(AXES), split, lab),
        check_vma=False,
    )
```

```python
import functools

import jax
import jax.numpy as jnp
from jax import lax
from jax.experimental import pallas as pl
from jax.experimental.pallas import tpu as pltpu
from jax.sharding import Mesh, PartitionSpec as P

AXES = ("xh", "core", "xl", "z", "y")
SIZES = {"xh": 2, "core": 2, "xl": 2, "z": 8, "y": 4}
EXTRA = 128
POS = 5
LO, MID, HI, CNT = 0, 8, 16, 24
VMEM = pl.BlockSpec(memory_space=pltpu.VMEM)
SMEM = pl.BlockSpec(memory_space=pltpu.SMEM)
NT = (((1,), (1,)), ((), ()))
TN = (((0,), (0,)), ((), ()))
LCH = 256
PROD = 1024
EXPO = 128


def shift(x, axis, step):
    n = SIZES[axis]
    return lax.ppermute(x, axis, [(i, (i + step) % n) for i in range(n)])


def scores_kernel(own_ref, oth_ref, w_ref, e_ref, m_ref, l_ref, s_ref, qt_ref):
    labels, width = w_ref.shape
    rows = own_ref.shape[0]
    both = 2 * rows
    qt_ref[:, :rows] = own_ref[:, :width].T
    qt_ref[:, rows:] = oth_ref[:, :width].T

    def product(i, top):
        at = pl.multiple_of(i * PROD, PROD)
        s = jnp.dot(w_ref[pl.ds(at, PROD), :], qt_ref[...], preferred_element_type=jnp.float32)
        s_ref[pl.ds(at, PROD), :] = s
        return jnp.maximum(top, jnp.max(s.reshape(PROD // 16, 16, both), 0))

    top = lax.fori_loop(0, labels // PROD, product, jnp.full((16, both), -1e30, jnp.float32))
    top = jnp.max(top, 0, keepdims=True)

    def expo(i, total):
        at = pl.multiple_of(i * EXPO, EXPO)
        e = jnp.exp(s_ref[pl.ds(at, EXPO), :] - top)
        e_ref[pl.ds(at, EXPO), :] = e.astype(jnp.bfloat16)
        return total + jnp.sum(e.reshape(EXPO // 16, 16, both), 0)

    total = lax.fori_loop(0, labels // EXPO, expo, jnp.zeros((16, both), jnp.float32))
    m_ref[...] = top
    l_ref[...] = top + jnp.log(jnp.sum(total, 0, keepdims=True))


def scores_call(own, oth, w):
    rows = own.shape[0]
    labels, width = w.shape
    line = jax.ShapeDtypeStruct((1, 2 * rows), jnp.float32)
    return pl.pallas_call(
        scores_kernel,
        out_shape=(jax.ShapeDtypeStruct((labels, 2 * rows), jnp.bfloat16), line, line),
        in_specs=[VMEM] * 3,
        out_specs=(VMEM,) * 3,
        scratch_shapes=[pltpu.VMEM((labels, 2 * rows), jnp.float32), pltpu.VMEM((width, 2 * rows), jnp.bfloat16)],
        compiler_params=pltpu.CompilerParams(vmem_limit_bytes=18 * 2**20),
        cost_estimate=pl.CostEstimate(flops=4 * rows * labels * width, bytes_accessed=labels * rows * 4, transcendentals=2 * rows * labels),
        name="scores",
    )(own, oth, w)


def hits_kernel(base_ref, *refs):
    blocks = refs[:8]
    w_ref, n_ref, key_ref, s_ref, t_ref = refs[8:]
    labels, width = w_ref.shape
    base = base_ref[0].astype(jnp.float32)
    row = lax.broadcasted_iota(jnp.int32, (8, EXTRA), 0)
    col = lax.broadcasted_iota(jnp.int32, (8, EXTRA), 1)
    digits = jnp.where(col == row + LO, 1.0, jnp.where(col == row + MID, 128.0, jnp.where(col == row + HI, 16384.0, 0.0)))
    digits = jnp.where(row < POS, digits, 0.0).astype(jnp.bfloat16)
    counting = jnp.where(col == CNT, 1.0, 0.0).astype(jnp.bfloat16)
    big = 1e9
    rows = blocks[0].shape[0]
    slot = lax.broadcasted_iota(jnp.int32, (8, rows), 0)
    lane = lax.broadcasted_iota(jnp.int32, (8, rows), 1)
    keys, weights, most = [], [], jnp.int32(0)
    for b, q_ref in enumerate(blocks):
        extra = q_ref[:, width:]
        ids = lax.dot_general(digits, extra, NT, preferred_element_type=jnp.float32)
        cnt = lax.dot_general(counting, extra, NT, preferred_element_type=jnp.float32)
        valid = (slot.astype(jnp.float32) < cnt) & (slot < POS)
        ids = jnp.where(valid, ids, -1.0)
        same = jnp.zeros((8, rows), jnp.float32)
        again = jnp.zeros((8, rows), jnp.float32)
        for j in range(POS):
            eq = jnp.where(ids == ids[j:j + 1, :], 1.0, 0.0)
            same = same + eq
            again = again + jnp.where(slot > j, eq, 0.0)
        local = ids - base
        hit = valid & (local >= 0.0) & (local < float(labels)) & (again == 0.0)
        weights.append(same / cnt)
        keys.append(jnp.where(hit, (lane * 8 + slot).astype(jnp.float32) * float(labels) + local, big))
        n = jnp.sum(jnp.where(hit, 1.0, 0.0)).astype(jnp.int32)
        n_ref[b] = n
        most = jnp.maximum(most, n)
    r16 = lax.broadcasted_iota(jnp.int32, (16, 16), 0)
    c16 = lax.broadcasted_iota(jnp.int32, (16, 16), 1)

    def step(i, keys):
        left = []
        for b in range(8):
            kf = jnp.min(keys[b])
            this = keys[b] == kf
            k = jnp.where(kf < big, kf, 0.0).astype(jnp.int32)
            label = k & (labels - 1)
            query = lax.div(k, 8 * labels)
            qat = pl.multiple_of((query >> 4) << 4, 16)
            lat = pl.multiple_of((label >> 4) << 4, 16)
            s16 = lax.dot_general(blocks[b][pl.ds(qat, 16), :width], w_ref[pl.ds(lat, 16), :], NT, preferred_element_type=jnp.float32)
            at = b * rows * POS + i
            key_ref[at] = k
            s_ref[at] = jnp.sum(jnp.where((r16 == query - qat) & (c16 == label - lat), s16, 0.0))
            t_ref[at] = jnp.sum(jnp.where(this, weights[b], 0.0))
            left.append(jnp.where(this, big, keys[b]))
        return tuple(left)

    lax.fori_loop(0, most, step, tuple(keys))


def hits_call(base, blocks, w):
    total = 8 * blocks[0].shape[0] * POS
    return pl.pallas_call(
        hits_kernel,
        out_shape=(
            jax.ShapeDtypeStruct((8,), jnp.int32),
            jax.ShapeDtypeStruct((total,), jnp.int32),
            jax.ShapeDtypeStruct((total,), jnp.float32),
            jax.ShapeDtypeStruct((total,), jnp.float32),
        ),
        in_specs=[SMEM] + [VMEM] * 9,
        out_specs=(SMEM,) * 4,
        compiler_params=pltpu.CompilerParams(vmem_limit_bytes=16 * 2**20),
        cost_estimate=pl.CostEstimate(flops=10**9, bytes_accessed=2**23, transcendentals=0),
        name="hits",
    )(base, *blocks, w)


def query_kernel(at_ref, n_ref, key_ref, s_ref, t_ref, lse_ref, m_ref, e0, e1, e2, e3, w_ref, p0, p1, p2, p3, own_ref, oth_ref, pos_ref):
    labels, width = w_ref.shape
    rows = e0.shape[1] // 2
    xh, y = at_ref[0], at_ref[1]
    half = rows // 2
    ps = (p0, p1, p2, p3)
    pos_ref[...] = jnp.zeros_like(pos_ref)
    for d, (e_ref, p_ref) in enumerate(zip((e0, e1, e2, e3), ps)):
        scale = jnp.exp(m_ref[d:d + 1, :] - lse_ref[d:d + 1, :])

        def scaled(i, carry):
            at = pl.multiple_of(i * 64, 64)
            p_ref[pl.ds(at, 64), :] = (e_ref[pl.ds(at, 64), :].astype(jnp.float32) * scale).astype(jnp.bfloat16)
            return carry

        lax.fori_loop(0, labels // 64, scaled, 0)

    r = lax.broadcasted_iota(jnp.int32, (16, half), 0)
    c = lax.broadcasted_iota(jnp.int32, (16, half), 1)
    c1 = lax.broadcasted_iota(jnp.int32, (1, EXTRA), 1)
    most = n_ref[0]
    for b in range(1, 8):
        most = jnp.maximum(most, n_ref[b])

    def patch(i, carry):
        todo = []
        for b in range(8):
            d, k = b // 2, b % 2
            at = b * rows * POS + i
            live = i < n_ref[b]
            key, s, weight = key_ref[at], s_ref[at], t_ref[at]
            label = key & (labels - 1)
            rest = lax.div(key, labels)
            slot = rest & 7
            query = rest >> 3
            lat = pl.multiple_of((label >> 4) << 4, 16)
            qhi = lax.div(query, half)
            qlo = query & (half - 1)
            qat = pl.multiple_of(k * rows + qhi * half, half)
            spot = (pl.ds(lat, 16), pl.ds(qat, half))
            value = jnp.exp(s - lse_ref[d:d + 1, pl.ds(qat, half)]) - weight
            row = jnp.where(live, label - lat, -1)
            old = ps[d][spot].astype(jnp.float32)
            new = jnp.where((r == row) & (c == qlo), value, old).astype(jnp.bfloat16)
            full = jnp.full((1, EXTRA), s * weight, jnp.float32)
            high = full.astype(jnp.bfloat16).astype(jnp.float32)
            mid = (full - high).astype(jnp.bfloat16).astype(jnp.float32)
            low = full - high - mid
            put = jnp.where(c1 == slot, high, jnp.where(c1 == slot + 8, mid, jnp.where(c1 == slot + 16, low, 0.0)))
            put = jnp.where(jnp.logical_and(live, qhi == xh), put, 0.0)
            into = (k, pl.ds(d * half + qlo, 1), slice(None))
            todo.append((d, spot, new, into, pos_ref[into] + put))
        for d, spot, new, into, pos in todo:
            ps[d][spot] = new
            pos_ref[into] = pos
        return carry

    lax.fori_loop(0, most, patch, 0)
    for d, p_ref in enumerate(ps):
        both = jnp.concatenate([p_ref[:, pl.ds(pl.multiple_of(k * rows + xh * half, half), half)] for k in range(2)], 1)
        u = lax.dot_general(both, w_ref[...], TN, preferred_element_type=jnp.float32)
        to = pl.ds(pl.multiple_of(((y + d) & 3) * half, half), half)
        for k, out in enumerate((own_ref, oth_ref)):
            out[to, :width] = u[k * half:(k + 1) * half].astype(jnp.bfloat16)
            out[to, width:] = pos_ref[k, d * half:(d + 1) * half, :].astype(jnp.bfloat16)


def query_call(at, hits, lse, m, es, w):
    labels, width = w.shape
    rows = es[0].shape[1] // 2
    out = jax.ShapeDtypeStruct((2 * rows, width + EXTRA), jnp.bfloat16)
    res = pl.pallas_call(
        query_kernel,
        out_shape=tuple(jax.ShapeDtypeStruct(e.shape, e.dtype) for e in es) + (out, out),
        in_specs=[SMEM] * 5 + [VMEM] * 7,
        out_specs=(VMEM,) * 6,
        scratch_shapes=[pltpu.VMEM((2, 2 * rows, EXTRA), jnp.float32)],
        input_output_aliases={7 + d: d for d in range(4)},
        compiler_params=pltpu.CompilerParams(vmem_limit_bytes=28 * 2**20),
        cost_estimate=pl.CostEstimate(flops=8 * rows * labels * width, bytes_accessed=2**24, transcendentals=0),
        name="query_part",
    )(at, *hits, lse, m, *es, w)
    return res[:4], res[4], res[5]


def class_kernel(core_ref, p0, p1, p2, p3, *refs):
    blocks = refs[:8]
    out_ref, mine_ref = refs[8:]
    rows = blocks[0].shape[0]
    width = out_ref.shape[1]
    acc = None
    for d, p_ref in enumerate((p0, p1, p2, p3)):
        for k in range(2):
            term = jnp.dot(p_ref[:, k * rows:(k + 1) * rows], blocks[2 * d + k][:, :width], preferred_element_type=jnp.float32)
            acc = term if acc is None else acc + term
    done = acc.astype(jnp.bfloat16)
    out_ref[...] = done
    mine_ref[...] = done


def class_call(core, ps, blocks, width):
    labels = ps[0].shape[0]
    steps = labels // LCH
    rows = blocks[0].shape[0]
    whole = lambda i, c: (0, 0)
    return pl.pallas_call(
        class_kernel,
        out_shape=tuple(jax.ShapeDtypeStruct((n * labels, width), jnp.bfloat16) for n in (2, 1)),
        grid_spec=pltpu.PrefetchScalarGridSpec(
            num_scalar_prefetch=1,
            grid=(steps,),
            in_specs=[pl.BlockSpec((LCH, 2 * rows), lambda i, c: (i, 0))] * 4 + [pl.BlockSpec(blocks[0].shape, whole)] * 8,
            out_specs=(pl.BlockSpec((LCH, width), lambda i, c: (c[0] * steps + i, 0)), pl.BlockSpec((LCH, width), lambda i, c: (i, 0))),
        ),
        compiler_params=pltpu.CompilerParams(vmem_limit_bytes=18 * 2**20),
        cost_estimate=pl.CostEstimate(flops=16 * rows * labels * width, bytes_accessed=2**24, transcendentals=0),
        name="class_part",
    )(core, *ps, *blocks)


def lse_of(parts, axis=None):
    if axis is None:
        top = functools.reduce(jnp.maximum, parts)
        return top + jnp.log(functools.reduce(jnp.add, [jnp.exp(p - top) for p in parts]))
    top = jnp.max(parts, axis)
    return top + jnp.log(jnp.sum(jnp.exp(parts - jnp.expand_dims(top, axis)), axis))


def body(embeddings, classifier, positives, counts):
    q_dev, width = embeddings.shape
    labels = classifier.shape[0] // 2
    xh, core, xl, z, y = (lax.axis_index(a) for a in AXES)
    rank = (xl * 8 + z) * 4 + y
    base = (rank * 2 + core) * labels

    blank = jnp.zeros((q_dev, 8 - POS), jnp.int32)
    extra = jnp.concatenate(
        [positives & 127, blank, (positives >> 7) & 127, blank, positives >> 14, blank, counts[:, None], jnp.zeros((q_dev, EXTRA - CNT - 1), jnp.int32)],
        1,
    ).astype(jnp.bfloat16)
    sent = jnp.concatenate([embeddings, extra], 1)
    copies = jnp.broadcast_to(sent[None], (32, q_dev, width + EXTRA)).reshape(32 * q_dev, width + EXTRA)
    mine = lax.all_to_all(copies, ("xh", "xl", "z"), 0, 0, tiled=True)
    own = [mine] + [shift(mine, "y", -d) for d in range(1, 4)]
    oth = [shift(b, "core", 1) for b in own]
    w = lax.dynamic_slice_in_dim(classifier, core * labels, labels)
    rows = mine.shape[0]

    oth, parts, after = [None] * 4, [None] * 4, None
    for turn in ((0,), (3,), (1, 2)):
        for d in turn:
            if after is not None:
                own[d], _ = lax.optimization_barrier((own[d], after))
            oth[d] = shift(own[d], "core", 1)
        for d in turn:
            parts[d] = scores_call(own[d], oth[d], w)
        after = parts[turn[-1]][1]
    es, ms, ls = zip(*parts)
    blocks = [b for pair in zip(own, oth) for b in pair]
    hits = hits_call(base[None], blocks, w)
    m = jnp.concatenate(ms, 0)
    stat = jnp.concatenate(ls, 0)
    stat = lse_of([stat, jnp.roll(shift(stat, "core", 1), rows, 1)])
    stat = lse_of([stat] + [jnp.roll(shift(stat, "y", -d), d, 0) for d in range(1, 4)])
    stat = stat.reshape(8, rows)
    lse = lse_of(lax.all_to_all(jnp.broadcast_to(stat[None], (16, 8, rows)), ("xl", "z"), 0, 0, tiled=True), 0)

    ps, u_own, u_oth = query_call(jnp.stack([xh, y]), hits, lse.reshape(4, 2 * rows), m, es, w)
    f32 = lambda a: a.astype(jnp.float32)
    u = (f32(u_own) + f32(shift(u_oth, "core", 1))).astype(jnp.bfloat16)
    first, u = lax.optimization_barrier((ps[0], u))
    got = lax.all_to_all(u, ("y", "xl", "z"), 0, 0, tiled=True)
    halves, mine_half = class_call(core[None], (first,) + tuple(ps[1:]), blocks, width)

    final = jnp.sum(f32(got).reshape(64, q_dev, width + EXTRA), 0)
    query_grad = final[:, :width].astype(jnp.bfloat16)
    pos_mean = jnp.sum(final[:, width:width + 24], 1)
    at = ((xh * 2 + xl) * 8 + z) * q_dev
    loss = lax.dynamic_slice(lse, (0, at), (1, q_dev))[0] - pos_mean
    class_grad = lax.dynamic_update_slice_in_dim(halves, shift(mine_half, "core", 1), (1 - core) * labels, 0)
    return loss, query_grad, class_grad


def solution(mesh):
    fine = Mesh(mesh.devices.reshape(tuple(SIZES[a] for a in AXES)), AXES)
    split = P(AXES, None)
    lab = P(("xl", "z", "y"), None)
    return jax.shard_map(
        body,
        mesh=fine,
        in_specs=(split, lab, split, P(AXES)),
        out_specs=(P(AXES), split, lab),
        check_vma=False,
    )
```

```python
import functools

import jax
import jax.numpy as jnp
from jax import lax
from jax.experimental import pallas as pl
from jax.experimental.pallas import tpu as pltpu
from jax.sharding import Mesh, PartitionSpec as P

AXES = ("xh", "core", "xl", "z", "y")
SIZES = {"xh": 2, "core": 2, "xl": 2, "z": 8, "y": 4}
EXTRA = 128
POS = 5
LO, MID, HI, CNT = 0, 8, 16, 24
VMEM = pl.BlockSpec(memory_space=pltpu.VMEM)
SMEM = pl.BlockSpec(memory_space=pltpu.SMEM)
HBM = pl.BlockSpec(memory_space=pltpu.HBM)
NT = (((1,), (1,)), ((), ()))
TN = (((0,), (0,)), ((), ()))
LCH = 256
PROD = 1024
EXPO = 128
PARTS = 4


def shift(x, axis, step):
    n = SIZES[axis]
    return lax.ppermute(x, axis, [(i, (i + step) % n) for i in range(n)])


def scores_kernel(own_ref, oth_ref, w_ref, e_ref, m_ref, l_ref, s_ref, qt_ref, held_ref, sem):
    labels, width = w_ref.shape
    rows = own_ref.shape[0]
    both = 2 * rows
    qt_ref[:, :rows] = own_ref[:, :width].T
    qt_ref[:, rows:] = oth_ref[:, :width].T

    def product(i, top):
        at = pl.multiple_of(i * PROD, PROD)
        s = jnp.dot(w_ref[pl.ds(at, PROD), :], qt_ref[...], preferred_element_type=jnp.float32)
        s_ref[pl.ds(at, PROD), :] = s
        return jnp.maximum(top, jnp.max(s.reshape(PROD // 16, 16, both), 0))

    top = lax.fori_loop(0, labels // PROD, product, jnp.full((16, both), -1e30, jnp.float32))
    top = jnp.max(top, 0, keepdims=True)

    def leave(i):
        part = pl.ds(pl.multiple_of(i * EXPO, EXPO), EXPO)
        return pltpu.make_async_copy(held_ref.at[part, :], e_ref.at[part, :], sem.at[i])

    def expo(i, total):
        at = pl.multiple_of(i * EXPO, EXPO)
        e = jnp.exp(s_ref[pl.ds(at, EXPO), :] - top)
        held_ref[pl.ds(at, EXPO), :] = e.astype(jnp.bfloat16)
        leave(i).start()
        return total + jnp.sum(e.reshape(EXPO // 16, 16, both), 0)

    total = lax.fori_loop(0, labels // EXPO, expo, jnp.zeros((16, both), jnp.float32))
    m_ref[...] = top
    l_ref[...] = top + jnp.log(jnp.sum(total, 0, keepdims=True))

    def gone(i, carry):
        leave(i).wait()
        return carry

    lax.fori_loop(0, labels // EXPO, gone, 0)


def scores_call(own, oth, w):
    rows = own.shape[0]
    labels, width = w.shape
    line = jax.ShapeDtypeStruct((1, 2 * rows), jnp.float32)
    return pl.pallas_call(
        scores_kernel,
        out_shape=(pltpu.HBM((labels, 2 * rows), jnp.bfloat16), line, line),
        in_specs=[VMEM] * 3,
        out_specs=(HBM, VMEM, VMEM),
        scratch_shapes=[
            pltpu.VMEM((labels, 2 * rows), jnp.float32),
            pltpu.VMEM((width, 2 * rows), jnp.bfloat16),
            pltpu.VMEM((labels, 2 * rows), jnp.bfloat16),
            pltpu.SemaphoreType.DMA((labels // EXPO,)),
        ],
        compiler_params=pltpu.CompilerParams(vmem_limit_bytes=18 * 2**20),
        cost_estimate=pl.CostEstimate(flops=1000, bytes_accessed=1000, transcendentals=0),
        name="scores",
    )(own, oth, w)


def hits_kernel(base_ref, *refs):
    sources = refs[:4]
    w_ref, n_ref, key_ref, s_ref, t_ref, blocks, sem = refs[4:]
    copies = [pltpu.make_async_copy(q, blocks.at[b], sem.at[b]) for b, q in enumerate(sources)]
    for copy in copies:
        copy.start()
    labels, width = w_ref.shape
    base = base_ref[0].astype(jnp.float32)
    row = lax.broadcasted_iota(jnp.int32, (8, EXTRA), 0)
    col = lax.broadcasted_iota(jnp.int32, (8, EXTRA), 1)
    digits = jnp.where(col == row + LO, 1.0, jnp.where(col == row + MID, 128.0, jnp.where(col == row + HI, 16384.0, 0.0)))
    digits = jnp.where(row < POS, digits, 0.0).astype(jnp.bfloat16)
    counting = jnp.where(col == CNT, 1.0, 0.0).astype(jnp.bfloat16)
    big = 1e9
    rows = blocks.shape[1]
    slot = lax.broadcasted_iota(jnp.int32, (8, rows), 0)
    lane = lax.broadcasted_iota(jnp.int32, (8, rows), 1)
    keys, weights, most = [], [], jnp.int32(0)
    for b in range(4):
        copies[b].wait()
        extra = blocks[b, :, width:]
        ids = lax.dot_general(digits, extra, NT, preferred_element_type=jnp.float32)
        cnt = lax.dot_general(counting, extra, NT, preferred_element_type=jnp.float32)
        valid = (slot.astype(jnp.float32) < cnt) & (slot < POS)
        ids = jnp.where(valid, ids, -1.0)
        same = jnp.zeros((8, rows), jnp.float32)
        again = jnp.zeros((8, rows), jnp.float32)
        for j in range(POS):
            eq = jnp.where(ids == ids[j:j + 1, :], 1.0, 0.0)
            same = same + eq
            again = again + jnp.where(slot > j, eq, 0.0)
        local = ids - base
        hit = valid & (local >= 0.0) & (local < float(labels)) & (again == 0.0)
        weights.append(same / cnt)
        keys.append(jnp.where(hit, (lane * 8 + slot).astype(jnp.float32) * float(labels) + local, big))
        n = jnp.sum(jnp.where(hit, 1.0, 0.0)).astype(jnp.int32)
        n_ref[b] = n
        most = jnp.maximum(most, n)
    r16 = lax.broadcasted_iota(jnp.int32, (16, width), 0)

    def step(i, keys):
        least = [jnp.min(k) for k in keys]
        found = [jnp.where(k < big, k, 0.0).astype(jnp.int32) for k in least]
        same = [k == kf for k, kf in zip(keys, least)]
        score, weight = [], []
        for b, k in enumerate(found):
            label = k & (labels - 1)
            query = lax.div(k, 8 * labels)
            qat = pl.multiple_of((query >> 4) << 4, 16)
            lat = pl.multiple_of((label >> 4) << 4, 16)
            row_q = jnp.where(r16 == query - qat, blocks[b, pl.ds(qat, 16), :width].astype(jnp.float32), 0.0)
            row_w = jnp.where(r16 == label - lat, w_ref[pl.ds(lat, 16), :].astype(jnp.float32), 0.0)
            score.append(jnp.sum(row_w * jnp.sum(row_q, 0, keepdims=True)))
            weight.append(jnp.sum(jnp.where(same[b], weights[b], 0.0)))
        for b in range(4):
            at = b * rows * POS + i
            key_ref[at] = found[b]
            s_ref[at] = score[b]
            t_ref[at] = weight[b]
        return tuple(jnp.where(t, big, k) for t, k in zip(same, keys))

    lax.fori_loop(0, most, step, tuple(keys))


def hits_call(base, blocks, w):
    total = 4 * blocks[0].shape[0] * POS
    return pl.pallas_call(
        hits_kernel,
        out_shape=(
            jax.ShapeDtypeStruct((4,), jnp.int32),
            jax.ShapeDtypeStruct((total,), jnp.int32),
            jax.ShapeDtypeStruct((total,), jnp.float32),
            jax.ShapeDtypeStruct((total,), jnp.float32),
        ),
        in_specs=[SMEM] + [HBM] * 4 + [VMEM],
        out_specs=(SMEM,) * 4,
        scratch_shapes=[pltpu.VMEM((4,) + blocks[0].shape, jnp.bfloat16), pltpu.SemaphoreType.DMA((4,))],
        compiler_params=pltpu.CompilerParams(vmem_limit_bytes=12 * 2**20),
        cost_estimate=pl.CostEstimate(flops=1000, bytes_accessed=1000, transcendentals=0),
        name="hits",
    )(base, *blocks, w)


def query_kernel(at_ref, na, ka, sa, ta, nb, kb, sb, tb, lse_ref, m_ref, e0, e1, e2, e3, w_ref, *outs):
    own_ref, oth_ref, pos_ref, held, sem = outs[4:]
    ps = [held.at[d] for d in range(4)]
    copies = [pltpu.make_async_copy(e, p, sem.at[d]) for d, (e, p) in enumerate(zip((e0, e1, e2, e3), ps))]
    for copy in copies:
        copy.start()
    labels, width = w_ref.shape
    lists = ((na, ka, sa, ta, 0), (na, ka, sa, ta, 2), (nb, kb, sb, tb, 0), (nb, kb, sb, tb, 2))
    rows = e0.shape[1] // 2
    xh, y = at_ref[0], at_ref[1]
    half = rows // 2
    pos_ref[...] = jnp.zeros_like(pos_ref)
    for d, p_ref in enumerate(ps):
        copies[d].wait()
        scale = jnp.exp(m_ref[d:d + 1, :] - lse_ref[d:d + 1, :])

        def scaled(i, carry):
            at = pl.multiple_of(i * 64, 64)
            p_ref[pl.ds(at, 64), :] = (p_ref[pl.ds(at, 64), :].astype(jnp.float32) * scale).astype(jnp.bfloat16)
            return carry

        lax.fori_loop(0, labels // 64, scaled, 0)

    r = lax.broadcasted_iota(jnp.int32, (16, half), 0)
    c = lax.broadcasted_iota(jnp.int32, (16, half), 1)
    c1 = lax.broadcasted_iota(jnp.int32, (1, EXTRA), 1)
    most = jnp.int32(0)
    for b in range(4):
        most = jnp.maximum(most, jnp.maximum(na[b], nb[b]))

    def patch(i, carry):
        todo = []
        for b in range(8):
            d, k = b // 2, b % 2
            n_ref, key_ref, s_ref, t_ref, first = lists[d]
            at = (first + k) * rows * POS + i
            live = i < n_ref[first + k]
            key, s, weight = jnp.where(live, key_ref[at], 0), s_ref[at], t_ref[at]
            label = key & (labels - 1)
            rest = lax.div(key, labels)
            slot = rest & 7
            query = rest >> 3
            lat = pl.multiple_of((label >> 4) << 4, 16)
            qhi = lax.div(query, half)
            qlo = query & (half - 1)
            qat = pl.multiple_of(k * rows + qhi * half, half)
            spot = (pl.ds(lat, 16), pl.ds(qat, half))
            value = jnp.exp(s - lse_ref[d:d + 1, pl.ds(qat, half)]) - weight
            row = jnp.where(live, label - lat, -1)
            old = ps[d][spot].astype(jnp.float32)
            new = jnp.where((r == row) & (c == qlo), value, old).astype(jnp.bfloat16)
            full = jnp.full((1, EXTRA), s * weight, jnp.float32)
            high = full.astype(jnp.bfloat16).astype(jnp.float32)
            mid = (full - high).astype(jnp.bfloat16).astype(jnp.float32)
            low = full - high - mid
            put = jnp.where(c1 == slot, high, jnp.where(c1 == slot + 8, mid, jnp.where(c1 == slot + 16, low, 0.0)))
            put = jnp.where(jnp.logical_and(live, qhi == xh), put, 0.0)
            into = (k, pl.ds(d * half + qlo, 1), slice(None))
            todo.append((d, spot, new, into, pos_ref[into] + put))
        for d, spot, new, into, pos in todo:
            ps[d][spot] = new
            pos_ref[into] = pos
        return carry

    lax.fori_loop(0, most, patch, 0)
    copies = [pltpu.make_async_copy(p, out, sem.at[d]) for d, (p, out) in enumerate(zip(ps, outs))]
    for copy in copies:
        copy.start()
    for d, p_ref in enumerate(ps):
        both = jnp.concatenate([p_ref[:, pl.ds(pl.multiple_of(k * rows + xh * half, half), half)] for k in range(2)], 1)
        u = lax.dot_general(both, w_ref[...], TN, preferred_element_type=jnp.float32)
        to = pl.ds(pl.multiple_of(((y + d) & 3) * half, half), half)
        for k, out in enumerate((own_ref, oth_ref)):
            out[to, :width] = u[k * half:(k + 1) * half].astype(jnp.bfloat16)
            out[to, width:] = pos_ref[k, d * half:(d + 1) * half, :].astype(jnp.bfloat16)
    for copy in copies:
        copy.wait()


def query_call(at, hits, lse, m, es, w):
    labels, width = w.shape
    rows = es[0].shape[1] // 2
    out = jax.ShapeDtypeStruct((2 * rows, width + EXTRA), jnp.bfloat16)
    res = pl.pallas_call(
        query_kernel,
        out_shape=tuple(pltpu.HBM(e.shape, e.dtype) for e in es) + (out, out),
        in_specs=[SMEM] * 9 + [VMEM] * 2 + [HBM] * 4 + [VMEM],
        out_specs=(HBM,) * 4 + (VMEM,) * 2,
        scratch_shapes=[pltpu.VMEM((2, 2 * rows, EXTRA), jnp.float32), pltpu.VMEM((4,) + es[0].shape, jnp.bfloat16), pltpu.SemaphoreType.DMA((4,))],
        compiler_params=pltpu.CompilerParams(vmem_limit_bytes=28 * 2**20),
        cost_estimate=pl.CostEstimate(flops=8 * rows * labels * width, bytes_accessed=2**24, transcendentals=0),
        name="query_part",
    )(at, *hits[0], *hits[1], lse, m, *[pltpu.with_memory_space_constraint(e, pltpu.HBM) for e in es], w)
    return res[:4], res[4], res[5]


def class_kernel(core_ref, p0, p1, p2, p3, *refs):
    blocks = refs[:8]
    out_ref, parts = refs[8], refs[9:]
    rows = blocks[0].shape[0]
    width = out_ref.shape[1]
    acc = None
    for d, p_ref in enumerate((p0, p1, p2, p3)):
        for k in range(2):
            term = jnp.dot(p_ref[:, k * rows:(k + 1) * rows], blocks[2 * d + k][:, :width], preferred_element_type=jnp.float32)
            acc = term if acc is None else acc + term
    done = acc.astype(jnp.bfloat16)
    out_ref[...] = done
    each = pl.num_programs(0) // len(parts)
    for j, part in enumerate(parts):
        @pl.when(pl.program_id(0) // each == j)
        def _():
            part[...] = done


def class_call(core, ps, blocks, width):
    labels = ps[0].shape[0]
    steps = labels // LCH
    each = steps // PARTS
    rows = blocks[0].shape[0]
    whole = lambda i, c: (0, 0)
    return pl.pallas_call(
        class_kernel,
        out_shape=(jax.ShapeDtypeStruct((2 * labels, width), jnp.bfloat16),) + (jax.ShapeDtypeStruct((labels // PARTS, width), jnp.bfloat16),) * PARTS,
        grid_spec=pltpu.PrefetchScalarGridSpec(
            num_scalar_prefetch=1,
            grid=(steps,),
            in_specs=[pl.BlockSpec((LCH, 2 * rows), lambda i, c: (i, 0))] * 4 + [pl.BlockSpec(blocks[0].shape, whole)] * 8,
            out_specs=(pl.BlockSpec((LCH, width), lambda i, c: (c[0] * steps + i, 0)),)
            + tuple(pl.BlockSpec((LCH, width), lambda i, c, j=j: (jnp.clip(i - j * each, 0, each - 1), 0)) for j in range(PARTS)),
        ),
        compiler_params=pltpu.CompilerParams(vmem_limit_bytes=20 * 2**20),
        cost_estimate=pl.CostEstimate(flops=16 * rows * labels * width, bytes_accessed=2**24, transcendentals=0),
        name="class_part",
    )(core, *[pltpu.with_memory_space_constraint(p, pltpu.HBM) for p in ps], *blocks)


def lse_of(parts, axis=None):
    if axis is None:
        top = functools.reduce(jnp.maximum, parts)
        return top + jnp.log(functools.reduce(jnp.add, [jnp.exp(p - top) for p in parts]))
    top = jnp.max(parts, axis)
    return top + jnp.log(jnp.sum(jnp.exp(parts - jnp.expand_dims(top, axis)), axis))


def body(embeddings, classifier, positives, counts):
    q_dev, width = embeddings.shape
    labels = classifier.shape[0] // 2
    xh, core, xl, z, y = (lax.axis_index(a) for a in AXES)
    rank = (xl * 8 + z) * 4 + y
    base = (rank * 2 + core) * labels

    blank = jnp.zeros((q_dev, 8 - POS), jnp.int32)
    extra = jnp.concatenate(
        [positives & 127, blank, (positives >> 7) & 127, blank, positives >> 14, blank, counts[:, None], jnp.zeros((q_dev, EXTRA - CNT - 1), jnp.int32)],
        1,
    ).astype(jnp.bfloat16)
    sent = jnp.concatenate([embeddings, extra], 1)
    copies = jnp.broadcast_to(sent[None], (32, q_dev, width + EXTRA)).reshape(32 * q_dev, width + EXTRA)
    mine = lax.all_to_all(copies, ("xh", "xl", "z"), 0, 0, tiled=True)
    own = [mine] + [shift(mine, "y", -d) for d in range(1, 4)]
    oth = [shift(b, "core", 1) for b in own]
    w = lax.dynamic_slice_in_dim(classifier, core * labels, labels)
    rows = mine.shape[0]

    oth, parts, ready = [None] * 4, [None] * 4, list(own)
    for d in range(4):
        if d:
            own[d], _ = lax.optimization_barrier((own[d], parts[0][1]))
        oth[d] = shift(own[d], "core", 1)
        ready[d] = own[d]
        if d >= 2:
            ready[d], _ = lax.optimization_barrier((own[d], hits[0][0]))
        parts[d] = scores_call(ready[d], oth[d], w)
        if d == 1:
            hits = [hits_call(base[None], (own[0], oth[0], own[1], oth[1]), w)]
    es, ms, ls = zip(*parts)
    blocks = [b for pair in zip(own, oth) for b in pair]
    hits.append(hits_call(base[None], blocks[4:], w))
    m = jnp.concatenate(ms, 0)
    stat = jnp.concatenate(ls, 0)
    stat = lse_of([stat, jnp.roll(shift(stat, "core", 1), rows, 1)])
    stat = lse_of([stat] + [jnp.roll(shift(stat, "y", -d), d, 0) for d in range(1, 4)])
    stat = stat.reshape(8, rows)
    lse = lse_of(lax.all_to_all(jnp.broadcast_to(stat[None], (16, 8, rows)), ("xl", "z"), 0, 0, tiled=True), 0)

    ps, u_own, u_oth = query_call(jnp.stack([xh, y]), hits, lse.reshape(4, 2 * rows), m, es, w)
    f32 = lambda a: a.astype(jnp.float32)
    u = (f32(u_own) + f32(shift(u_oth, "core", 1))).astype(jnp.bfloat16)
    first, u = lax.optimization_barrier((ps[0], u))
    got = lax.all_to_all(u, ("y", "xl", "z"), 0, 0, tiled=True)
    class_grad, *mine_parts = class_call(core[None], (first,) + tuple(ps[1:]), blocks, width)

    final = jnp.sum(f32(got).reshape(64, q_dev, width + EXTRA), 0)
    query_grad = final[:, :width].astype(jnp.bfloat16)
    pos_mean = jnp.sum(final[:, width:width + 24], 1)
    at = ((xh * 2 + xl) * 8 + z) * q_dev
    loss = lax.dynamic_slice(lse, (0, at), (1, q_dev))[0] - pos_mean
    for j, part in enumerate(mine_parts):
        class_grad = lax.dynamic_update_slice_in_dim(class_grad, shift(part, "core", 1), (1 - core) * labels + j * part.shape[0], 0)
    return loss, query_grad, class_grad


def solution(mesh):
    fine = Mesh(mesh.devices.reshape(tuple(SIZES[a] for a in AXES)), AXES)
    split = P(AXES, None)
    lab = P(("xl", "z", "y"), None)
    return jax.shard_map(
        body,
        mesh=fine,
        in_specs=(split, lab, split, P(AXES)),
        out_specs=(P(AXES), split, lab),
        check_vma=False,
    )
```

```python
import functools

import jax
import jax.numpy as jnp
from jax import lax
from jax.experimental import pallas as pl
from jax.experimental.pallas import tpu as pltpu
from jax.sharding import Mesh, PartitionSpec as P

AXES = ("xh", "core", "xl", "z", "y")
SIZES = {"xh": 2, "core": 2, "xl": 2, "z": 8, "y": 4}
EXTRA = 128
POS = 5
LO, MID, HI, CNT = 0, 8, 16, 24
VMEM = pl.BlockSpec(memory_space=pltpu.VMEM)
SMEM = pl.BlockSpec(memory_space=pltpu.SMEM)
ANY = pl.BlockSpec(memory_space=pl.ANY)
HBM = pl.BlockSpec(memory_space=pltpu.HBM)
NT = (((1,), (1,)), ((), ()))
TN = (((0,), (0,)), ((), ()))
LCH = 256
PROD = 1024
EXPO = 128
PARTS = 2
CLASS = 512


def shift(x, axis, step):
    n = SIZES[axis]
    return lax.ppermute(x, axis, [(i, (i + step) % n) for i in range(n)])


def in_hbm(arrays):
    return [pltpu.with_memory_space_constraint(a, pltpu.HBM) for a in arrays]


def scores_kernel(own_ref, oth_ref, w_ref, e_ref, m_ref, l_ref, q_ref, s_ref, qt_ref, held_ref, sem):
    labels, width = w_ref.shape
    rows = own_ref.shape[0]
    both = 2 * rows
    copies = [pltpu.make_async_copy(a, q_ref.at[k], sem.at[k]) for k, a in enumerate((own_ref, oth_ref))]
    for copy in copies:
        copy.start()
    for k, copy in enumerate(copies):
        copy.wait()
        qt_ref[:, k * rows:(k + 1) * rows] = q_ref[k, :, :width].T

    def product(i, top):
        at = pl.multiple_of(i * PROD, PROD)
        s = jnp.dot(w_ref[pl.ds(at, PROD), :], qt_ref[...], preferred_element_type=jnp.float32)
        s_ref[pl.ds(at, PROD), :] = s
        return jnp.maximum(top, jnp.max(s.reshape(PROD // 16, 16, both), 0))

    top = lax.fori_loop(0, labels // PROD, product, jnp.full((16, both), -1e30, jnp.float32))
    top = jnp.max(top, 0, keepdims=True)

    def leave(i):
        part = pl.ds(pl.multiple_of(i * EXPO, EXPO), EXPO)
        return pltpu.make_async_copy(held_ref.at[part, :], e_ref.at[part, :], sem.at[i])

    def expo(i, total):
        at = pl.multiple_of(i * EXPO, EXPO)
        e = jnp.exp(s_ref[pl.ds(at, EXPO), :] - top)
        held_ref[pl.ds(at, EXPO), :] = e.astype(jnp.bfloat16)
        leave(i).start()
        return total + jnp.sum(e.reshape(EXPO // 16, 16, both), 0)

    total = lax.fori_loop(0, labels // EXPO, expo, jnp.zeros((16, both), jnp.float32))
    m_ref[...] = top
    l_ref[...] = top + jnp.log(jnp.sum(total, 0, keepdims=True))

    def gone(i, carry):
        leave(i).wait()
        return carry

    lax.fori_loop(0, labels // EXPO, gone, 0)


def scores_call(own, oth, w):
    rows = own.shape[0]
    labels, width = w.shape
    line = jax.ShapeDtypeStruct((1, 2 * rows), jnp.float32)
    return pl.pallas_call(
        scores_kernel,
        out_shape=(pltpu.HBM((labels, 2 * rows), jnp.bfloat16), line, line),
        in_specs=[ANY, ANY, VMEM],
        out_specs=(HBM, VMEM, VMEM),
        scratch_shapes=[
            pltpu.VMEM((2,) + own.shape, jnp.bfloat16),
            pltpu.VMEM((labels, 2 * rows), jnp.float32),
            pltpu.VMEM((width, 2 * rows), jnp.bfloat16),
            pltpu.VMEM((labels, 2 * rows), jnp.bfloat16),
            pltpu.SemaphoreType.DMA((labels // EXPO,)),
        ],
        compiler_params=pltpu.CompilerParams(vmem_limit_bytes=18 * 2**20),
        cost_estimate=pl.CostEstimate(flops=1000, bytes_accessed=1000, transcendentals=0),
        name="scores",
    )(own, oth, w)


def hits_kernel(base_ref, *refs):
    sources = refs[:8]
    w_ref, n_ref, key_ref, s_ref, t_ref, blocks, sem = refs[8:]
    copies = [pltpu.make_async_copy(q, blocks.at[b], sem.at[b]) for b, q in enumerate(sources)]
    for copy in copies:
        copy.start()
    labels, width = w_ref.shape
    base = base_ref[0].astype(jnp.float32)
    row = lax.broadcasted_iota(jnp.int32, (8, EXTRA), 0)
    col = lax.broadcasted_iota(jnp.int32, (8, EXTRA), 1)
    digits = jnp.where(col == row + LO, 1.0, jnp.where(col == row + MID, 128.0, jnp.where(col == row + HI, 16384.0, 0.0)))
    digits = jnp.where(row < POS, digits, 0.0).astype(jnp.bfloat16)
    counting = jnp.where(col == CNT, 1.0, 0.0).astype(jnp.bfloat16)
    big = 1e9
    rows = blocks.shape[1]
    slot = lax.broadcasted_iota(jnp.int32, (8, rows), 0)
    lane = lax.broadcasted_iota(jnp.int32, (8, rows), 1)
    keys, weights, most = [], [], jnp.int32(0)
    for b in range(8):
        copies[b].wait()
        extra = blocks[b, :, width:]
        ids = lax.dot_general(digits, extra, NT, preferred_element_type=jnp.float32)
        cnt = lax.dot_general(counting, extra, NT, preferred_element_type=jnp.float32)
        valid = (slot.astype(jnp.float32) < cnt) & (slot < POS)
        ids = jnp.where(valid, ids, -1.0)
        same = jnp.zeros((8, rows), jnp.float32)
        again = jnp.zeros((8, rows), jnp.float32)
        for j in range(POS):
            eq = jnp.where(ids == ids[j:j + 1, :], 1.0, 0.0)
            same = same + eq
            again = again + jnp.where(slot > j, eq, 0.0)
        local = ids - base
        hit = valid & (local >= 0.0) & (local < float(labels)) & (again == 0.0)
        weights.append(same / cnt)
        keys.append(jnp.where(hit, (lane * 8 + slot).astype(jnp.float32) * float(labels) + local, big))
        n = jnp.sum(jnp.where(hit, 1.0, 0.0)).astype(jnp.int32)
        n_ref[b] = n
        most = jnp.maximum(most, n)
    r16 = lax.broadcasted_iota(jnp.int32, (16, width), 0)

    def step(i, keys):
        least = [jnp.min(k) for k in keys]
        found = [jnp.where(k < big, k, 0.0).astype(jnp.int32) for k in least]
        same = [k == kf for k, kf in zip(keys, least)]
        score, weight = [], []
        for b, k in enumerate(found):
            label = k & (labels - 1)
            query = lax.div(k, 8 * labels)
            qat = pl.multiple_of((query >> 4) << 4, 16)
            lat = pl.multiple_of((label >> 4) << 4, 16)
            row_q = jnp.where(r16 == query - qat, blocks[b, pl.ds(qat, 16), :width].astype(jnp.float32), 0.0)
            row_w = jnp.where(r16 == label - lat, w_ref[pl.ds(lat, 16), :].astype(jnp.float32), 0.0)
            score.append(jnp.sum(row_w * jnp.sum(row_q, 0, keepdims=True)))
            weight.append(jnp.sum(jnp.where(same[b], weights[b], 0.0)))
        for b in range(8):
            at = b * rows * POS + i
            key_ref[at] = found[b]
            s_ref[at] = score[b]
            t_ref[at] = weight[b]
        return tuple(jnp.where(t, big, k) for t, k in zip(same, keys))

    lax.fori_loop(0, most, step, tuple(keys))


def hits_call(base, blocks, w):
    total = 8 * blocks[0].shape[0] * POS
    return pl.pallas_call(
        hits_kernel,
        out_shape=(
            jax.ShapeDtypeStruct((8,), jnp.int32),
            jax.ShapeDtypeStruct((total,), jnp.int32),
            jax.ShapeDtypeStruct((total,), jnp.float32),
            jax.ShapeDtypeStruct((total,), jnp.float32),
        ),
        in_specs=[SMEM] + [HBM] * 8 + [VMEM],
        out_specs=(SMEM,) * 4,
        scratch_shapes=[pltpu.VMEM((8,) + blocks[0].shape, jnp.bfloat16), pltpu.SemaphoreType.DMA((8,))],
        compiler_params=pltpu.CompilerParams(vmem_limit_bytes=16 * 2**20),
        cost_estimate=pl.CostEstimate(flops=1000, bytes_accessed=1000, transcendentals=0),
        name="hits",
    )(base, *in_hbm(blocks), w)


def query_kernel(at_ref, n_ref, key_ref, s_ref, t_ref, lse_ref, m_ref, e0, e1, e2, e3, w_ref, *outs):
    own_ref, oth_ref, pos_ref, held, sem = outs[4:]
    ps = [held.at[d] for d in range(4)]
    copies = [pltpu.make_async_copy(e, p, sem.at[d]) for d, (e, p) in enumerate(zip((e0, e1, e2, e3), ps))]
    for copy in copies:
        copy.start()
    labels, width = w_ref.shape
    rows = e0.shape[1] // 2
    xh, y = at_ref[0], at_ref[1]
    half = rows // 2
    pos_ref[...] = jnp.zeros_like(pos_ref)
    for d, p_ref in enumerate(ps):
        copies[d].wait()
        scale = jnp.exp(m_ref[d:d + 1, :] - lse_ref[d:d + 1, :])

        def scaled(i, carry):
            at = pl.multiple_of(i * 64, 64)
            p_ref[pl.ds(at, 64), :] = (p_ref[pl.ds(at, 64), :].astype(jnp.float32) * scale).astype(jnp.bfloat16)
            return carry

        lax.fori_loop(0, labels // 64, scaled, 0)

    r = lax.broadcasted_iota(jnp.int32, (16, half), 0)
    c = lax.broadcasted_iota(jnp.int32, (16, half), 1)
    c1 = lax.broadcasted_iota(jnp.int32, (1, EXTRA), 1)
    most = jnp.int32(0)
    for b in range(8):
        most = jnp.maximum(most, n_ref[b])

    def patch(i, carry):
        todo = []
        for b in range(8):
            d, k = b // 2, b % 2
            at = b * rows * POS + i
            live = i < n_ref[b]
            key, s, weight = jnp.where(live, key_ref[at], 0), s_ref[at], t_ref[at]
            label = key & (labels - 1)
            rest = lax.div(key, labels)
            slot = rest & 7
            query = rest >> 3
            lat = pl.multiple_of((label >> 4) << 4, 16)
            qhi = lax.div(query, half)
            qlo = query & (half - 1)
            qat = pl.multiple_of(k * rows + qhi * half, half)
            spot = (pl.ds(lat, 16), pl.ds(qat, half))
            value = jnp.exp(s - lse_ref[d:d + 1, pl.ds(qat, half)]) - weight
            row = jnp.where(live, label - lat, -1)
            old = ps[d][spot].astype(jnp.float32)
            new = jnp.where((r == row) & (c == qlo), value, old).astype(jnp.bfloat16)
            full = jnp.full((1, EXTRA), s * weight, jnp.float32)
            high = full.astype(jnp.bfloat16).astype(jnp.float32)
            mid = (full - high).astype(jnp.bfloat16).astype(jnp.float32)
            low = full - high - mid
            put = jnp.where(c1 == slot, high, jnp.where(c1 == slot + 8, mid, jnp.where(c1 == slot + 16, low, 0.0)))
            put = jnp.where(jnp.logical_and(live, qhi == xh), put, 0.0)
            into = (k, pl.ds(d * half + qlo, 1), slice(None))
            todo.append((d, spot, new, into, pos_ref[into] + put))
        for d, spot, new, into, pos in todo:
            ps[d][spot] = new
            pos_ref[into] = pos
        return carry

    lax.fori_loop(0, most, patch, 0)
    copies = [pltpu.make_async_copy(p, out, sem.at[d]) for d, (p, out) in enumerate(zip(ps, outs))]
    for copy in copies:
        copy.start()
    for d, p_ref in enumerate(ps):
        both = jnp.concatenate([p_ref[:, pl.ds(pl.multiple_of(k * rows + xh * half, half), half)] for k in range(2)], 1)
        u = lax.dot_general(both, w_ref[...], TN, preferred_element_type=jnp.float32)
        to = pl.ds(pl.multiple_of(((y + d) & 3) * half, half), half)
        for k, out in enumerate((own_ref, oth_ref)):
            out[to, :width] = u[k * half:(k + 1) * half].astype(jnp.bfloat16)
            out[to, width:] = pos_ref[k, d * half:(d + 1) * half, :].astype(jnp.bfloat16)
    for copy in copies:
        copy.wait()


def query_call(at, hits, lse, m, es, w):
    labels, width = w.shape
    rows = es[0].shape[1] // 2
    out = jax.ShapeDtypeStruct((2 * rows, width + EXTRA), jnp.bfloat16)
    res = pl.pallas_call(
        query_kernel,
        out_shape=tuple(pltpu.HBM(e.shape, e.dtype) for e in es) + (out, out),
        in_specs=[SMEM] * 5 + [VMEM] * 2 + [HBM] * 4 + [VMEM],
        out_specs=(HBM,) * 4 + (VMEM,) * 2,
        scratch_shapes=[pltpu.VMEM((2, 2 * rows, EXTRA), jnp.float32), pltpu.VMEM((4,) + es[0].shape, jnp.bfloat16), pltpu.SemaphoreType.DMA((4,))],
        compiler_params=pltpu.CompilerParams(vmem_limit_bytes=28 * 2**20),
        cost_estimate=pl.CostEstimate(flops=8 * rows * labels * width, bytes_accessed=2**24, transcendentals=0),
        name="query_part",
    )(at, *hits, lse, m, *in_hbm(es), w)
    return res[:4], res[4], res[5]


def class_kernel(core_ref, p0, p1, p2, p3, *refs):
    blocks = refs[:8]
    out_ref, mine_ref = refs[-2:]
    rows = blocks[0].shape[0]
    width = out_ref.shape[1]
    acc = None
    for d, p_ref in enumerate((p0, p1, p2, p3)):
        for k in range(2):
            term = jnp.dot(p_ref[:, k * rows:(k + 1) * rows], blocks[2 * d + k][:, :width], preferred_element_type=jnp.float32)
            acc = term if acc is None else acc + term
    done = acc.astype(jnp.bfloat16)
    out_ref[...] = done
    mine_ref[...] = done


def class_call(core, ps, blocks, width, part, before):
    labels = ps[0].shape[0]
    steps = labels // CLASS
    each = steps // PARTS
    rows = blocks[0].shape[0]
    whole = lambda i, c: (0, 0)
    kept = () if before is None else (before,)
    return pl.pallas_call(
        class_kernel,
        out_shape=tuple(jax.ShapeDtypeStruct((n, width), jnp.bfloat16) for n in (2 * labels, labels // PARTS)),
        grid_spec=pltpu.PrefetchScalarGridSpec(
            num_scalar_prefetch=1,
            grid=(each,),
            in_specs=[pl.BlockSpec((CLASS, 2 * rows), lambda i, c: (part * each + i, 0))] * 4
            + [pl.BlockSpec(blocks[0].shape, whole)] * 8
            + [HBM] * len(kept),
            out_specs=(
                pl.BlockSpec((CLASS, width), lambda i, c: (c[0] * steps + part * each + i, 0)),
                pl.BlockSpec((CLASS, width), lambda i, c: (i, 0)),
            ),
        ),
        input_output_aliases={13: 0} if kept else {},
        compiler_params=pltpu.CompilerParams(vmem_limit_bytes=24 * 2**20),
        cost_estimate=pl.CostEstimate(flops=16 * rows * labels * width // PARTS, bytes_accessed=2**23, transcendentals=0),
        name="class_part",
    )(core, *in_hbm(ps), *in_hbm(blocks), *kept)


def place_kernel(core_ref, *refs):
    parts, out_ref, sem = refs[:PARTS], refs[-2], refs[-1]
    rows = parts[0].shape[0]
    first = (1 - core_ref[0]) * (PARTS * rows)
    copies = [
        pltpu.make_async_copy(p, out_ref.at[pl.ds(pl.multiple_of(first + j * rows, rows), rows), :], sem.at[j]) for j, p in enumerate(parts)
    ]
    for copy in copies:
        copy.start()
    for copy in copies:
        copy.wait()


def place_call(core, parts, into):
    return pl.pallas_call(
        place_kernel,
        out_shape=jax.ShapeDtypeStruct(into.shape, into.dtype),
        in_specs=[SMEM] + [ANY] * PARTS + [HBM],
        out_specs=HBM,
        scratch_shapes=[pltpu.SemaphoreType.DMA((PARTS,))],
        input_output_aliases={1 + PARTS: 0},
        cost_estimate=pl.CostEstimate(flops=1000, bytes_accessed=1000, transcendentals=0),
        name="place",
    )(core, *parts, into)


def lse_of(parts, axis=None):
    if axis is None:
        top = functools.reduce(jnp.maximum, parts)
        return top + jnp.log(functools.reduce(jnp.add, [jnp.exp(p - top) for p in parts]))
    top = jnp.max(parts, axis)
    return top + jnp.log(jnp.sum(jnp.exp(parts - jnp.expand_dims(top, axis)), axis))


def body(embeddings, classifier, positives, counts):
    q_dev, width = embeddings.shape
    labels = classifier.shape[0] // 2
    xh, core, xl, z, y = (lax.axis_index(a) for a in AXES)
    rank = (xl * 8 + z) * 4 + y
    base = (rank * 2 + core) * labels

    blank = jnp.zeros((q_dev, 8 - POS), jnp.int32)
    extra = jnp.concatenate(
        [positives & 127, blank, (positives >> 7) & 127, blank, positives >> 14, blank, counts[:, None], jnp.zeros((q_dev, EXTRA - CNT - 1), jnp.int32)],
        1,
    ).astype(jnp.bfloat16)
    sent = jnp.concatenate([embeddings, extra], 1)
    spread = lambda x, n: jnp.broadcast_to(x[None], (n,) + x.shape).reshape((n * x.shape[0],) + x.shape[1:])
    column = lax.all_to_all(spread(sent, SIZES["z"]), "z", 0, 0, tiled=True)
    mine = lax.all_to_all(spread(column, 4), ("xh", "xl"), 0, 0, tiled=True)
    own = [mine, shift(mine, "y", -1), None, shift(mine, "y", 1)]
    relay = [(c * 4 + i, c * 4 + (i + 2 * c - 1) % 4) for c in range(2) for i in range(4)]
    own[2] = lax.ppermute(jnp.where(core == 0, own[1], own[3]), ("core", "y"), relay)
    w = lax.dynamic_slice_in_dim(classifier, core * labels, labels)
    rows = mine.shape[0]

    oth, parts = [None] * 4, [None] * 4
    for d in (0, 1, 3, 2):
        if d:
            done = (parts[1][1], parts[3][1]) if d == 2 else (parts[0][1],)
            own[d] = lax.optimization_barrier((own[d],) + done)[0]
        oth[d] = shift(own[d], "core", 1)
        parts[d] = scores_call(own[d], oth[d], w)
    es, ms, ls = zip(*parts)
    blocks = [b for pair in zip(own, oth) for b in pair]
    hits = hits_call(base[None], blocks, w)
    m = jnp.concatenate(ms, 0)
    stat = jnp.concatenate(ls, 0)
    stat = lse_of([stat, jnp.roll(shift(stat, "core", 1), rows, 1)])
    stat = lse_of([stat] + [jnp.roll(shift(stat, "y", -d), d, 0) for d in range(1, 4)])
    stat = stat.reshape(8, rows)
    lse = lse_of(lax.all_to_all(jnp.broadcast_to(stat[None], (16, 8, rows)), ("xl", "z"), 0, 0, tiled=True), 0)

    ps, u_own, u_oth = query_call(jnp.stack([xh, y]), hits, lse.reshape(4, 2 * rows), m, es, w)
    f32 = lambda a: a.astype(jnp.float32)
    u = (f32(u_own) + f32(shift(u_oth, "core", 1))).astype(jnp.bfloat16)
    first, u = lax.optimization_barrier((ps[0], u))
    got = lax.all_to_all(u, ("y", "xl", "z"), 0, 0, tiled=True)
    class_grad, sent_parts = None, []
    for j in range(PARTS):
        class_grad, mine_part = class_call(core[None], (first,) + tuple(ps[1:]), blocks, width, j, class_grad)
        sent_parts.append(shift(mine_part, "core", 1))
    class_grad = place_call(core[None], sent_parts, class_grad)

    final = jnp.sum(f32(got).reshape(64, q_dev, width + EXTRA), 0)
    query_grad = final[:, :width].astype(jnp.bfloat16)
    pos_mean = jnp.sum(final[:, width:width + 24], 1)
    at = ((xh * 2 + xl) * 8 + z) * q_dev
    loss = lax.dynamic_slice(lse, (0, at), (1, q_dev))[0] - pos_mean
    return loss, query_grad, class_grad


def solution(mesh):
    fine = Mesh(mesh.devices.reshape(tuple(SIZES[a] for a in AXES)), AXES)
    split = P(AXES, None)
    lab = P(("xl", "z", "y"), None)
    return jax.shard_map(
        body,
        mesh=fine,
        in_specs=(split, lab, split, P(AXES)),
        out_specs=(P(AXES), split, lab),
        check_vma=False,
    )
```

```python
import functools

import jax
import jax.numpy as jnp
from jax import lax
from jax.experimental import pallas as pl
from jax.experimental.pallas import tpu as pltpu
from jax.sharding import Mesh, PartitionSpec as P

AXES = ("xh", "core", "xl", "z", "y")
SIZES = {"xh": 2, "core": 2, "xl": 2, "z": 8, "y": 4}
EXTRA = 128
POS = 5
LO, MID, HI, CNT = 0, 8, 16, 24
VMEM = pl.BlockSpec(memory_space=pltpu.VMEM)
SMEM = pl.BlockSpec(memory_space=pltpu.SMEM)
ANY = pl.BlockSpec(memory_space=pl.ANY)
HBM = pl.BlockSpec(memory_space=pltpu.HBM)
NT = (((1,), (1,)), ((), ()))
TN = (((0,), (0,)), ((), ()))
LCH = 256
PROD = 1024
EXPO = 128
PARTS = 2
EARLY = 2
CLASS = 512


def shift(x, axis, step):
    n = SIZES[axis]
    return lax.ppermute(x, axis, [(i, (i + step) % n) for i in range(n)])


def in_hbm(arrays):
    return [pltpu.with_memory_space_constraint(a, pltpu.HBM) for a in arrays]


def scores_kernel(own_ref, oth_ref, w_ref, e_ref, m_ref, l_ref, q_ref, s_ref, qt_ref, held_ref, sem):
    labels, width = w_ref.shape
    rows = own_ref.shape[0]
    both = 2 * rows
    copies = [pltpu.make_async_copy(a, q_ref.at[k], sem.at[k]) for k, a in enumerate((own_ref, oth_ref))]
    for copy in copies:
        copy.start()
    for k, copy in enumerate(copies):
        copy.wait()
        qt_ref[:, k * rows:(k + 1) * rows] = q_ref[k, :, :width].T

    def product(i, top):
        at = pl.multiple_of(i * PROD, PROD)
        s = jnp.dot(w_ref[pl.ds(at, PROD), :], qt_ref[...], preferred_element_type=jnp.float32)
        s_ref[pl.ds(at, PROD), :] = s
        return jnp.maximum(top, jnp.max(s.reshape(PROD // 16, 16, both), 0))

    top = lax.fori_loop(0, labels // PROD, product, jnp.full((16, both), -1e30, jnp.float32))
    top = jnp.max(top, 0, keepdims=True)

    def leave(i):
        part = pl.ds(pl.multiple_of(i * EXPO, EXPO), EXPO)
        return pltpu.make_async_copy(held_ref.at[part, :], e_ref.at[part, :], sem.at[i])

    def expo(i, total):
        at = pl.multiple_of(i * EXPO, EXPO)
        e = jnp.exp(s_ref[pl.ds(at, EXPO), :] - top)
        held_ref[pl.ds(at, EXPO), :] = e.astype(jnp.bfloat16)
        leave(i).start()
        return total + jnp.sum(e.reshape(EXPO // 16, 16, both), 0)

    total = lax.fori_loop(0, labels // EXPO, expo, jnp.zeros((16, both), jnp.float32))
    m_ref[...] = top
    l_ref[...] = top + jnp.log(jnp.sum(total, 0, keepdims=True))

    def gone(i, carry):
        leave(i).wait()
        return carry

    lax.fori_loop(0, labels // EXPO, gone, 0)


def scores_call(own, oth, w):
    rows = own.shape[0]
    labels, width = w.shape
    line = jax.ShapeDtypeStruct((1, 2 * rows), jnp.float32)
    return pl.pallas_call(
        scores_kernel,
        out_shape=(pltpu.HBM((labels, 2 * rows), jnp.bfloat16), line, line),
        in_specs=[ANY, ANY, VMEM],
        out_specs=(HBM, VMEM, VMEM),
        scratch_shapes=[
            pltpu.VMEM((2,) + own.shape, jnp.bfloat16),
            pltpu.VMEM((labels, 2 * rows), jnp.float32),
            pltpu.VMEM((width, 2 * rows), jnp.bfloat16),
            pltpu.VMEM((labels, 2 * rows), jnp.bfloat16),
            pltpu.SemaphoreType.DMA((labels // EXPO,)),
        ],
        compiler_params=pltpu.CompilerParams(vmem_limit_bytes=18 * 2**20),
        cost_estimate=pl.CostEstimate(flops=1000, bytes_accessed=1000, transcendentals=0),
        name="scores",
    )(own, oth, w)


def hits_kernel(base_ref, *refs):
    count = len(refs) - 7
    sources = refs[:count]
    w_ref, n_ref, key_ref, s_ref, t_ref, blocks, sem = refs[count:]
    copies = [pltpu.make_async_copy(q, blocks.at[b], sem.at[b]) for b, q in enumerate(sources)]
    for copy in copies:
        copy.start()
    labels, width = w_ref.shape
    base = base_ref[0].astype(jnp.float32)
    row = lax.broadcasted_iota(jnp.int32, (8, EXTRA), 0)
    col = lax.broadcasted_iota(jnp.int32, (8, EXTRA), 1)
    digits = jnp.where(col == row + LO, 1.0, jnp.where(col == row + MID, 128.0, jnp.where(col == row + HI, 16384.0, 0.0)))
    digits = jnp.where(row < POS, digits, 0.0).astype(jnp.bfloat16)
    counting = jnp.where(col == CNT, 1.0, 0.0).astype(jnp.bfloat16)
    big = 1e9
    rows = blocks.shape[1]
    slot = lax.broadcasted_iota(jnp.int32, (8, rows), 0)
    lane = lax.broadcasted_iota(jnp.int32, (8, rows), 1)
    keys, weights, most = [], [], jnp.int32(0)
    for b in range(count):
        copies[b].wait()
        extra = blocks[b, :, width:]
        ids = lax.dot_general(digits, extra, NT, preferred_element_type=jnp.float32)
        cnt = lax.dot_general(counting, extra, NT, preferred_element_type=jnp.float32)
        valid = (slot.astype(jnp.float32) < cnt) & (slot < POS)
        ids = jnp.where(valid, ids, -1.0)
        same = jnp.zeros((8, rows), jnp.float32)
        again = jnp.zeros((8, rows), jnp.float32)
        for j in range(POS):
            eq = jnp.where(ids == ids[j:j + 1, :], 1.0, 0.0)
            same = same + eq
            again = again + jnp.where(slot > j, eq, 0.0)
        local = ids - base
        hit = valid & (local >= 0.0) & (local < float(labels)) & (again == 0.0)
        weights.append(same / cnt)
        keys.append(jnp.where(hit, (lane * 8 + slot).astype(jnp.float32) * float(labels) + local, big))
        n = jnp.sum(jnp.where(hit, 1.0, 0.0)).astype(jnp.int32)
        n_ref[b] = n
        most = jnp.maximum(most, n)
    r16 = lax.broadcasted_iota(jnp.int32, (16, width), 0)

    def step(i, keys):
        least = [jnp.min(k) for k in keys]
        found = [jnp.where(k < big, k, 0.0).astype(jnp.int32) for k in least]
        same = [k == kf for k, kf in zip(keys, least)]
        score, weight = [], []
        for b, k in enumerate(found):
            label = k & (labels - 1)
            query = lax.div(k, 8 * labels)
            qat = pl.multiple_of((query >> 4) << 4, 16)
            lat = pl.multiple_of((label >> 4) << 4, 16)
            row_q = jnp.where(r16 == query - qat, blocks[b, pl.ds(qat, 16), :width].astype(jnp.float32), 0.0)
            row_w = jnp.where(r16 == label - lat, w_ref[pl.ds(lat, 16), :].astype(jnp.float32), 0.0)
            score.append(jnp.sum(row_w * jnp.sum(row_q, 0, keepdims=True)))
            weight.append(jnp.sum(jnp.where(same[b], weights[b], 0.0)))
        for b in range(count):
            at = b * rows * POS + i
            key_ref[at] = found[b]
            s_ref[at] = score[b]
            t_ref[at] = weight[b]
        return tuple(jnp.where(t, big, k) for t, k in zip(same, keys))

    lax.fori_loop(0, most, step, tuple(keys))


def hits_call(base, blocks, w):
    count = len(blocks)
    total = count * blocks[0].shape[0] * POS
    return pl.pallas_call(
        hits_kernel,
        out_shape=(
            jax.ShapeDtypeStruct((count,), jnp.int32),
            jax.ShapeDtypeStruct((total,), jnp.int32),
            jax.ShapeDtypeStruct((total,), jnp.float32),
            jax.ShapeDtypeStruct((total,), jnp.float32),
        ),
        in_specs=[SMEM] + [HBM] * count + [VMEM],
        out_specs=(SMEM,) * 4,
        scratch_shapes=[pltpu.VMEM((count,) + blocks[0].shape, jnp.bfloat16), pltpu.SemaphoreType.DMA((count,))],
        compiler_params=pltpu.CompilerParams(vmem_limit_bytes=16 * 2**20),
        cost_estimate=pl.CostEstimate(flops=1000, bytes_accessed=1000, transcendentals=0),
        name="hits",
    )(base, *in_hbm(blocks), w)


def query_kernel(at_ref, na, ka, sa, ta, nb, kb, sb, tb, lse_ref, m_ref, e0, e1, e2, e3, w_ref, *outs):
    own_ref, oth_ref, pos_ref, held, sem = outs[4:]
    ps = [held.at[d] for d in range(4)]
    copies = [pltpu.make_async_copy(e, p, sem.at[d]) for d, (e, p) in enumerate(zip((e0, e1, e2, e3), ps))]
    for copy in copies:
        copy.start()
    labels, width = w_ref.shape
    rows = e0.shape[1] // 2
    xh, y = at_ref[0], at_ref[1]
    half = rows // 2
    pos_ref[...] = jnp.zeros_like(pos_ref)
    for d, p_ref in enumerate(ps):
        copies[d].wait()
        scale = jnp.exp(m_ref[d:d + 1, :] - lse_ref[d:d + 1, :])

        def scaled(i, carry):
            at = pl.multiple_of(i * 64, 64)
            p_ref[pl.ds(at, 64), :] = (p_ref[pl.ds(at, 64), :].astype(jnp.float32) * scale).astype(jnp.bfloat16)
            return carry

        lax.fori_loop(0, labels // 64, scaled, 0)

    r = lax.broadcasted_iota(jnp.int32, (16, half), 0)
    c = lax.broadcasted_iota(jnp.int32, (16, half), 1)
    c1 = lax.broadcasted_iota(jnp.int32, (1, EXTRA), 1)
    most = jnp.int32(0)
    for b in range(8):
        most = jnp.maximum(most, na[b] if b < EARLY else nb[b - EARLY])

    def patch(i, carry):
        todo = []
        for b in range(8):
            d, k = b // 2, b % 2
            n_ref, key_ref, s_ref, t_ref = (na, ka, sa, ta) if b < EARLY else (nb, kb, sb, tb)
            spot = b if b < EARLY else b - EARLY
            at = spot * rows * POS + i
            live = i < n_ref[spot]
            key, s, weight = jnp.where(live, key_ref[at], 0), s_ref[at], t_ref[at]
            label = key & (labels - 1)
            rest = lax.div(key, labels)
            slot = rest & 7
            query = rest >> 3
            lat = pl.multiple_of((label >> 4) << 4, 16)
            qhi = lax.div(query, half)
            qlo = query & (half - 1)
            qat = pl.multiple_of(k * rows + qhi * half, half)
            spot = (pl.ds(lat, 16), pl.ds(qat, half))
            value = jnp.exp(s - lse_ref[d:d + 1, pl.ds(qat, half)]) - weight
            row = jnp.where(live, label - lat, -1)
            old = ps[d][spot].astype(jnp.float32)
            new = jnp.where((r == row) & (c == qlo), value, old).astype(jnp.bfloat16)
            full = jnp.full((1, EXTRA), s * weight, jnp.float32)
            high = full.astype(jnp.bfloat16).astype(jnp.float32)
            mid = (full - high).astype(jnp.bfloat16).astype(jnp.float32)
            low = full - high - mid
            put = jnp.where(c1 == slot, high, jnp.where(c1 == slot + 8, mid, jnp.where(c1 == slot + 16, low, 0.0)))
            put = jnp.where(jnp.logical_and(live, qhi == xh), put, 0.0)
            into = (k, pl.ds(d * half + qlo, 1), slice(None))
            todo.append((d, spot, new, into, pos_ref[into] + put))
        for d, spot, new, into, pos in todo:
            ps[d][spot] = new
            pos_ref[into] = pos
        return carry

    lax.fori_loop(0, most, patch, 0)
    copies = [pltpu.make_async_copy(p, out, sem.at[d]) for d, (p, out) in enumerate(zip(ps, outs))]
    for copy in copies:
        copy.start()
    for d, p_ref in enumerate(ps):
        both = jnp.concatenate([p_ref[:, pl.ds(pl.multiple_of(k * rows + xh * half, half), half)] for k in range(2)], 1)
        u = lax.dot_general(both, w_ref[...], TN, preferred_element_type=jnp.float32)
        to = pl.ds(pl.multiple_of(((y + d) & 3) * half, half), half)
        for k, out in enumerate((own_ref, oth_ref)):
            out[to, :width] = u[k * half:(k + 1) * half].astype(jnp.bfloat16)
            out[to, width:] = pos_ref[k, d * half:(d + 1) * half, :].astype(jnp.bfloat16)
    for copy in copies:
        copy.wait()


def query_call(at, hits, lse, m, es, w):
    labels, width = w.shape
    rows = es[0].shape[1] // 2
    out = jax.ShapeDtypeStruct((2 * rows, width + EXTRA), jnp.bfloat16)
    res = pl.pallas_call(
        query_kernel,
        out_shape=tuple(pltpu.HBM(e.shape, e.dtype) for e in es) + (out, out),
        in_specs=[SMEM] * 9 + [VMEM] * 2 + [HBM] * 4 + [VMEM],
        out_specs=(HBM,) * 4 + (VMEM,) * 2,
        scratch_shapes=[pltpu.VMEM((2, 2 * rows, EXTRA), jnp.float32), pltpu.VMEM((4,) + es[0].shape, jnp.bfloat16), pltpu.SemaphoreType.DMA((4,))],
        compiler_params=pltpu.CompilerParams(vmem_limit_bytes=28 * 2**20),
        cost_estimate=pl.CostEstimate(flops=8 * rows * labels * width, bytes_accessed=2**24, transcendentals=0),
        name="query_part",
    )(at, *hits[0], *hits[1], lse, m, *in_hbm(es), w)
    return res[:4], res[4], res[5]


def class_kernel(core_ref, p0, p1, p2, p3, *refs):
    blocks = refs[:8]
    out_ref, mine_ref = refs[-2:]
    rows = blocks[0].shape[0]
    width = out_ref.shape[1]
    acc = None
    for d, p_ref in enumerate((p0, p1, p2, p3)):
        for k in range(2):
            term = jnp.dot(p_ref[:, k * rows:(k + 1) * rows], blocks[2 * d + k][:, :width], preferred_element_type=jnp.float32)
            acc = term if acc is None else acc + term
    done = acc.astype(jnp.bfloat16)
    out_ref[...] = done
    mine_ref[...] = done


def class_call(core, ps, blocks, width, part, before):
    labels = ps[0].shape[0]
    steps = labels // CLASS
    each = steps // PARTS
    rows = blocks[0].shape[0]
    whole = lambda i, c: (0, 0)
    kept = () if before is None else (before,)
    return pl.pallas_call(
        class_kernel,
        out_shape=tuple(jax.ShapeDtypeStruct((n, width), jnp.bfloat16) for n in (2 * labels, labels // PARTS)),
        grid_spec=pltpu.PrefetchScalarGridSpec(
            num_scalar_prefetch=1,
            grid=(each,),
            in_specs=[pl.BlockSpec((CLASS, 2 * rows), lambda i, c: (part * each + i, 0))] * 4
            + [pl.BlockSpec(blocks[0].shape, whole)] * 8
            + [HBM] * len(kept),
            out_specs=(
                pl.BlockSpec((CLASS, width), lambda i, c: (c[0] * steps + part * each + i, 0)),
                pl.BlockSpec((CLASS, width), lambda i, c: (i, 0)),
            ),
        ),
        input_output_aliases={13: 0} if kept else {},
        compiler_params=pltpu.CompilerParams(vmem_limit_bytes=24 * 2**20),
        cost_estimate=pl.CostEstimate(flops=16 * rows * labels * width // PARTS, bytes_accessed=2**23, transcendentals=0),
        name="class_part",
    )(core, *in_hbm(ps), *blocks, *kept)


def place_kernel(core_ref, *refs):
    parts, out_ref, sem = refs[:PARTS], refs[-2], refs[-1]
    rows = parts[0].shape[0]
    first = (1 - core_ref[0]) * (PARTS * rows)
    copies = [
        pltpu.make_async_copy(p, out_ref.at[pl.ds(pl.multiple_of(first + j * rows, rows), rows), :], sem.at[j]) for j, p in enumerate(parts)
    ]
    for copy in copies:
        copy.start()
    for copy in copies:
        copy.wait()


def place_call(core, parts, into):
    return pl.pallas_call(
        place_kernel,
        out_shape=jax.ShapeDtypeStruct(into.shape, into.dtype),
        in_specs=[SMEM] + [VMEM] * PARTS + [HBM],
        out_specs=HBM,
        scratch_shapes=[pltpu.SemaphoreType.DMA((PARTS,))],
        input_output_aliases={1 + PARTS: 0},
        compiler_params=pltpu.CompilerParams(vmem_limit_bytes=8 * 2**20),
        cost_estimate=pl.CostEstimate(flops=1000, bytes_accessed=1000, transcendentals=0),
        name="place",
    )(core, *parts, into)


def lse_of(parts, axis=None):
    if axis is None:
        top = functools.reduce(jnp.maximum, parts)
        return top + jnp.log(functools.reduce(jnp.add, [jnp.exp(p - top) for p in parts]))
    top = jnp.max(parts, axis)
    return top + jnp.log(jnp.sum(jnp.exp(parts - jnp.expand_dims(top, axis)), axis))


def body(embeddings, classifier, positives, counts):
    q_dev, width = embeddings.shape
    labels = classifier.shape[0] // 2
    xh, core, xl, z, y = (lax.axis_index(a) for a in AXES)
    rank = (xl * 8 + z) * 4 + y
    base = (rank * 2 + core) * labels

    blank = jnp.zeros((q_dev, 8 - POS), jnp.int32)
    extra = jnp.concatenate(
        [positives & 127, blank, (positives >> 7) & 127, blank, positives >> 14, blank, counts[:, None], jnp.zeros((q_dev, EXTRA - CNT - 1), jnp.int32)],
        1,
    ).astype(jnp.bfloat16)
    sent = jnp.concatenate([embeddings, extra], 1)
    spread = lambda x, n: jnp.broadcast_to(x[None], (n,) + x.shape).reshape((n * x.shape[0],) + x.shape[1:])
    column = lax.all_to_all(spread(sent, SIZES["z"]), "z", 0, 0, tiled=True)
    mine = lax.all_to_all(spread(column, 4), ("xh", "xl"), 0, 0, tiled=True)
    own = [mine, shift(mine, "y", -1), None, shift(mine, "y", 1)]
    relay = [(c * 4 + i, c * 4 + (i + 2 * c - 1) % 4) for c in range(2) for i in range(4)]
    own[2] = lax.ppermute(jnp.where(core == 0, own[1], own[3]), ("core", "y"), relay)
    w = lax.dynamic_slice_in_dim(classifier, core * labels, labels)
    rows = mine.shape[0]

    oth, parts = [None] * 4, [None] * 4
    for d in (0, 1, 3, 2):
        if d:
            done = (parts[1][1], parts[3][1]) if d == 2 else (hits[0][0],)
            own[d] = lax.optimization_barrier((own[d],) + done)[0]
        oth[d] = shift(own[d], "core", 1)
        parts[d] = scores_call(own[d], oth[d], w)
        if d == 0:
            first = lax.optimization_barrier((own[0], parts[0][1]))[0]
            hits = [hits_call(base[None], (first, oth[0]), w)]
    es, ms, ls = zip(*parts)
    blocks = [b for pair in zip(own, oth) for b in pair]
    hits.append(hits_call(base[None], blocks[EARLY:], w))
    m = jnp.concatenate(ms, 0)
    stat = jnp.concatenate(ls, 0)
    stat = lse_of([stat, jnp.roll(shift(stat, "core", 1), rows, 1)])
    stat = lse_of([stat] + [jnp.roll(shift(stat, "y", -d), d, 0) for d in range(1, 4)])
    stat = stat.reshape(8, rows)
    lse = lse_of(lax.all_to_all(jnp.broadcast_to(stat[None], (16, 8, rows)), ("xl", "z"), 0, 0, tiled=True), 0)

    ps, u_own, u_oth = query_call(jnp.stack([xh, y]), hits, lse.reshape(4, 2 * rows), m, es, w)
    f32 = lambda a: a.astype(jnp.float32)
    u = (f32(u_own) + f32(shift(u_oth, "core", 1))).astype(jnp.bfloat16)
    first, u = lax.optimization_barrier((ps[0], u))
    got = lax.all_to_all(u, ("y", "xl", "z"), 0, 0, tiled=True)
    class_grad, sent_parts = None, []
    for j in range(PARTS):
        class_grad, mine_part = class_call(core[None], (first,) + tuple(ps[1:]), blocks, width, j, class_grad)
        sent_parts.append(shift(mine_part, "core", 1))
    class_grad = place_call(core[None], sent_parts, class_grad)

    final = jnp.sum(f32(got).reshape(64, q_dev, width + EXTRA), 0)
    query_grad = final[:, :width].astype(jnp.bfloat16)
    pos_mean = jnp.sum(final[:, width:width + 24], 1)
    at = ((xh * 2 + xl) * 8 + z) * q_dev
    loss = lax.dynamic_slice(lse, (0, at), (1, q_dev))[0] - pos_mean
    return loss, query_grad, class_grad


def solution(mesh):
    fine = Mesh(mesh.devices.reshape(tuple(SIZES[a] for a in AXES)), AXES)
    split = P(AXES, None)
    lab = P(("xl", "z", "y"), None)
    return jax.shard_map(
        body,
        mesh=fine,
        in_specs=(split, lab, split, P(AXES)),
        out_specs=(P(AXES), split, lab),
        check_vma=False,
    )
```

```python
import functools

import jax
import jax.numpy as jnp
from jax import lax
from jax.experimental import pallas as pl
from jax.experimental.pallas import tpu as pltpu
from jax.sharding import Mesh, PartitionSpec as P

AXES = ("xh", "core", "xl", "z", "y")
SIZES = {"xh": 2, "core": 2, "xl": 2, "z": 8, "y": 4}
EXTRA = 128
POS = 5
LO, MID, HI, CNT = 0, 8, 16, 24
VMEM = pl.BlockSpec(memory_space=pltpu.VMEM)
SMEM = pl.BlockSpec(memory_space=pltpu.SMEM)
ANY = pl.BlockSpec(memory_space=pl.ANY)
HBM = pl.BlockSpec(memory_space=pltpu.HBM)
NT = (((1,), (1,)), ((), ()))
TN = (((0,), (0,)), ((), ()))
LCH = 256
PROD = 1024
EXPO = 128
SPLIT = (2, 2)
PARTS = len(SPLIT)
EARLY = 2
CLASS = 512


def shift(x, axis, step):
    n = SIZES[axis]
    return lax.ppermute(x, axis, [(i, (i + step) % n) for i in range(n)])


def in_hbm(arrays):
    return [pltpu.with_memory_space_constraint(a, pltpu.HBM) for a in arrays]


def scores_kernel(own_ref, oth_ref, w_ref, e_ref, m_ref, l_ref, q_ref, s_ref, qt_ref, held_ref, sem):
    labels, width = w_ref.shape
    rows = own_ref.shape[0]
    both = 2 * rows
    copies = [pltpu.make_async_copy(a, q_ref.at[k], sem.at[k]) for k, a in enumerate((own_ref, oth_ref))]
    for copy in copies:
        copy.start()
    for k, copy in enumerate(copies):
        copy.wait()
        qt_ref[:, k * rows:(k + 1) * rows] = q_ref[k, :, :width].T

    def product(i, top):
        at = pl.multiple_of(i * PROD, PROD)
        s = jnp.dot(w_ref[pl.ds(at, PROD), :], qt_ref[...], preferred_element_type=jnp.float32)
        s_ref[pl.ds(at, PROD), :] = s
        return jnp.maximum(top, jnp.max(s.reshape(PROD // 16, 16, both), 0))

    top = lax.fori_loop(0, labels // PROD, product, jnp.full((16, both), -1e30, jnp.float32))
    top = jnp.max(top, 0, keepdims=True)

    def leave(i):
        part = pl.ds(pl.multiple_of(i * EXPO, EXPO), EXPO)
        return pltpu.make_async_copy(held_ref.at[part, :], e_ref.at[part, :], sem.at[i])

    def expo(i, total):
        at = pl.multiple_of(i * EXPO, EXPO)
        e = jnp.exp(s_ref[pl.ds(at, EXPO), :] - top)
        held_ref[pl.ds(at, EXPO), :] = e.astype(jnp.bfloat16)
        leave(i).start()
        return total + jnp.sum(e.reshape(EXPO // 16, 16, both), 0)

    total = lax.fori_loop(0, labels // EXPO, expo, jnp.zeros((16, both), jnp.float32))
    m_ref[...] = top
    l_ref[...] = top + jnp.log(jnp.sum(total, 0, keepdims=True))

    def gone(i, carry):
        leave(i).wait()
        return carry

    lax.fori_loop(0, labels // EXPO, gone, 0)


def scores_call(own, oth, w):
    rows = own.shape[0]
    labels, width = w.shape
    line = jax.ShapeDtypeStruct((1, 2 * rows), jnp.float32)
    return pl.pallas_call(
        scores_kernel,
        out_shape=(pltpu.HBM((labels, 2 * rows), jnp.bfloat16), line, line),
        in_specs=[ANY, ANY, VMEM],
        out_specs=(HBM, VMEM, VMEM),
        scratch_shapes=[
            pltpu.VMEM((2,) + own.shape, jnp.bfloat16),
            pltpu.VMEM((labels, 2 * rows), jnp.float32),
            pltpu.VMEM((width, 2 * rows), jnp.bfloat16),
            pltpu.VMEM((labels, 2 * rows), jnp.bfloat16),
            pltpu.SemaphoreType.DMA((labels // EXPO,)),
        ],
        compiler_params=pltpu.CompilerParams(vmem_limit_bytes=18 * 2**20),
        cost_estimate=pl.CostEstimate(flops=1000, bytes_accessed=1000, transcendentals=0),
        name="scores",
    )(own, oth, w)


def hits_kernel(base_ref, *refs):
    count = len(refs) - 7
    sources = refs[:count]
    w_ref, n_ref, key_ref, s_ref, t_ref, blocks, sem = refs[count:]
    copies = [pltpu.make_async_copy(q, blocks.at[b], sem.at[b]) for b, q in enumerate(sources)]
    for copy in copies:
        copy.start()
    labels, width = w_ref.shape
    base = base_ref[0].astype(jnp.float32)
    row = lax.broadcasted_iota(jnp.int32, (8, EXTRA), 0)
    col = lax.broadcasted_iota(jnp.int32, (8, EXTRA), 1)
    digits = jnp.where(col == row + LO, 1.0, jnp.where(col == row + MID, 128.0, jnp.where(col == row + HI, 16384.0, 0.0)))
    digits = jnp.where(row < POS, digits, 0.0).astype(jnp.bfloat16)
    counting = jnp.where(col == CNT, 1.0, 0.0).astype(jnp.bfloat16)
    big = 1e9
    rows = blocks.shape[1]
    slot = lax.broadcasted_iota(jnp.int32, (8, rows), 0)
    lane = lax.broadcasted_iota(jnp.int32, (8, rows), 1)
    keys, weights, most = [], [], jnp.int32(0)
    for b in range(count):
        copies[b].wait()
        extra = blocks[b, :, width:]
        ids = lax.dot_general(digits, extra, NT, preferred_element_type=jnp.float32)
        cnt = lax.dot_general(counting, extra, NT, preferred_element_type=jnp.float32)
        valid = (slot.astype(jnp.float32) < cnt) & (slot < POS)
        ids = jnp.where(valid, ids, -1.0)
        same = jnp.zeros((8, rows), jnp.float32)
        again = jnp.zeros((8, rows), jnp.float32)
        for j in range(POS):
            eq = jnp.where(ids == ids[j:j + 1, :], 1.0, 0.0)
            same = same + eq
            again = again + jnp.where(slot > j, eq, 0.0)
        local = ids - base
        hit = valid & (local >= 0.0) & (local < float(labels)) & (again == 0.0)
        weights.append(same / cnt)
        keys.append(jnp.where(hit, (lane * 8 + slot).astype(jnp.float32) * float(labels) + local, big))
        n = jnp.sum(jnp.where(hit, 1.0, 0.0)).astype(jnp.int32)
        n_ref[b] = n
        most = jnp.maximum(most, n)
    r16 = lax.broadcasted_iota(jnp.int32, (16, width), 0)

    def step(i, keys):
        least = [jnp.min(k) for k in keys]
        found = [jnp.where(k < big, k, 0.0).astype(jnp.int32) for k in least]
        same = [k == kf for k, kf in zip(keys, least)]
        score, weight = [], []
        for b, k in enumerate(found):
            label = k & (labels - 1)
            query = lax.div(k, 8 * labels)
            qat = pl.multiple_of((query >> 4) << 4, 16)
            lat = pl.multiple_of((label >> 4) << 4, 16)
            row_q = jnp.where(r16 == query - qat, blocks[b, pl.ds(qat, 16), :width].astype(jnp.float32), 0.0)
            row_w = jnp.where(r16 == label - lat, w_ref[pl.ds(lat, 16), :].astype(jnp.float32), 0.0)
            score.append(jnp.sum(row_w * jnp.sum(row_q, 0, keepdims=True)))
            weight.append(jnp.sum(jnp.where(same[b], weights[b], 0.0)))
        for b in range(count):
            at = b * rows * POS + i
            key_ref[at] = found[b]
            s_ref[at] = score[b]
            t_ref[at] = weight[b]
        return tuple(jnp.where(t, big, k) for t, k in zip(same, keys))

    lax.fori_loop(0, most, step, tuple(keys))


def hits_call(base, blocks, w):
    count = len(blocks)
    total = count * blocks[0].shape[0] * POS
    return pl.pallas_call(
        hits_kernel,
        out_shape=(
            jax.ShapeDtypeStruct((count,), jnp.int32),
            jax.ShapeDtypeStruct((total,), jnp.int32),
            jax.ShapeDtypeStruct((total,), jnp.float32),
            jax.ShapeDtypeStruct((total,), jnp.float32),
        ),
        in_specs=[SMEM] + [HBM] * count + [VMEM],
        out_specs=(SMEM,) * 4,
        scratch_shapes=[pltpu.VMEM((count,) + blocks[0].shape, jnp.bfloat16), pltpu.SemaphoreType.DMA((count,))],
        compiler_params=pltpu.CompilerParams(vmem_limit_bytes=16 * 2**20),
        cost_estimate=pl.CostEstimate(flops=1000, bytes_accessed=1000, transcendentals=0),
        name="hits",
    )(base, *in_hbm(blocks), w)


def query_kernel(at_ref, na, ka, sa, ta, nb, kb, sb, tb, lse_ref, m_ref, e0, e1, e2, e3, w_ref, *outs):
    own_ref, oth_ref, pos_ref, held, sem = outs[4:]
    ps = [held.at[d] for d in range(4)]
    copies = [pltpu.make_async_copy(e, p, sem.at[d]) for d, (e, p) in enumerate(zip((e0, e1, e2, e3), ps))]
    for copy in copies:
        copy.start()
    labels, width = w_ref.shape
    rows = e0.shape[1] // 2
    xh, y = at_ref[0], at_ref[1]
    half = rows // 2
    pos_ref[...] = jnp.zeros_like(pos_ref)
    for d, p_ref in enumerate(ps):
        copies[d].wait()
        scale = jnp.exp(m_ref[d:d + 1, :] - lse_ref[d:d + 1, :])

        def scaled(i, carry):
            at = pl.multiple_of(i * 64, 64)
            p_ref[pl.ds(at, 64), :] = (p_ref[pl.ds(at, 64), :].astype(jnp.float32) * scale).astype(jnp.bfloat16)
            return carry

        lax.fori_loop(0, labels // 64, scaled, 0)

    r = lax.broadcasted_iota(jnp.int32, (16, half), 0)
    c = lax.broadcasted_iota(jnp.int32, (16, half), 1)
    c1 = lax.broadcasted_iota(jnp.int32, (1, EXTRA), 1)
    most = jnp.int32(0)
    for b in range(8):
        most = jnp.maximum(most, na[b] if b < EARLY else nb[b - EARLY])

    def patch(i, carry):
        todo = []
        for b in range(8):
            d, k = b // 2, b % 2
            n_ref, key_ref, s_ref, t_ref = (na, ka, sa, ta) if b < EARLY else (nb, kb, sb, tb)
            spot = b if b < EARLY else b - EARLY
            at = spot * rows * POS + i
            live = i < n_ref[spot]
            key, s, weight = jnp.where(live, key_ref[at], 0), s_ref[at], t_ref[at]
            label = key & (labels - 1)
            rest = lax.div(key, labels)
            slot = rest & 7
            query = rest >> 3
            lat = pl.multiple_of((label >> 4) << 4, 16)
            qhi = lax.div(query, half)
            qlo = query & (half - 1)
            qat = pl.multiple_of(k * rows + qhi * half, half)
            spot = (pl.ds(lat, 16), pl.ds(qat, half))
            value = jnp.exp(s - lse_ref[d:d + 1, pl.ds(qat, half)]) - weight
            row = jnp.where(live, label - lat, -1)
            old = ps[d][spot].astype(jnp.float32)
            new = jnp.where((r == row) & (c == qlo), value, old).astype(jnp.bfloat16)
            full = jnp.full((1, EXTRA), s * weight, jnp.float32)
            high = full.astype(jnp.bfloat16).astype(jnp.float32)
            mid = (full - high).astype(jnp.bfloat16).astype(jnp.float32)
            low = full - high - mid
            put = jnp.where(c1 == slot, high, jnp.where(c1 == slot + 8, mid, jnp.where(c1 == slot + 16, low, 0.0)))
            put = jnp.where(jnp.logical_and(live, qhi == xh), put, 0.0)
            into = (k, pl.ds(d * half + qlo, 1), slice(None))
            todo.append((d, spot, new, into, pos_ref[into] + put))
        for d, spot, new, into, pos in todo:
            ps[d][spot] = new
            pos_ref[into] = pos
        return carry

    lax.fori_loop(0, most, patch, 0)
    copies = [pltpu.make_async_copy(p, out, sem.at[d]) for d, (p, out) in enumerate(zip(ps, outs))]
    for copy in copies:
        copy.start()
    for d, p_ref in enumerate(ps):
        both = jnp.concatenate([p_ref[:, pl.ds(pl.multiple_of(k * rows + xh * half, half), half)] for k in range(2)], 1)
        u = lax.dot_general(both, w_ref[...], TN, preferred_element_type=jnp.float32)
        to = pl.ds(pl.multiple_of(((y + d) & 3) * half, half), half)
        for k, out in enumerate((own_ref, oth_ref)):
            out[to, :width] = u[k * half:(k + 1) * half].astype(jnp.bfloat16)
            out[to, width:] = pos_ref[k, d * half:(d + 1) * half, :].astype(jnp.bfloat16)
    for copy in copies:
        copy.wait()


def query_call(at, hits, lse, m, es, w):
    labels, width = w.shape
    rows = es[0].shape[1] // 2
    out = jax.ShapeDtypeStruct((2 * rows, width + EXTRA), jnp.bfloat16)
    res = pl.pallas_call(
        query_kernel,
        out_shape=tuple(pltpu.HBM(e.shape, e.dtype) for e in es) + (out, out),
        in_specs=[SMEM] * 9 + [VMEM] * 2 + [HBM] * 4 + [VMEM],
        out_specs=(HBM,) * 4 + (VMEM,) * 2,
        scratch_shapes=[pltpu.VMEM((2, 2 * rows, EXTRA), jnp.float32), pltpu.VMEM((4,) + es[0].shape, jnp.bfloat16), pltpu.SemaphoreType.DMA((4,))],
        compiler_params=pltpu.CompilerParams(vmem_limit_bytes=28 * 2**20),
        cost_estimate=pl.CostEstimate(flops=8 * rows * labels * width, bytes_accessed=2**24, transcendentals=0),
        name="query_part",
    )(at, *hits[0], *hits[1], lse, m, *in_hbm(es), w)
    return res[:4], res[4], res[5]


def class_kernel(core_ref, p0, p1, p2, p3, *refs):
    blocks = refs[:8]
    out_ref, mine_ref = refs[-2:]
    rows = blocks[0].shape[0]
    width = out_ref.shape[1]
    acc = None
    for d, p_ref in enumerate((p0, p1, p2, p3)):
        for k in range(2):
            term = jnp.dot(p_ref[:, k * rows:(k + 1) * rows], blocks[2 * d + k][:, :width], preferred_element_type=jnp.float32)
            acc = term if acc is None else acc + term
    done = acc.astype(jnp.bfloat16)
    out_ref[...] = done
    mine_ref[...] = done


def class_call(core, ps, blocks, width, part, before):
    labels = ps[0].shape[0]
    steps = labels // CLASS
    start, each = sum(SPLIT[:part]), SPLIT[part]
    rows = blocks[0].shape[0]
    whole = lambda i, c: (0, 0)
    kept = () if before is None else (before,)
    return pl.pallas_call(
        class_kernel,
        out_shape=tuple(jax.ShapeDtypeStruct((n, width), jnp.bfloat16) for n in (2 * labels, each * CLASS)),
        grid_spec=pltpu.PrefetchScalarGridSpec(
            num_scalar_prefetch=1,
            grid=(each,),
            in_specs=[pl.BlockSpec((CLASS, 2 * rows), lambda i, c: (start + i, 0))] * 4
            + [pl.BlockSpec(blocks[0].shape, whole)] * 8
            + [HBM] * len(kept),
            out_specs=(
                pl.BlockSpec((CLASS, width), lambda i, c: (c[0] * steps + start + i, 0)),
                pl.BlockSpec((CLASS, width), lambda i, c: (i, 0)),
            ),
        ),
        input_output_aliases={13: 0} if kept else {},
        compiler_params=pltpu.CompilerParams(vmem_limit_bytes=24 * 2**20),
        cost_estimate=pl.CostEstimate(flops=16 * rows * each * CLASS * width, bytes_accessed=2**23, transcendentals=0),
        name="class_part",
    )(core, *in_hbm(ps), *blocks, *kept)


def place_kernel(core_ref, *refs):
    parts, out_ref, sem = refs[:PARTS], refs[-2], refs[-1]
    first = (1 - core_ref[0]) * (out_ref.shape[0] // 2)
    copies = [
        pltpu.make_async_copy(p, out_ref.at[pl.ds(pl.multiple_of(first + sum(SPLIT[:j]) * CLASS, CLASS), p.shape[0]), :], sem.at[j])
        for j, p in enumerate(parts)
    ]
    for copy in copies:
        copy.start()
    for copy in copies:
        copy.wait()


def place_call(core, parts, into):
    return pl.pallas_call(
        place_kernel,
        out_shape=jax.ShapeDtypeStruct(into.shape, into.dtype),
        in_specs=[SMEM] + [VMEM] * PARTS + [HBM],
        out_specs=HBM,
        scratch_shapes=[pltpu.SemaphoreType.DMA((PARTS,))],
        input_output_aliases={1 + PARTS: 0},
        compiler_params=pltpu.CompilerParams(vmem_limit_bytes=8 * 2**20),
        cost_estimate=pl.CostEstimate(flops=1000, bytes_accessed=1000, transcendentals=0),
        name="place",
    )(core, *parts, into)


def pack_kernel(counts_ref, emb_ref, pos_ref, out_ref):
    q_dev = emb_ref.shape[0]
    row = lax.broadcasted_iota(jnp.int32, (q_dev, EXTRA), 0)
    lane = lax.broadcasted_iota(jnp.int32, (q_dev, EXTRA), 1)
    extra = jnp.zeros((q_dev, EXTRA), jnp.int32)
    for j in range(POS):
        ids = pos_ref[:, j:j + 1]
        for first, digit in ((LO, ids & 127), (MID, (ids >> 7) & 127), (HI, ids >> 14)):
            extra = jnp.where(lane == first + j, digit, extra)
    for i in range(q_dev):
        extra = jnp.where((row == i) & (lane == CNT), counts_ref[i], extra)
    one = jnp.concatenate([emb_ref[...].astype(jnp.float32), extra.astype(jnp.float32)], 1)
    two = jnp.concatenate([one, one], 0).astype(jnp.bfloat16)
    for i in range(out_ref.shape[0] // two.shape[0]):
        out_ref[i * two.shape[0]:(i + 1) * two.shape[0], :] = two


def pack_call(embeddings, positives, counts):
    q_dev, width = embeddings.shape
    return pl.pallas_call(
        pack_kernel,
        out_shape=jax.ShapeDtypeStruct((SIZES["z"] * q_dev, width + EXTRA), jnp.bfloat16),
        in_specs=[SMEM, VMEM, VMEM],
        out_specs=VMEM,
        name="pack",
    )(counts, embeddings, positives)


def close_kernel(got_ref, grad_ref, tail_ref):
    q_dev, width = grad_ref.shape
    step = 2 * q_dev
    total = got_ref[:step, :].astype(jnp.float32)
    for i in range(1, got_ref.shape[0] // step):
        total = total + got_ref[i * step:(i + 1) * step, :].astype(jnp.float32)
    total = total[:q_dev] + total[q_dev:]
    grad_ref[...] = total[:, :width].astype(jnp.bfloat16)
    tail_ref[...] = total[:, width:]


def close_call(got, q_dev, width):
    return pl.pallas_call(
        close_kernel,
        out_shape=(jax.ShapeDtypeStruct((q_dev, width), jnp.bfloat16), jax.ShapeDtypeStruct((q_dev, EXTRA), jnp.float32)),
        in_specs=[VMEM],
        out_specs=(VMEM, VMEM),
        name="close",
    )(got)


def lse_of(parts, axis=None):
    if axis is None:
        top = functools.reduce(jnp.maximum, parts)
        return top + jnp.log(functools.reduce(jnp.add, [jnp.exp(p - top) for p in parts]))
    top = jnp.max(parts, axis)
    return top + jnp.log(jnp.sum(jnp.exp(parts - jnp.expand_dims(top, axis)), axis))


def body(embeddings, classifier, positives, counts):
    q_dev, width = embeddings.shape
    labels = classifier.shape[0] // 2
    xh, core, xl, z, y = (lax.axis_index(a) for a in AXES)
    rank = (xl * 8 + z) * 4 + y
    base = (rank * 2 + core) * labels

    spread = lambda x, n: jnp.broadcast_to(x[None], (n,) + x.shape).reshape((n * x.shape[0],) + x.shape[1:])
    column = lax.all_to_all(pack_call(embeddings, positives, counts), "z", 0, 0, tiled=True)
    mine = lax.all_to_all(spread(column, 4), ("xh", "xl"), 0, 0, tiled=True)
    own = [mine, shift(mine, "y", -1), None, shift(mine, "y", 1)]
    relay = [(c * 4 + i, c * 4 + (i + 2 * c - 1) % 4) for c in range(2) for i in range(4)]
    own[2] = lax.ppermute(jnp.where(core == 0, own[1], own[3]), ("core", "y"), relay)
    w = lax.dynamic_slice_in_dim(classifier, core * labels, labels)
    rows = mine.shape[0]

    oth, parts = [None] * 4, [None] * 4
    for d in (0, 1, 3, 2):
        if d:
            done = (parts[1][1], parts[3][1]) if d == 2 else (hits[0][0],)
            own[d] = lax.optimization_barrier((own[d],) + done)[0]
        oth[d] = shift(own[d], "core", 1)
        parts[d] = scores_call(own[d], oth[d], w)
        if d == 0:
            first = lax.optimization_barrier((own[0], parts[0][1]))[0]
            hits = [hits_call(base[None], (first, oth[0]), w)]
    es, ms, ls = zip(*parts)
    blocks = [b for pair in zip(own, oth) for b in pair]
    hits.append(hits_call(base[None], blocks[EARLY:], w))
    m = jnp.concatenate(ms, 0)
    stat = jnp.concatenate(ls, 0)
    stat = lse_of([stat, jnp.roll(shift(stat, "core", 1), rows, 1)])
    stat = lse_of([stat] + [jnp.roll(shift(stat, "y", -d), d, 0) for d in range(1, 4)])
    stat = stat.reshape(8, rows)
    lse = lse_of(lax.all_to_all(jnp.broadcast_to(stat[None], (16, 8, rows)), ("xl", "z"), 0, 0, tiled=True), 0)

    ps, u_own, u_oth = query_call(jnp.stack([xh, y]), hits, lse.reshape(4, 2 * rows), m, es, w)
    f32 = lambda a: a.astype(jnp.float32)
    u = (f32(u_own) + f32(shift(u_oth, "core", 1))).astype(jnp.bfloat16)
    first, u = lax.optimization_barrier((ps[0], u))
    by_y = lax.all_to_all(u, "y", 0, 0, tiled=True)
    v = jnp.sum(f32(by_y).reshape((4, -1) + by_y.shape[1:]), 0).astype(jnp.bfloat16)
    class_grad, one = class_call(core[None], (first,) + tuple(ps[1:]), blocks, width, 0, None)
    second, v, one = lax.optimization_barrier((ps[0], v, one))
    got = lax.all_to_all(v, ("xl", "z"), 0, 0, tiled=True)
    class_grad, two = class_call(core[None], (second,) + tuple(ps[1:]), blocks, width, 1, class_grad)
    two, got = lax.optimization_barrier((two, got))
    sent_parts = [shift(one, "core", 1), shift(two, "core", 1)]
    class_grad = place_call(core[None], sent_parts, class_grad)

    query_grad, tail = close_call(got, q_dev, width)
    pos_mean = jnp.sum(tail, 1)
    at = ((xh * 2 + xl) * 8 + z) * q_dev
    loss = lax.dynamic_slice(lse, (0, at), (1, q_dev))[0] - pos_mean
    return loss, query_grad, class_grad


def solution(mesh):
    fine = Mesh(mesh.devices.reshape(tuple(SIZES[a] for a in AXES)), AXES)
    split = P(AXES, None)
    lab = P(("xl", "z", "y"), None)
    return jax.shard_map(
        body,
        mesh=fine,
        in_specs=(split, lab, split, P(AXES)),
        out_specs=(P(AXES), split, lab),
        check_vma=False,
    )
```

```python
import functools

import jax
import jax.numpy as jnp
from jax import lax
from jax.experimental import pallas as pl
from jax.experimental.pallas import tpu as pltpu
from jax.sharding import Mesh, PartitionSpec as P

AXES = ("xh", "core", "xl", "z", "y")
SIZES = {"xh": 2, "core": 2, "xl": 2, "z": 8, "y": 4}
EXTRA = 128
POS = 5
LO, MID, HI, CNT = 0, 8, 16, 24
VMEM = pl.BlockSpec(memory_space=pltpu.VMEM)
SMEM = pl.BlockSpec(memory_space=pltpu.SMEM)
ANY = pl.BlockSpec(memory_space=pl.ANY)
HBM = pl.BlockSpec(memory_space=pltpu.HBM)
NT = (((1,), (1,)), ((), ()))
TN = (((0,), (0,)), ((), ()))
LCH = 256
PROD = 1024
EXPO = 128
SPLIT = (2, 2)
PARTS = len(SPLIT)
EARLY = 2
CLASS = 512


def shift(x, axis, step):
    n = SIZES[axis]
    return lax.ppermute(x, axis, [(i, (i + step) % n) for i in range(n)])


def in_hbm(arrays):
    return [pltpu.with_memory_space_constraint(a, pltpu.HBM) for a in arrays]


def scores_kernel(xh_ref, own_ref, oth_ref, w_ref, e_ref, m_ref, l_ref, kept_ref, q_ref, s_ref, qt_ref, held_ref, sem, keep_sem):
    labels, width = w_ref.shape
    rows = own_ref.shape[0]
    both = 2 * rows
    copies = [pltpu.make_async_copy(a, q_ref.at[k], sem.at[k]) for k, a in enumerate((own_ref, oth_ref))]
    for copy in copies:
        copy.start()
    half = rows // 2
    keep = []
    for k, copy in enumerate(copies):
        copy.wait()
        for x in range(2):
            rowsx = pl.ds(pl.multiple_of((xh_ref[0] ^ x) * half, half), half)
            at = x * rows + k * half
            keep.append(pltpu.make_async_copy(q_ref.at[k, rowsx, pl.ds(0, width)], kept_ref.at[pl.ds(at, half), :], keep_sem.at[2 * k + x]))
            keep[-1].start()
            qt_ref[:, at:at + half] = q_ref[k, rowsx, :width].T

    def product(i, top):
        at = pl.multiple_of(i * PROD, PROD)
        s = jnp.dot(w_ref[pl.ds(at, PROD), :], qt_ref[...], preferred_element_type=jnp.float32)
        s_ref[pl.ds(at, PROD), :] = s
        return jnp.maximum(top, jnp.max(s.reshape(PROD // 16, 16, both), 0))

    top = lax.fori_loop(0, labels // PROD, product, jnp.full((16, both), -1e30, jnp.float32))
    top = jnp.max(top, 0, keepdims=True)

    def leave(i):
        part = pl.ds(pl.multiple_of(i * EXPO, EXPO), EXPO)
        return pltpu.make_async_copy(held_ref.at[part, :], e_ref.at[part, :], sem.at[i])

    def expo(i, total):
        at = pl.multiple_of(i * EXPO, EXPO)
        e = jnp.exp(s_ref[pl.ds(at, EXPO), :] - top)
        held_ref[pl.ds(at, EXPO), :] = e.astype(jnp.bfloat16)
        leave(i).start()
        return total + jnp.sum(e.reshape(EXPO // 16, 16, both), 0)

    total = lax.fori_loop(0, labels // EXPO, expo, jnp.zeros((16, both), jnp.float32))
    m_ref[...] = top
    l_ref[...] = top + jnp.log(jnp.sum(total, 0, keepdims=True))

    def gone(i, carry):
        leave(i).wait()
        return carry

    lax.fori_loop(0, labels // EXPO, gone, 0)
    for copy in keep:
        copy.wait()


def scores_call(xh, own, oth, w):
    rows = own.shape[0]
    labels, width = w.shape
    line = jax.ShapeDtypeStruct((1, 2 * rows), jnp.float32)
    return pl.pallas_call(
        scores_kernel,
        out_shape=(pltpu.HBM((labels, 2 * rows), jnp.bfloat16), line, line, pltpu.HBM((2 * rows, width), jnp.bfloat16)),
        in_specs=[SMEM, ANY, ANY, VMEM],
        out_specs=(HBM, VMEM, VMEM, HBM),
        scratch_shapes=[
            pltpu.VMEM((2,) + own.shape, jnp.bfloat16),
            pltpu.VMEM((labels, 2 * rows), jnp.float32),
            pltpu.VMEM((width, 2 * rows), jnp.bfloat16),
            pltpu.VMEM((labels, 2 * rows), jnp.bfloat16),
            pltpu.SemaphoreType.DMA((labels // EXPO,)),
            pltpu.SemaphoreType.DMA((4,)),
        ],
        compiler_params=pltpu.CompilerParams(vmem_limit_bytes=18 * 2**20),
        cost_estimate=pl.CostEstimate(flops=1000, bytes_accessed=1000, transcendentals=0),
        name="scores",
    )(xh, own, oth, w)


def hits_kernel(base_ref, *refs):
    count = len(refs) - 7
    sources = refs[:count]
    w_ref, n_ref, key_ref, s_ref, t_ref, blocks, sem = refs[count:]
    copies = [pltpu.make_async_copy(q, blocks.at[b], sem.at[b]) for b, q in enumerate(sources)]
    for copy in copies:
        copy.start()
    labels, width = w_ref.shape
    base = base_ref[0].astype(jnp.float32)
    half = sources[0].shape[0] // 2
    starts = [pl.multiple_of((base_ref[1] ^ x) * half, half) for x in range(2)]
    row = lax.broadcasted_iota(jnp.int32, (8, EXTRA), 0)
    col = lax.broadcasted_iota(jnp.int32, (8, EXTRA), 1)
    digits = jnp.where(col == row + LO, 1.0, jnp.where(col == row + MID, 128.0, jnp.where(col == row + HI, 16384.0, 0.0)))
    digits = jnp.where(row < POS, digits, 0.0).astype(jnp.bfloat16)
    counting = jnp.where(col == CNT, 1.0, 0.0).astype(jnp.bfloat16)
    big = 1e9
    rows = half
    slot = lax.broadcasted_iota(jnp.int32, (8, rows), 0)
    lane = lax.broadcasted_iota(jnp.int32, (8, rows), 1)
    keys, weights, most = [], [], jnp.int32(0)
    for part in range(2 * count):
        b = part // 2
        if part % 2 == 0:
            copies[b].wait()
        extra = blocks[b, pl.ds(starts[part % 2], half), width:]
        ids = lax.dot_general(digits, extra, NT, preferred_element_type=jnp.float32)
        cnt = lax.dot_general(counting, extra, NT, preferred_element_type=jnp.float32)
        valid = (slot.astype(jnp.float32) < cnt) & (slot < POS)
        ids = jnp.where(valid, ids, -1.0)
        same = jnp.zeros((8, rows), jnp.float32)
        again = jnp.zeros((8, rows), jnp.float32)
        for j in range(POS):
            eq = jnp.where(ids == ids[j:j + 1, :], 1.0, 0.0)
            same = same + eq
            again = again + jnp.where(slot > j, eq, 0.0)
        local = ids - base
        hit = valid & (local >= 0.0) & (local < float(labels)) & (again == 0.0)
        weights.append(same / cnt)
        keys.append(jnp.where(hit, (lane * 8 + slot).astype(jnp.float32) * float(labels) + local, big))
        n = jnp.sum(jnp.where(hit, 1.0, 0.0)).astype(jnp.int32)
        n_ref[part] = n
        most = jnp.maximum(most, n)
    r16 = lax.broadcasted_iota(jnp.int32, (16, width), 0)

    def step(i, keys):
        least = [jnp.min(k) for k in keys]
        found = [jnp.where(k < big, k, 0.0).astype(jnp.int32) for k in least]
        same = [k == kf for k, kf in zip(keys, least)]
        score, weight = [], []
        for part, k in enumerate(found):
            b = part // 2
            label = k & (labels - 1)
            query = lax.div(k, 8 * labels)
            qat = pl.multiple_of((query >> 4) << 4, 16)
            brow = pl.multiple_of(starts[part % 2] + qat, 16)
            lat = pl.multiple_of((label >> 4) << 4, 16)
            row_q = jnp.where(r16 == query - qat, blocks[b, pl.ds(brow, 16), :width].astype(jnp.float32), 0.0)
            row_w = jnp.where(r16 == label - lat, w_ref[pl.ds(lat, 16), :].astype(jnp.float32), 0.0)
            score.append(jnp.sum(row_w * jnp.sum(row_q, 0, keepdims=True)))
            weight.append(jnp.sum(jnp.where(same[part], weights[part], 0.0)))
        for part in range(2 * count):
            at = part * rows * POS + i
            key_ref[at] = found[part]
            s_ref[at] = score[part]
            t_ref[at] = weight[part]
        return tuple(jnp.where(t, big, k) for t, k in zip(same, keys))

    lax.fori_loop(0, most, step, tuple(keys))


def hits_call(base, blocks, w):
    count = len(blocks)
    total = count * blocks[0].shape[0] * POS
    return pl.pallas_call(
        hits_kernel,
        out_shape=(
            jax.ShapeDtypeStruct((2 * count,), jnp.int32),
            jax.ShapeDtypeStruct((total,), jnp.int32),
            jax.ShapeDtypeStruct((total,), jnp.float32),
            jax.ShapeDtypeStruct((total,), jnp.float32),
        ),
        in_specs=[SMEM] + [HBM] * count + [VMEM],
        out_specs=(SMEM,) * 4,
        scratch_shapes=[pltpu.VMEM((count,) + blocks[0].shape, jnp.bfloat16), pltpu.SemaphoreType.DMA((count,))],
        compiler_params=pltpu.CompilerParams(vmem_limit_bytes=16 * 2**20),
        cost_estimate=pl.CostEstimate(flops=1000, bytes_accessed=1000, transcendentals=0),
        name="hits",
    )(base, *in_hbm(blocks), w)


def grad_kernel(x, at_ref, na, ka, sa, ta, nb, kb, sb, tb, lse_ref, m_ref, e0, e1, e2, e3, *refs):
    labels, rows = e0.shape[0], e0.shape[1] // 2
    half = rows // 2
    if x == 0:
        w_ref, outs = refs[0], refs[1:5]
        own_ref, oth_ref, pos_ref = refs[5:8]
        width = w_ref.shape[1]
        pos_ref[...] = jnp.zeros_like(pos_ref)
    else:
        outs = refs[:4]
    held, sem = refs[-2:]
    lanes = slice(x * rows, (x + 1) * rows)
    ps = [held.at[d] for d in range(4)]
    copies = [pltpu.make_async_copy(e.at[:, lanes], p, sem.at[d]) for d, (e, p) in enumerate(zip((e0, e1, e2, e3), ps))]
    for copy in copies:
        copy.start()
    for d, p_ref in enumerate(ps):
        copies[d].wait()
        scale = jnp.exp(m_ref[d:d + 1, lanes] - lse_ref[d:d + 1, lanes])

        def scaled(i, carry):
            at = pl.multiple_of(i * 128, 128)
            p_ref[pl.ds(at, 128), :] = (p_ref[pl.ds(at, 128), :].astype(jnp.float32) * scale).astype(jnp.bfloat16)
            return carry

        lax.fori_loop(0, labels // 128, scaled, 0)

    r = lax.broadcasted_iota(jnp.int32, (16, half), 0)
    c = lax.broadcasted_iota(jnp.int32, (16, half), 1)
    c1 = lax.broadcasted_iota(jnp.int32, (1, EXTRA), 1)
    lists = []
    for b in range(8):
        group, spot = ((na, ka, sa, ta), b) if b < EARLY else ((nb, kb, sb, tb), b - EARLY)
        lists.append(group + (2 * spot + x,))
    most = jnp.int32(0)
    for n_ref, _, _, _, part in lists:
        most = jnp.maximum(most, n_ref[part])

    def patch(i, carry):
        todo = []
        for b, (n_ref, key_ref, s_ref, t_ref, part) in enumerate(lists):
            d, k = b // 2, b % 2
            at = part * half * POS + i
            live = i < n_ref[part]
            key, s, weight = jnp.where(live, key_ref[at], 0), s_ref[at], t_ref[at]
            label = key & (labels - 1)
            rest = lax.div(key, labels)
            slot = rest & 7
            query = rest >> 3
            lat = pl.multiple_of((label >> 4) << 4, 16)
            spot = (pl.ds(lat, 16), slice(k * half, (k + 1) * half))
            first = x * rows + k * half
            value = jnp.exp(s - lse_ref[d:d + 1, first:first + half]) - weight
            row = jnp.where(live, label - lat, -1)
            old = ps[d][spot].astype(jnp.float32)
            new = jnp.where((r == row) & (c == query), value, old).astype(jnp.bfloat16)
            into = pos = None
            if x == 0:
                full = jnp.full((1, EXTRA), s * weight, jnp.float32)
                high = full.astype(jnp.bfloat16).astype(jnp.float32)
                mid = (full - high).astype(jnp.bfloat16).astype(jnp.float32)
                low = full - high - mid
                put = jnp.where(c1 == slot, high, jnp.where(c1 == slot + 8, mid, jnp.where(c1 == slot + 16, low, 0.0)))
                into = (k, pl.ds(d * half + query, 1), slice(None))
                pos = pos_ref[into] + jnp.where(live, put, 0.0)
            todo.append((d, spot, new, into, pos))
        for d, spot, new, into, pos in todo:
            ps[d][spot] = new
            if x == 0:
                pos_ref[into] = pos
        return carry

    lax.fori_loop(0, most, patch, 0)
    copies = [pltpu.make_async_copy(p, out, sem.at[d]) for d, (p, out) in enumerate(zip(ps, outs))]
    for copy in copies:
        copy.start()
    if x == 0:
        for d, p_ref in enumerate(ps):
            u = lax.dot_general(p_ref[...], w_ref[...], TN, preferred_element_type=jnp.float32)
            to = pl.ds(pl.multiple_of(((at_ref[0] + d) & 3) * half, half), half)
            for k, out in enumerate((own_ref, oth_ref)):
                out[to, :width] = u[k * half:(k + 1) * half].astype(jnp.bfloat16)
                out[to, width:] = pos_ref[k, d * half:(d + 1) * half, :].astype(jnp.bfloat16)
    for copy in copies:
        copy.wait()


def grad_call(x, at, hits, lse, m, es, w=None):
    labels, rows = es[0].shape[0], es[0].shape[1] // 2
    p = (pltpu.HBM((labels, rows), jnp.bfloat16),) * 4
    held = [pltpu.VMEM((4, labels, rows), jnp.bfloat16), pltpu.SemaphoreType.DMA((4,))]
    more, specs, u, pos = (), [], (), []
    if x == 0:
        more, specs = (w,), [VMEM]
        u = (jax.ShapeDtypeStruct((2 * rows, w.shape[1] + EXTRA), jnp.bfloat16),) * 2
        pos = [pltpu.VMEM((2, 2 * rows, EXTRA), jnp.float32)]
    res = pl.pallas_call(
        functools.partial(grad_kernel, x),
        out_shape=p + u,
        in_specs=[SMEM] * 9 + [VMEM] * 2 + [HBM] * 4 + specs,
        out_specs=(HBM,) * 4 + (VMEM,) * len(u),
        scratch_shapes=pos + held,
        compiler_params=pltpu.CompilerParams(vmem_limit_bytes=20 * 2**20),
        cost_estimate=pl.CostEstimate(flops=4 * labels * rows * 4096 if x == 0 else 1000, bytes_accessed=2**23, transcendentals=0),
        name="rest_part" if x else "query_part",
    )(at, *hits[0], *hits[1], lse, m, *in_hbm(es), *more)
    return res[:4], res[4:]


def class_kernel(core_ref, *refs):
    ps, blocks = refs[:8], refs[8:12]
    out_ref, mine_ref = refs[-2:]
    rows = ps[0].shape[1]
    width = out_ref.shape[1]
    acc = None
    for d in range(4):
        for x in range(2):
            term = jnp.dot(ps[4 * x + d][...], blocks[d][x * rows:(x + 1) * rows, :], preferred_element_type=jnp.float32)
            acc = term if acc is None else acc + term
    done = acc.astype(jnp.bfloat16)
    out_ref[...] = done
    mine_ref[...] = done


def class_call(core, ps, blocks, width, part, before):
    labels = ps[0].shape[0]
    steps = labels // CLASS
    start, each = sum(SPLIT[:part]), SPLIT[part]
    rows = ps[0].shape[1]
    whole = lambda i, c: (0, 0)
    kept = () if before is None else (before,)
    return pl.pallas_call(
        class_kernel,
        out_shape=tuple(jax.ShapeDtypeStruct((n, width), jnp.bfloat16) for n in (2 * labels, each * CLASS)),
        grid_spec=pltpu.PrefetchScalarGridSpec(
            num_scalar_prefetch=1,
            grid=(each,),
            in_specs=[pl.BlockSpec((CLASS, rows), lambda i, c: (start + i, 0))] * 8
            + [pl.BlockSpec(blocks[0].shape, whole)] * 4
            + [HBM] * len(kept),
            out_specs=(
                pl.BlockSpec((CLASS, width), lambda i, c: (c[0] * steps + start + i, 0)),
                pl.BlockSpec((CLASS, width), lambda i, c: (i, 0)),
            ),
        ),
        input_output_aliases={13: 0} if kept else {},
        compiler_params=pltpu.CompilerParams(vmem_limit_bytes=24 * 2**20),
        cost_estimate=pl.CostEstimate(flops=16 * rows * each * CLASS * width, bytes_accessed=2**23, transcendentals=0),
        name="class_part",
    )(core, *in_hbm(ps), *blocks, *kept)


def place_kernel(core_ref, *refs):
    parts, out_ref, sem = refs[:PARTS], refs[-2], refs[-1]
    first = (1 - core_ref[0]) * (out_ref.shape[0] // 2)
    copies = [
        pltpu.make_async_copy(p, out_ref.at[pl.ds(pl.multiple_of(first + sum(SPLIT[:j]) * CLASS, CLASS), p.shape[0]), :], sem.at[j])
        for j, p in enumerate(parts)
    ]
    for copy in copies:
        copy.start()
    for copy in copies:
        copy.wait()


def place_call(core, parts, into):
    return pl.pallas_call(
        place_kernel,
        out_shape=jax.ShapeDtypeStruct(into.shape, into.dtype),
        in_specs=[SMEM] + [VMEM] * PARTS + [HBM],
        out_specs=HBM,
        scratch_shapes=[pltpu.SemaphoreType.DMA((PARTS,))],
        input_output_aliases={1 + PARTS: 0},
        compiler_params=pltpu.CompilerParams(vmem_limit_bytes=8 * 2**20),
        cost_estimate=pl.CostEstimate(flops=1000, bytes_accessed=1000, transcendentals=0),
        name="place",
    )(core, *parts, into)


def pack_kernel(counts_ref, emb_ref, pos_ref, out_ref):
    q_dev = emb_ref.shape[0]
    row = lax.broadcasted_iota(jnp.int32, (q_dev, EXTRA), 0)
    lane = lax.broadcasted_iota(jnp.int32, (q_dev, EXTRA), 1)
    extra = jnp.zeros((q_dev, EXTRA), jnp.int32)
    for j in range(POS):
        ids = pos_ref[:, j:j + 1]
        for first, digit in ((LO, ids & 127), (MID, (ids >> 7) & 127), (HI, ids >> 14)):
            extra = jnp.where(lane == first + j, digit, extra)
    for i in range(q_dev):
        extra = jnp.where((row == i) & (lane == CNT), counts_ref[i], extra)
    one = jnp.concatenate([emb_ref[...].astype(jnp.float32), extra.astype(jnp.float32)], 1)
    two = jnp.concatenate([one, one], 0).astype(jnp.bfloat16)
    for i in range(out_ref.shape[0] // two.shape[0]):
        out_ref[i * two.shape[0]:(i + 1) * two.shape[0], :] = two


def pack_call(embeddings, positives, counts):
    q_dev, width = embeddings.shape
    return pl.pallas_call(
        pack_kernel,
        out_shape=jax.ShapeDtypeStruct((SIZES["z"] * q_dev, width + EXTRA), jnp.bfloat16),
        in_specs=[SMEM, VMEM, VMEM],
        out_specs=VMEM,
        name="pack",
    )(counts, embeddings, positives)


def take_kernel(core_ref, all_ref, out_ref, sem):
    rows = out_ref.shape[0]
    part = rows // 4
    first = core_ref[0] * rows
    copies = [
        pltpu.make_async_copy(all_ref.at[pl.ds(pl.multiple_of(first + i * part, part), part), :], out_ref.at[pl.ds(i * part, part), :], sem.at[i])
        for i in range(4)
    ]
    for copy in copies:
        copy.start()
    for copy in copies:
        copy.wait()


def take_call(core, everything):
    rows, width = everything.shape
    return pl.pallas_call(
        take_kernel,
        out_shape=jax.ShapeDtypeStruct((rows // 2, width), everything.dtype),
        in_specs=[SMEM, HBM],
        out_specs=VMEM,
        scratch_shapes=[pltpu.SemaphoreType.DMA((4,))],
        compiler_params=pltpu.CompilerParams(vmem_limit_bytes=8 * 2**20),
        cost_estimate=pl.CostEstimate(flops=1000, bytes_accessed=1000, transcendentals=0),
        name="take",
    )(core, *in_hbm([everything]))


def close_kernel(got_ref, grad_ref, tail_ref):
    q_dev, width = grad_ref.shape
    step = 2 * q_dev
    total = got_ref[:step, :].astype(jnp.float32)
    for i in range(1, got_ref.shape[0] // step):
        total = total + got_ref[i * step:(i + 1) * step, :].astype(jnp.float32)
    total = total[:q_dev] + total[q_dev:]
    grad_ref[...] = total[:, :width].astype(jnp.bfloat16)
    tail_ref[...] = total[:, width:]


def close_call(got, q_dev, width):
    return pl.pallas_call(
        close_kernel,
        out_shape=(jax.ShapeDtypeStruct((q_dev, width), jnp.bfloat16), jax.ShapeDtypeStruct((q_dev, EXTRA), jnp.float32)),
        in_specs=[VMEM],
        out_specs=(VMEM, VMEM),
        name="close",
    )(got)


def lse_of(parts, axis=None):
    if axis is None:
        top = functools.reduce(jnp.maximum, parts)
        return top + jnp.log(functools.reduce(jnp.add, [jnp.exp(p - top) for p in parts]))
    top = jnp.max(parts, axis)
    return top + jnp.log(jnp.sum(jnp.exp(parts - jnp.expand_dims(top, axis)), axis))


def body(embeddings, classifier, positives, counts):
    q_dev, width = embeddings.shape
    labels = classifier.shape[0] // 2
    xh, core, xl, z, y = (lax.axis_index(a) for a in AXES)
    rank = (xl * 8 + z) * 4 + y
    base = (rank * 2 + core) * labels

    spread = lambda x, n: jnp.broadcast_to(x[None], (n,) + x.shape).reshape((n * x.shape[0],) + x.shape[1:])
    column = lax.all_to_all(pack_call(embeddings, positives, counts), "z", 0, 0, tiled=True)
    mine = lax.all_to_all(spread(column, 4), ("xh", "xl"), 0, 0, tiled=True)
    own = [mine, shift(mine, "y", -1), None, shift(mine, "y", 1)]
    relay = [(c * 4 + i, c * 4 + (i + 2 * c - 1) % 4) for c in range(2) for i in range(4)]
    own[2] = lax.ppermute(jnp.where(core == 0, own[1], own[3]), ("core", "y"), relay)
    w = take_call(core[None], classifier)
    rows = mine.shape[0]

    oth, parts = [None] * 4, [None] * 4
    for d in (0, 1, 3, 2):
        if d:
            done = (parts[1][1], parts[3][1]) if d == 2 else (hits[0][0],)
            own[d] = lax.optimization_barrier((own[d],) + done)[0]
        oth[d] = shift(own[d], "core", 1)
        parts[d] = scores_call(xh[None], own[d], oth[d], w)
        if d == 0:
            first = lax.optimization_barrier((own[0], parts[0][1]))[0]
            hits = [hits_call(jnp.stack([base, xh]), (first, oth[0]), w)]
    es, ms, ls, kept = zip(*parts)
    blocks = [b for pair in zip(own, oth) for b in pair]
    hits.append(hits_call(jnp.stack([base, xh]), blocks[EARLY:], w))
    m = jnp.concatenate(ms, 0)
    stat = jnp.concatenate(ls, 0)
    their, n = shift(stat, "core", 1), rows // 2
    their = jnp.concatenate([their[:, n:2 * n], their[:, :n], their[:, 3 * n:], their[:, 2 * n:3 * n]], 1)
    stat = lse_of([stat, their])
    stat = lse_of([stat] + [jnp.roll(shift(stat, "y", -d), d, 0) for d in range(1, 4)])
    stat = stat.reshape(8, rows)
    lse = lse_of(lax.all_to_all(jnp.broadcast_to(stat[None], (16, 8, rows)), ("xl", "z"), 0, 0, tiled=True), 0)

    lines = lse.reshape(4, 2 * rows)
    ps, (u_own, u_oth) = grad_call(0, y[None], hits, lines, m, es, w)
    f32 = lambda a: a.astype(jnp.float32)
    u = (f32(u_own) + f32(shift(u_oth, "core", 1))).astype(jnp.bfloat16)
    lines, u = lax.optimization_barrier((lines, u))
    ps += grad_call(1, y[None], hits, lines, m, es)[0]
    by_y = lax.all_to_all(u, "y", 0, 0, tiled=True)
    v = jnp.sum(f32(by_y).reshape((4, -1) + by_y.shape[1:]), 0).astype(jnp.bfloat16)
    class_grad, one = class_call(core[None], ps, kept, width, 0, None)
    second, v, one = lax.optimization_barrier((ps[0], v, one))
    got = lax.all_to_all(v, ("xl", "z"), 0, 0, tiled=True)
    class_grad, two = class_call(core[None], (second,) + tuple(ps[1:]), kept, width, 1, class_grad)
    two, got = lax.optimization_barrier((two, got))
    sent_parts = [shift(one, "core", 1), shift(two, "core", 1)]
    class_grad = place_call(core[None], sent_parts, class_grad)

    query_grad, tail = close_call(got, q_dev, width)
    pos_mean = jnp.sum(tail, 1)
    at = (xl * 8 + z) * q_dev
    loss = lax.dynamic_slice(lse, (0, at), (1, q_dev))[0] - pos_mean
    return loss, query_grad, class_grad


def solution(mesh):
    fine = Mesh(mesh.devices.reshape(tuple(SIZES[a] for a in AXES)), AXES)
    split = P(AXES, None)
    lab = P(("xl", "z", "y"), None)
    return jax.shard_map(
        body,
        mesh=fine,
        in_specs=(split, lab, split, P(AXES)),
        out_specs=(P(AXES), split, lab),
        check_vma=False,
    )
```

```python
import functools

import jax
import jax.numpy as jnp
from jax import lax
from jax.experimental import pallas as pl
from jax.experimental.pallas import tpu as pltpu
from jax.sharding import Mesh, PartitionSpec as P

AXES = ("xh", "core", "xl", "z", "y")
SIZES = {"xh": 2, "core": 2, "xl": 2, "z": 8, "y": 4}
EXTRA = 128
POS = 5
LO, MID, HI, CNT = 0, 8, 16, 24
VMEM = pl.BlockSpec(memory_space=pltpu.VMEM)
SMEM = pl.BlockSpec(memory_space=pltpu.SMEM)
ANY = pl.BlockSpec(memory_space=pl.ANY)
HBM = pl.BlockSpec(memory_space=pltpu.HBM)
NT = (((1,), (1,)), ((), ()))
TN = (((0,), (0,)), ((), ()))
LCH = 256
PROD = 1024
EXPO = 128
SPLIT = (2, 2)
PARTS = len(SPLIT)
EARLY = 2
CLASS = 512


def shift(x, axis, step):
    n = SIZES[axis]
    return lax.ppermute(x, axis, [(i, (i + step) % n) for i in range(n)])


def in_hbm(arrays):
    return [pltpu.with_memory_space_constraint(a, pltpu.HBM) for a in arrays]


def scores_kernel(xh_ref, own_ref, oth_ref, w_ref, e_ref, m_ref, l_ref, kept_ref, q_ref, s_ref, qt_ref, held_ref, sem, keep_sem):
    labels, width = w_ref.shape
    rows = own_ref.shape[0]
    both = 2 * rows
    copies = [pltpu.make_async_copy(a, q_ref.at[k], sem.at[k]) for k, a in enumerate((own_ref, oth_ref))]
    for copy in copies:
        copy.start()
    half = rows // 2
    keep = []
    for k, copy in enumerate(copies):
        copy.wait()
        for x in range(2):
            rowsx = pl.ds(pl.multiple_of((xh_ref[0] ^ x) * half, half), half)
            at = x * rows + k * half
            keep.append(pltpu.make_async_copy(q_ref.at[k, rowsx, pl.ds(0, width)], kept_ref.at[pl.ds(at, half), :], keep_sem.at[2 * k + x]))
            keep[-1].start()
            qt_ref[:, at:at + half] = q_ref[k, rowsx, :width].T

    def product(i, top):
        at = pl.multiple_of(i * PROD, PROD)
        s = jnp.dot(w_ref[pl.ds(at, PROD), :], qt_ref[...], preferred_element_type=jnp.float32)
        s_ref[pl.ds(at, PROD), :] = s
        return jnp.maximum(top, jnp.max(s.reshape(PROD // 16, 16, both), 0))

    top = lax.fori_loop(0, labels // PROD, product, jnp.full((16, both), -1e30, jnp.float32))
    top = jnp.max(top, 0, keepdims=True)

    def leave(i):
        part = pl.ds(pl.multiple_of(i * EXPO, EXPO), EXPO)
        return pltpu.make_async_copy(held_ref.at[part, :], e_ref.at[part, :], sem.at[i])

    def expo(i, total):
        at = pl.multiple_of(i * EXPO, EXPO)
        e = jnp.exp(s_ref[pl.ds(at, EXPO), :] - top)
        held_ref[pl.ds(at, EXPO), :] = e.astype(jnp.bfloat16)
        leave(i).start()
        return total + jnp.sum(e.reshape(EXPO // 16, 16, both), 0)

    total = lax.fori_loop(0, labels // EXPO, expo, jnp.zeros((16, both), jnp.float32))
    m_ref[...] = top
    l_ref[...] = top + jnp.log(jnp.sum(total, 0, keepdims=True))

    def gone(i, carry):
        leave(i).wait()
        return carry

    lax.fori_loop(0, labels // EXPO, gone, 0)
    for copy in keep:
        copy.wait()


def scores_call(xh, own, oth, w):
    rows = own.shape[0]
    labels, width = w.shape
    line = jax.ShapeDtypeStruct((1, 2 * rows), jnp.float32)
    return pl.pallas_call(
        scores_kernel,
        out_shape=(pltpu.HBM((labels, 2 * rows), jnp.bfloat16), line, line, pltpu.HBM((2 * rows, width), jnp.bfloat16)),
        in_specs=[SMEM, ANY, ANY, VMEM],
        out_specs=(HBM, VMEM, VMEM, HBM),
        scratch_shapes=[
            pltpu.VMEM((2,) + own.shape, jnp.bfloat16),
            pltpu.VMEM((labels, 2 * rows), jnp.float32),
            pltpu.VMEM((width, 2 * rows), jnp.bfloat16),
            pltpu.VMEM((labels, 2 * rows), jnp.bfloat16),
            pltpu.SemaphoreType.DMA((labels // EXPO,)),
            pltpu.SemaphoreType.DMA((4,)),
        ],
        compiler_params=pltpu.CompilerParams(vmem_limit_bytes=18 * 2**20),
        cost_estimate=pl.CostEstimate(flops=1000, bytes_accessed=1000, transcendentals=0),
        name="scores",
    )(xh, own, oth, w)


def hits_kernel(base_ref, *refs):
    count = len(refs) - 7
    sources = refs[:count]
    w_ref, n_ref, key_ref, s_ref, t_ref, blocks, sem = refs[count:]
    copies = [pltpu.make_async_copy(q, blocks.at[b], sem.at[b]) for b, q in enumerate(sources)]
    for copy in copies:
        copy.start()
    labels, width = w_ref.shape
    base = base_ref[0].astype(jnp.float32)
    half = sources[0].shape[0] // 2
    starts = [pl.multiple_of((base_ref[1] ^ x) * half, half) for x in range(2)]
    row = lax.broadcasted_iota(jnp.int32, (8, EXTRA), 0)
    col = lax.broadcasted_iota(jnp.int32, (8, EXTRA), 1)
    digits = jnp.where(col == row + LO, 1.0, jnp.where(col == row + MID, 128.0, jnp.where(col == row + HI, 16384.0, 0.0)))
    digits = jnp.where(row < POS, digits, 0.0).astype(jnp.bfloat16)
    counting = jnp.where(col == CNT, 1.0, 0.0).astype(jnp.bfloat16)
    big = 1e9
    rows = half
    slot = lax.broadcasted_iota(jnp.int32, (8, rows), 0)
    lane = lax.broadcasted_iota(jnp.int32, (8, rows), 1)
    keys, weights, most = [], [], jnp.int32(0)
    for part in range(2 * count):
        b = part // 2
        if part % 2 == 0:
            copies[b].wait()
        extra = blocks[b, pl.ds(starts[part % 2], half), width:]
        ids = lax.dot_general(digits, extra, NT, preferred_element_type=jnp.float32)
        cnt = lax.dot_general(counting, extra, NT, preferred_element_type=jnp.float32)
        valid = (slot.astype(jnp.float32) < cnt) & (slot < POS)
        ids = jnp.where(valid, ids, -1.0)
        same = jnp.zeros((8, rows), jnp.float32)
        again = jnp.zeros((8, rows), jnp.float32)
        for j in range(POS):
            eq = jnp.where(ids == ids[j:j + 1, :], 1.0, 0.0)
            same = same + eq
            again = again + jnp.where(slot > j, eq, 0.0)
        local = ids - base
        hit = valid & (local >= 0.0) & (local < float(labels)) & (again == 0.0)
        weights.append(same / cnt)
        keys.append(jnp.where(hit, (lane * 8 + slot).astype(jnp.float32) * float(labels) + local, big))
        n = jnp.sum(jnp.where(hit, 1.0, 0.0)).astype(jnp.int32)
        n_ref[part] = n
        most = jnp.maximum(most, n)
    r16 = lax.broadcasted_iota(jnp.int32, (16, width), 0)

    def step(i, keys):
        least = [jnp.min(k) for k in keys]
        found = [jnp.where(k < big, k, 0.0).astype(jnp.int32) for k in least]
        same = [k == kf for k, kf in zip(keys, least)]
        score, weight = [], []
        for part, k in enumerate(found):
            b = part // 2
            label = k & (labels - 1)
            query = lax.div(k, 8 * labels)
            qat = pl.multiple_of((query >> 4) << 4, 16)
            brow = pl.multiple_of(starts[part % 2] + qat, 16)
            lat = pl.multiple_of((label >> 4) << 4, 16)
            row_q = jnp.where(r16 == query - qat, blocks[b, pl.ds(brow, 16), :width].astype(jnp.float32), 0.0)
            row_w = jnp.where(r16 == label - lat, w_ref[pl.ds(lat, 16), :].astype(jnp.float32), 0.0)
            score.append(jnp.sum(row_w * jnp.sum(row_q, 0, keepdims=True)))
            weight.append(jnp.sum(jnp.where(same[part], weights[part], 0.0)))
        for part in range(2 * count):
            at = part * rows * POS + i
            key_ref[at] = found[part]
            s_ref[at] = score[part]
            t_ref[at] = weight[part]
        return tuple(jnp.where(t, big, k) for t, k in zip(same, keys))

    lax.fori_loop(0, most, step, tuple(keys))


def hits_call(base, blocks, w):
    count = len(blocks)
    total = count * blocks[0].shape[0] * POS
    return pl.pallas_call(
        hits_kernel,
        out_shape=(
            jax.ShapeDtypeStruct((2 * count,), jnp.int32),
            jax.ShapeDtypeStruct((total,), jnp.int32),
            jax.ShapeDtypeStruct((total,), jnp.float32),
            jax.ShapeDtypeStruct((total,), jnp.float32),
        ),
        in_specs=[SMEM] + [HBM] * count + [VMEM],
        out_specs=(SMEM,) * 4,
        scratch_shapes=[pltpu.VMEM((count,) + blocks[0].shape, jnp.bfloat16), pltpu.SemaphoreType.DMA((count,))],
        compiler_params=pltpu.CompilerParams(vmem_limit_bytes=16 * 2**20),
        cost_estimate=pl.CostEstimate(flops=1000, bytes_accessed=1000, transcendentals=0),
        name="hits",
    )(base, *in_hbm(blocks), w)


def grad_kernel(x, at_ref, na, ka, sa, ta, nb, kb, sb, tb, lse_ref, m_ref, e0, e1, e2, e3, *refs):
    labels, rows = e0.shape[0], e0.shape[1] // 2
    half = rows // 2
    if x == 0:
        w_ref, outs = refs[0], refs[1:5]
        own_ref, oth_ref, pos_ref = refs[5:8]
        width = w_ref.shape[1]
        pos_ref[...] = jnp.zeros_like(pos_ref)
    else:
        outs = refs[:4]
    held, sem = refs[-2:]
    lanes = slice(x * rows, (x + 1) * rows)
    ps = [held.at[d] for d in range(4)]
    copies = [pltpu.make_async_copy(e.at[:, lanes], p, sem.at[d]) for d, (e, p) in enumerate(zip((e0, e1, e2, e3), ps))]
    for copy in copies:
        copy.start()
    for d, p_ref in enumerate(ps):
        copies[d].wait()
        scale = jnp.exp(m_ref[d:d + 1, lanes] - lse_ref[d:d + 1, lanes])

        def scaled(i, carry):
            at = pl.multiple_of(i * 128, 128)
            p_ref[pl.ds(at, 128), :] = (p_ref[pl.ds(at, 128), :].astype(jnp.float32) * scale).astype(jnp.bfloat16)
            return carry

        lax.fori_loop(0, labels // 128, scaled, 0)

    r = lax.broadcasted_iota(jnp.int32, (16, half), 0)
    c = lax.broadcasted_iota(jnp.int32, (16, half), 1)
    c1 = lax.broadcasted_iota(jnp.int32, (1, EXTRA), 1)
    lists = []
    for b in range(8):
        group, spot = ((na, ka, sa, ta), b) if b < EARLY else ((nb, kb, sb, tb), b - EARLY)
        lists.append(group + (2 * spot + x,))
    most = jnp.int32(0)
    for n_ref, _, _, _, part in lists:
        most = jnp.maximum(most, n_ref[part])

    def patch(i, carry):
        todo = []
        for b, (n_ref, key_ref, s_ref, t_ref, part) in enumerate(lists):
            d, k = b // 2, b % 2
            at = part * half * POS + i
            live = i < n_ref[part]
            key, s, weight = jnp.where(live, key_ref[at], 0), s_ref[at], t_ref[at]
            label = key & (labels - 1)
            rest = lax.div(key, labels)
            slot = rest & 7
            query = rest >> 3
            lat = pl.multiple_of((label >> 4) << 4, 16)
            spot = (pl.ds(lat, 16), slice(k * half, (k + 1) * half))
            first = x * rows + k * half
            value = jnp.exp(s - lse_ref[d:d + 1, first:first + half]) - weight
            row = jnp.where(live, label - lat, -1)
            old = ps[d][spot].astype(jnp.float32)
            new = jnp.where((r == row) & (c == query), value, old).astype(jnp.bfloat16)
            into = pos = None
            if x == 0:
                full = jnp.full((1, EXTRA), s * weight, jnp.float32)
                high = full.astype(jnp.bfloat16).astype(jnp.float32)
                mid = (full - high).astype(jnp.bfloat16).astype(jnp.float32)
                low = full - high - mid
                put = jnp.where(c1 == slot, high, jnp.where(c1 == slot + 8, mid, jnp.where(c1 == slot + 16, low, 0.0)))
                into = (k, pl.ds(d * half + query, 1), slice(None))
                pos = pos_ref[into] + jnp.where(live, put, 0.0)
            todo.append((d, spot, new, into, pos))
        for d, spot, new, into, pos in todo:
            ps[d][spot] = new
            if x == 0:
                pos_ref[into] = pos
        return carry

    lax.fori_loop(0, most, patch, 0)
    copies = [pltpu.make_async_copy(p, out, sem.at[d]) for d, (p, out) in enumerate(zip(ps, outs))]
    for copy in copies:
        copy.start()
    if x == 0:
        for d, p_ref in enumerate(ps):
            u = lax.dot_general(p_ref[...], w_ref[...], TN, preferred_element_type=jnp.float32)
            to = pl.ds(pl.multiple_of(((at_ref[0] + d) & 3) * half, half), half)
            for k, out in enumerate((own_ref, oth_ref)):
                out[to, :width] = u[k * half:(k + 1) * half].astype(jnp.bfloat16)
                out[to, width:] = pos_ref[k, d * half:(d + 1) * half, :].astype(jnp.bfloat16)
    for copy in copies:
        copy.wait()


def grad_call(x, at, hits, lse, m, es, w=None):
    labels, rows = es[0].shape[0], es[0].shape[1] // 2
    p = (pltpu.HBM((labels, rows), jnp.bfloat16),) * 4
    held = [pltpu.VMEM((4, labels, rows), jnp.bfloat16), pltpu.SemaphoreType.DMA((4,))]
    more, specs, u, pos = (), [], (), []
    if x == 0:
        more, specs = (w,), [VMEM]
        u = (jax.ShapeDtypeStruct((2 * rows, w.shape[1] + EXTRA), jnp.bfloat16),) * 2
        pos = [pltpu.VMEM((2, 2 * rows, EXTRA), jnp.float32)]
    res = pl.pallas_call(
        functools.partial(grad_kernel, x),
        out_shape=p + u,
        in_specs=[SMEM] * 9 + [VMEM] * 2 + [HBM] * 4 + specs,
        out_specs=(HBM,) * 4 + (VMEM,) * len(u),
        scratch_shapes=pos + held,
        compiler_params=pltpu.CompilerParams(vmem_limit_bytes=20 * 2**20),
        cost_estimate=pl.CostEstimate(flops=4 * labels * rows * 4096 if x == 0 else 1000, bytes_accessed=2**23, transcendentals=0),
        name="rest_part" if x else "query_part",
    )(at, *hits[0], *hits[1], lse, m, *in_hbm(es), *more)
    return res[:4], res[4:]


def class_kernel(core_ref, *refs):
    ps, blocks = refs[:8], refs[8:12]
    out_ref, mine_ref = refs[-2:]
    rows = ps[0].shape[1]
    width = out_ref.shape[1]
    acc = None
    for d in range(4):
        for x in range(2):
            term = jnp.dot(ps[4 * x + d][...], blocks[d][x * rows:(x + 1) * rows, :], preferred_element_type=jnp.float32)
            acc = term if acc is None else acc + term
    done = acc.astype(jnp.bfloat16)
    out_ref[...] = done
    mine_ref[...] = done


def class_call(core, ps, blocks, width, part, before):
    labels = ps[0].shape[0]
    steps = labels // CLASS
    start, each = sum(SPLIT[:part]), SPLIT[part]
    rows = ps[0].shape[1]
    whole = lambda i, c: (0, 0)
    kept = () if before is None else (before,)
    return pl.pallas_call(
        class_kernel,
        out_shape=(jax.ShapeDtypeStruct((2 * labels, width), jnp.bfloat16), pltpu.HBM((each * CLASS, width), jnp.bfloat16)),
        grid_spec=pltpu.PrefetchScalarGridSpec(
            num_scalar_prefetch=1,
            grid=(each,),
            in_specs=[pl.BlockSpec((CLASS, rows), lambda i, c: (start + i, 0))] * 8
            + [pl.BlockSpec(blocks[0].shape, whole)] * 4
            + [HBM] * len(kept),
            out_specs=(
                pl.BlockSpec((CLASS, width), lambda i, c: (c[0] * steps + start + i, 0)),
                pl.BlockSpec((CLASS, width), lambda i, c: (i, 0)),
            ),
        ),
        input_output_aliases={13: 0} if kept else {},
        compiler_params=pltpu.CompilerParams(vmem_limit_bytes=24 * 2**20),
        cost_estimate=pl.CostEstimate(flops=16 * rows * each * CLASS * width, bytes_accessed=2**23, transcendentals=0),
        name="class_part",
    )(core, *in_hbm(ps), *blocks, *kept)


def place_kernel(core_ref, *refs):
    parts, out_ref, sem = refs[:PARTS], refs[-2], refs[-1]
    first = (1 - core_ref[0]) * (out_ref.shape[0] // 2)
    copies = [
        pltpu.make_async_copy(p, out_ref.at[pl.ds(pl.multiple_of(first + sum(SPLIT[:j]) * CLASS, CLASS), p.shape[0]), :], sem.at[j])
        for j, p in enumerate(parts)
    ]
    for copy in copies:
        copy.start()
    for copy in copies:
        copy.wait()


def place_call(core, parts, into):
    return pl.pallas_call(
        place_kernel,
        out_shape=jax.ShapeDtypeStruct(into.shape, into.dtype),
        in_specs=[SMEM] + [VMEM] * PARTS + [HBM],
        out_specs=HBM,
        scratch_shapes=[pltpu.SemaphoreType.DMA((PARTS,))],
        input_output_aliases={1 + PARTS: 0},
        compiler_params=pltpu.CompilerParams(vmem_limit_bytes=8 * 2**20),
        cost_estimate=pl.CostEstimate(flops=1000, bytes_accessed=1000, transcendentals=0),
        name="place",
    )(core, *parts, into)


def pack_kernel(counts_ref, emb_ref, pos_ref, out_ref):
    q_dev = emb_ref.shape[0]
    row = lax.broadcasted_iota(jnp.int32, (q_dev, EXTRA), 0)
    lane = lax.broadcasted_iota(jnp.int32, (q_dev, EXTRA), 1)
    extra = jnp.zeros((q_dev, EXTRA), jnp.int32)
    for j in range(POS):
        ids = pos_ref[:, j:j + 1]
        for first, digit in ((LO, ids & 127), (MID, (ids >> 7) & 127), (HI, ids >> 14)):
            extra = jnp.where(lane == first + j, digit, extra)
    for i in range(q_dev):
        extra = jnp.where((row == i) & (lane == CNT), counts_ref[i], extra)
    one = jnp.concatenate([emb_ref[...].astype(jnp.float32), extra.astype(jnp.float32)], 1)
    two = jnp.concatenate([one, one], 0).astype(jnp.bfloat16)
    for i in range(out_ref.shape[0] // two.shape[0]):
        out_ref[i * two.shape[0]:(i + 1) * two.shape[0], :] = two


def pack_call(embeddings, positives, counts):
    q_dev, width = embeddings.shape
    return pl.pallas_call(
        pack_kernel,
        out_shape=jax.ShapeDtypeStruct((SIZES["z"] * q_dev, width + EXTRA), jnp.bfloat16),
        in_specs=[SMEM, VMEM, VMEM],
        out_specs=VMEM,
        name="pack",
    )(counts, embeddings, positives)


def take_kernel(core_ref, all_ref, out_ref, sem):
    rows = out_ref.shape[0]
    part = rows // 4
    first = core_ref[0] * rows
    copies = [
        pltpu.make_async_copy(all_ref.at[pl.ds(pl.multiple_of(first + i * part, part), part), :], out_ref.at[pl.ds(i * part, part), :], sem.at[i])
        for i in range(4)
    ]
    for copy in copies:
        copy.start()
    for copy in copies:
        copy.wait()


def take_call(core, everything):
    rows, width = everything.shape
    return pl.pallas_call(
        take_kernel,
        out_shape=jax.ShapeDtypeStruct((rows // 2, width), everything.dtype),
        in_specs=[SMEM, HBM],
        out_specs=VMEM,
        scratch_shapes=[pltpu.SemaphoreType.DMA((4,))],
        compiler_params=pltpu.CompilerParams(vmem_limit_bytes=8 * 2**20),
        cost_estimate=pl.CostEstimate(flops=1000, bytes_accessed=1000, transcendentals=0),
        name="take",
    )(core, *in_hbm([everything]))


def close_kernel(got_ref, grad_ref, tail_ref):
    q_dev, width = grad_ref.shape
    step = 2 * q_dev
    total = got_ref[:step, :].astype(jnp.float32)
    for i in range(1, got_ref.shape[0] // step):
        total = total + got_ref[i * step:(i + 1) * step, :].astype(jnp.float32)
    total = total[:q_dev] + total[q_dev:]
    grad_ref[...] = total[:, :width].astype(jnp.bfloat16)
    tail_ref[...] = total[:, width:]


def close_call(got, q_dev, width):
    return pl.pallas_call(
        close_kernel,
        out_shape=(jax.ShapeDtypeStruct((q_dev, width), jnp.bfloat16), jax.ShapeDtypeStruct((q_dev, EXTRA), jnp.float32)),
        in_specs=[VMEM],
        out_specs=(VMEM, VMEM),
        name="close",
    )(got)


def lse_of(parts, axis=None):
    if axis is None:
        top = functools.reduce(jnp.maximum, parts)
        return top + jnp.log(functools.reduce(jnp.add, [jnp.exp(p - top) for p in parts]))
    top = jnp.max(parts, axis)
    return top + jnp.log(jnp.sum(jnp.exp(parts - jnp.expand_dims(top, axis)), axis))


def body(embeddings, classifier, positives, counts):
    q_dev, width = embeddings.shape
    labels = classifier.shape[0] // 2
    xh, core, xl, z, y = (lax.axis_index(a) for a in AXES)
    rank = (xl * 8 + z) * 4 + y
    base = (rank * 2 + core) * labels

    spread = lambda x, n: jnp.broadcast_to(x[None], (n,) + x.shape).reshape((n * x.shape[0],) + x.shape[1:])
    column = lax.all_to_all(pack_call(embeddings, positives, counts), "z", 0, 0, tiled=True)
    mine = lax.all_to_all(spread(column, 4), ("xh", "xl"), 0, 0, tiled=True)
    own = [mine, shift(mine, "y", -1), None, shift(mine, "y", 1)]
    relay = [(c * 4 + i, c * 4 + (i + 2 * c - 1) % 4) for c in range(2) for i in range(4)]
    own[2] = lax.ppermute(jnp.where(core == 0, own[1], own[3]), ("core", "y"), relay)
    w = take_call(core[None], classifier)
    rows = mine.shape[0]

    oth, parts = [None] * 4, [None] * 4
    for d in (0, 1, 3, 2):
        if d:
            done = (parts[1][1], parts[3][1]) if d == 2 else (hits[0][0],)
            own[d] = lax.optimization_barrier((own[d],) + done)[0]
        oth[d] = shift(own[d], "core", 1)
        parts[d] = scores_call(xh[None], own[d], oth[d], w)
        if d == 0:
            first = lax.optimization_barrier((own[0], parts[0][1]))[0]
            hits = [hits_call(jnp.stack([base, xh]), (first, oth[0]), w)]
    es, ms, ls, kept = zip(*parts)
    blocks = [b for pair in zip(own, oth) for b in pair]
    hits.append(hits_call(jnp.stack([base, xh]), blocks[EARLY:], w))
    m = jnp.concatenate(ms, 0)
    stat = jnp.concatenate(ls, 0)
    their, n = shift(stat, "core", 1), rows // 2
    their = jnp.concatenate([their[:, n:2 * n], their[:, :n], their[:, 3 * n:], their[:, 2 * n:3 * n]], 1)
    stat = lse_of([stat, their])
    stat = lse_of([stat] + [jnp.roll(shift(stat, "y", -d), d, 0) for d in range(1, 4)])
    stat = stat.reshape(8, rows)
    lse = lse_of(lax.all_to_all(jnp.broadcast_to(stat[None], (16, 8, rows)), ("xl", "z"), 0, 0, tiled=True), 0)

    lines = lse.reshape(4, 2 * rows)
    ps, (u_own, u_oth) = grad_call(0, y[None], hits, lines, m, es, w)
    f32 = lambda a: a.astype(jnp.float32)
    u = (f32(u_own) + f32(shift(u_oth, "core", 1))).astype(jnp.bfloat16)
    lines, u = lax.optimization_barrier((lines, u))
    ps += grad_call(1, y[None], hits, lines, m, es)[0]
    by_y = lax.all_to_all(u, "y", 0, 0, tiled=True)
    v = jnp.sum(f32(by_y).reshape((4, -1) + by_y.shape[1:]), 0).astype(jnp.bfloat16)
    class_grad, one = class_call(core[None], ps, kept, width, 0, None)
    second, v, one = lax.optimization_barrier((ps[0], v, one))
    got = lax.all_to_all(v, ("xl", "z"), 0, 0, tiled=True)
    class_grad, two = class_call(core[None], (second,) + tuple(ps[1:]), in_hbm(kept), width, 1, class_grad)
    two, got = lax.optimization_barrier((two, got))
    sent_parts = [shift(one, "core", 1), shift(two, "core", 1)]
    class_grad = place_call(core[None], sent_parts, class_grad)

    query_grad, tail = close_call(got, q_dev, width)
    pos_mean = jnp.sum(tail, 1)
    at = (xl * 8 + z) * q_dev
    loss = lax.dynamic_slice(lse, (0, at), (1, q_dev))[0] - pos_mean
    return loss, query_grad, class_grad


def solution(mesh):
    fine = Mesh(mesh.devices.reshape(tuple(SIZES[a] for a in AXES)), AXES)
    split = P(AXES, None)
    lab = P(("xl", "z", "y"), None)
    return jax.shard_map(
        body,
        mesh=fine,
        in_specs=(split, lab, split, P(AXES)),
        out_specs=(P(AXES), split, lab),
        check_vma=False,
    )
```

```python
import functools

import jax
import jax.numpy as jnp
from jax import lax
from jax.experimental import pallas as pl
from jax.experimental.pallas import tpu as pltpu
from jax.sharding import Mesh, PartitionSpec as P

AXES = ("xh", "core", "xl", "z", "y")
SIZES = {"xh": 2, "core": 2, "xl": 2, "z": 8, "y": 4}
EXTRA = 128
POS = 5
LO, MID, HI, CNT = 0, 8, 16, 24
VMEM = pl.BlockSpec(memory_space=pltpu.VMEM)
SMEM = pl.BlockSpec(memory_space=pltpu.SMEM)
ANY = pl.BlockSpec(memory_space=pl.ANY)
HBM = pl.BlockSpec(memory_space=pltpu.HBM)
NT = (((1,), (1,)), ((), ()))
TN = (((0,), (0,)), ((), ()))
LCH = 256
PROD = 1024
EXPO = 128
SPLIT = (2, 2)
PARTS = len(SPLIT)
CLASS = 512


def shift(x, axis, step):
    n = SIZES[axis]
    return lax.ppermute(x, axis, [(i, (i + step) % n) for i in range(n)])


def in_hbm(arrays):
    return [pltpu.with_memory_space_constraint(a, pltpu.HBM) for a in arrays]


def scores_kernel(xh_ref, own_ref, oth_ref, w_ref, e_ref, m_ref, l_ref, kept_ref, q_ref, s_ref, qt_ref, held_ref, sem, keep_sem):
    labels, width = w_ref.shape
    rows = own_ref.shape[0]
    both = 2 * rows
    copies = [pltpu.make_async_copy(a, q_ref.at[k], sem.at[k]) for k, a in enumerate((own_ref, oth_ref))]
    for copy in copies:
        copy.start()
    half = rows // 2
    keep = []
    for k, copy in enumerate(copies):
        copy.wait()
        for x in range(2):
            rowsx = pl.ds(pl.multiple_of((xh_ref[0] ^ x) * half, half), half)
            at = x * rows + k * half
            keep.append(pltpu.make_async_copy(q_ref.at[k, rowsx, pl.ds(0, width)], kept_ref.at[pl.ds(at, half), :], keep_sem.at[2 * k + x]))
            keep[-1].start()
            qt_ref[:, at:at + half] = q_ref[k, rowsx, :width].T

    def product(i, top):
        at = pl.multiple_of(i * PROD, PROD)
        s = jnp.dot(w_ref[pl.ds(at, PROD), :], qt_ref[...], preferred_element_type=jnp.float32)
        s_ref[pl.ds(at, PROD), :] = s
        return jnp.maximum(top, jnp.max(s.reshape(PROD // 16, 16, both), 0))

    top = lax.fori_loop(0, labels // PROD, product, jnp.full((16, both), -1e30, jnp.float32))
    top = jnp.max(top, 0, keepdims=True)

    def leave(i):
        part = pl.ds(pl.multiple_of(i * EXPO, EXPO), EXPO)
        return pltpu.make_async_copy(held_ref.at[part, :], e_ref.at[part, :], sem.at[i])

    def expo(i, total):
        at = pl.multiple_of(i * EXPO, EXPO)
        e = jnp.exp(s_ref[pl.ds(at, EXPO), :] - top)
        held_ref[pl.ds(at, EXPO), :] = e.astype(jnp.bfloat16)
        leave(i).start()
        return total + jnp.sum(e.reshape(EXPO // 16, 16, both), 0)

    total = lax.fori_loop(0, labels // EXPO, expo, jnp.zeros((16, both), jnp.float32))
    m_ref[...] = top
    l_ref[...] = top + jnp.log(jnp.sum(total, 0, keepdims=True))

    def gone(i, carry):
        leave(i).wait()
        return carry

    lax.fori_loop(0, labels // EXPO, gone, 0)
    for copy in keep:
        copy.wait()


def scores_call(xh, own, oth, w):
    rows = own.shape[0]
    labels, width = w.shape
    line = jax.ShapeDtypeStruct((1, 2 * rows), jnp.float32)
    return pl.pallas_call(
        scores_kernel,
        out_shape=(pltpu.HBM((labels, 2 * rows), jnp.bfloat16), line, line, pltpu.HBM((2 * rows, width), jnp.bfloat16)),
        in_specs=[SMEM, ANY, ANY, VMEM],
        out_specs=(HBM, VMEM, VMEM, HBM),
        scratch_shapes=[
            pltpu.VMEM((2,) + own.shape, jnp.bfloat16),
            pltpu.VMEM((labels, 2 * rows), jnp.float32),
            pltpu.VMEM((width, 2 * rows), jnp.bfloat16),
            pltpu.VMEM((labels, 2 * rows), jnp.bfloat16),
            pltpu.SemaphoreType.DMA((labels // EXPO,)),
            pltpu.SemaphoreType.DMA((4,)),
        ],
        compiler_params=pltpu.CompilerParams(vmem_limit_bytes=18 * 2**20),
        cost_estimate=pl.CostEstimate(flops=1000, bytes_accessed=1000, transcendentals=0),
        name="scores",
    )(xh, own, oth, w)


def hits_kernel(base_ref, *refs):
    count = len(refs) - 7
    sources = refs[:count]
    w_ref, n_ref, key_ref, s_ref, t_ref, blocks, sem = refs[count:]
    copies = [pltpu.make_async_copy(q, blocks.at[b], sem.at[b]) for b, q in enumerate(sources)]
    for copy in copies:
        copy.start()
    labels, width = w_ref.shape
    base = base_ref[0].astype(jnp.float32)
    half = sources[0].shape[0] // 2
    starts = [pl.multiple_of((base_ref[1] ^ x) * half, half) for x in range(2)]
    row = lax.broadcasted_iota(jnp.int32, (8, EXTRA), 0)
    col = lax.broadcasted_iota(jnp.int32, (8, EXTRA), 1)
    digits = jnp.where(col == row + LO, 1.0, jnp.where(col == row + MID, 128.0, jnp.where(col == row + HI, 16384.0, 0.0)))
    digits = jnp.where(row < POS, digits, 0.0).astype(jnp.bfloat16)
    counting = jnp.where(col == CNT, 1.0, 0.0).astype(jnp.bfloat16)
    big = 1e9
    rows = half
    slot = lax.broadcasted_iota(jnp.int32, (8, rows), 0)
    lane = lax.broadcasted_iota(jnp.int32, (8, rows), 1)
    keys, weights, most = [], [], jnp.int32(0)
    for part in range(2 * count):
        b = part // 2
        if part % 2 == 0:
            copies[b].wait()
        extra = blocks[b, pl.ds(starts[part % 2], half), width:]
        ids = lax.dot_general(digits, extra, NT, preferred_element_type=jnp.float32)
        cnt = lax.dot_general(counting, extra, NT, preferred_element_type=jnp.float32)
        valid = (slot.astype(jnp.float32) < cnt) & (slot < POS)
        ids = jnp.where(valid, ids, -1.0)
        same = jnp.zeros((8, rows), jnp.float32)
        again = jnp.zeros((8, rows), jnp.float32)
        for j in range(POS):
            eq = jnp.where(ids == ids[j:j + 1, :], 1.0, 0.0)
            same = same + eq
            again = again + jnp.where(slot > j, eq, 0.0)
        local = ids - base
        hit = valid & (local >= 0.0) & (local < float(labels)) & (again == 0.0)
        weights.append(same / cnt)
        keys.append(jnp.where(hit, (lane * 8 + slot).astype(jnp.float32) * float(labels) + local, big))
        n = jnp.sum(jnp.where(hit, 1.0, 0.0)).astype(jnp.int32)
        n_ref[part] = n
        most = jnp.maximum(most, n)
    r16 = lax.broadcasted_iota(jnp.int32, (16, width), 0)

    def step(i, keys):
        least = [jnp.min(k) for k in keys]
        found = [jnp.where(k < big, k, 0.0).astype(jnp.int32) for k in least]
        same = [k == kf for k, kf in zip(keys, least)]
        score, weight = [], []
        for part, k in enumerate(found):
            b = part // 2
            label = k & (labels - 1)
            query = lax.div(k, 8 * labels)
            qat = pl.multiple_of((query >> 4) << 4, 16)
            brow = pl.multiple_of(starts[part % 2] + qat, 16)
            lat = pl.multiple_of((label >> 4) << 4, 16)
            row_q = jnp.where(r16 == query - qat, blocks[b, pl.ds(brow, 16), :width].astype(jnp.float32), 0.0)
            row_w = jnp.where(r16 == label - lat, w_ref[pl.ds(lat, 16), :].astype(jnp.float32), 0.0)
            score.append(jnp.sum(row_w * jnp.sum(row_q, 0, keepdims=True)))
            weight.append(jnp.sum(jnp.where(same[part], weights[part], 0.0)))
        for part in range(2 * count):
            at = part * rows * POS + i
            key_ref[at] = found[part]
            s_ref[at] = score[part]
            t_ref[at] = weight[part]
        return tuple(jnp.where(t, big, k) for t, k in zip(same, keys))

    lax.fori_loop(0, most, step, tuple(keys))


def hits_call(base, blocks, w):
    count = len(blocks)
    total = count * blocks[0].shape[0] * POS
    return pl.pallas_call(
        hits_kernel,
        out_shape=(
            jax.ShapeDtypeStruct((2 * count,), jnp.int32),
            jax.ShapeDtypeStruct((total,), jnp.int32),
            jax.ShapeDtypeStruct((total,), jnp.float32),
            jax.ShapeDtypeStruct((total,), jnp.float32),
        ),
        in_specs=[SMEM] + [HBM] * count + [VMEM],
        out_specs=(SMEM,) * 4,
        scratch_shapes=[pltpu.VMEM((count,) + blocks[0].shape, jnp.bfloat16), pltpu.SemaphoreType.DMA((count,))],
        compiler_params=pltpu.CompilerParams(vmem_limit_bytes=16 * 2**20),
        cost_estimate=pl.CostEstimate(flops=1000, bytes_accessed=1000, transcendentals=0),
        name="hits",
    )(base, *in_hbm(blocks), w)


def grad_kernel(x, at_ref, na, ka, sa, ta, nb, kb, sb, tb, nc, kc, sc, tc, lse_ref, m_ref, e0, e1, e2, e3, *refs):
    labels, rows = e0.shape[0], e0.shape[1] // 2
    half = rows // 2
    if x == 0:
        w_ref, outs = refs[0], refs[1:5]
        own_ref, oth_ref, pos_ref = refs[5:8]
        width = w_ref.shape[1]
        pos_ref[...] = jnp.zeros_like(pos_ref)
    else:
        outs = refs[:4]
    held, sem = refs[-2:]
    lanes = slice(x * rows, (x + 1) * rows)
    ps = [held.at[d] for d in range(4)]
    copies = [pltpu.make_async_copy(e.at[:, lanes], p, sem.at[d]) for d, (e, p) in enumerate(zip((e0, e1, e2, e3), ps))]
    for copy in copies:
        copy.start()
    for d, p_ref in enumerate(ps):
        copies[d].wait()
        scale = jnp.exp(m_ref[d:d + 1, lanes] - lse_ref[d:d + 1, lanes])

        def scaled(i, carry):
            at = pl.multiple_of(i * 128, 128)
            p_ref[pl.ds(at, 128), :] = (p_ref[pl.ds(at, 128), :].astype(jnp.float32) * scale).astype(jnp.bfloat16)
            return carry

        lax.fori_loop(0, labels // 128, scaled, 0)

    r = lax.broadcasted_iota(jnp.int32, (16, half), 0)
    c = lax.broadcasted_iota(jnp.int32, (16, half), 1)
    c1 = lax.broadcasted_iota(jnp.int32, (1, EXTRA), 1)
    lists = []
    for b in range(8):
        group = ((na, ka, sa, ta), (nb, kb, sb, tb), (nc, kc, sc, tc), (nb, kb, sb, tb))[b // 2]
        spot = b if b < 2 else b % 2 + (2 if b >= 6 else 0)
        lists.append(group + (2 * spot + x,))
    most = jnp.int32(0)
    for n_ref, _, _, _, part in lists:
        most = jnp.maximum(most, n_ref[part])

    def patch(i, carry):
        todo = []
        for b, (n_ref, key_ref, s_ref, t_ref, part) in enumerate(lists):
            d, k = b // 2, b % 2
            at = part * half * POS + i
            live = i < n_ref[part]
            key, s, weight = jnp.where(live, key_ref[at], 0), s_ref[at], t_ref[at]
            label = key & (labels - 1)
            rest = lax.div(key, labels)
            slot = rest & 7
            query = rest >> 3
            lat = pl.multiple_of((label >> 4) << 4, 16)
            spot = (pl.ds(lat, 16), slice(k * half, (k + 1) * half))
            first = x * rows + k * half
            value = jnp.exp(s - lse_ref[d:d + 1, first:first + half]) - weight
            row = jnp.where(live, label - lat, -1)
            old = ps[d][spot].astype(jnp.float32)
            new = jnp.where((r == row) & (c == query), value, old).astype(jnp.bfloat16)
            into = pos = None
            if x == 0:
                full = jnp.full((1, EXTRA), s * weight, jnp.float32)
                high = full.astype(jnp.bfloat16).astype(jnp.float32)
                mid = (full - high).astype(jnp.bfloat16).astype(jnp.float32)
                low = full - high - mid
                put = jnp.where(c1 == slot, high, jnp.where(c1 == slot + 8, mid, jnp.where(c1 == slot + 16, low, 0.0)))
                into = (k, pl.ds(d * half + query, 1), slice(None))
                pos = pos_ref[into] + jnp.where(live, put, 0.0)
            todo.append((d, spot, new, into, pos))
        for d, spot, new, into, pos in todo:
            ps[d][spot] = new
            if x == 0:
                pos_ref[into] = pos
        return carry

    lax.fori_loop(0, most, patch, 0)
    copies = [pltpu.make_async_copy(p, out, sem.at[d]) for d, (p, out) in enumerate(zip(ps, outs))]
    for copy in copies:
        copy.start()
    if x == 0:
        for d, p_ref in enumerate(ps):
            u = lax.dot_general(p_ref[...], w_ref[...], TN, preferred_element_type=jnp.float32)
            to = pl.ds(pl.multiple_of(((at_ref[0] + d) & 3) * half, half), half)
            for k, out in enumerate((own_ref, oth_ref)):
                out[to, :width] = u[k * half:(k + 1) * half].astype(jnp.bfloat16)
                out[to, width:] = pos_ref[k, d * half:(d + 1) * half, :].astype(jnp.bfloat16)
    for copy in copies:
        copy.wait()


def grad_call(x, at, hits, lse, m, es, w=None):
    labels, rows = es[0].shape[0], es[0].shape[1] // 2
    p = (pltpu.HBM((labels, rows), jnp.bfloat16),) * 4
    held = [pltpu.VMEM((4, labels, rows), jnp.bfloat16), pltpu.SemaphoreType.DMA((4,))]
    more, specs, u, pos = (), [], (), []
    if x == 0:
        more, specs = (w,), [VMEM]
        u = (jax.ShapeDtypeStruct((2 * rows, w.shape[1] + EXTRA), jnp.bfloat16),) * 2
        pos = [pltpu.VMEM((2, 2 * rows, EXTRA), jnp.float32)]
    res = pl.pallas_call(
        functools.partial(grad_kernel, x),
        out_shape=p + u,
        in_specs=[SMEM] * 13 + [VMEM] * 2 + [HBM] * 4 + specs,
        out_specs=(HBM,) * 4 + (VMEM,) * len(u),
        scratch_shapes=pos + held,
        compiler_params=pltpu.CompilerParams(vmem_limit_bytes=20 * 2**20),
        cost_estimate=pl.CostEstimate(flops=4 * labels * rows * 4096 if x == 0 else 1000, bytes_accessed=2**23, transcendentals=0),
        name="rest_part" if x else "query_part",
    )(at, *hits[0], *hits[1], *hits[2], lse, m, *in_hbm(es), *more)
    return res[:4], res[4:]


def class_kernel(core_ref, *refs):
    ps, blocks = refs[:8], refs[8:12]
    out_ref, mine_ref = refs[-2:]
    rows = ps[0].shape[1]
    width = out_ref.shape[1]
    acc = None
    for d in range(4):
        for x in range(2):
            term = jnp.dot(ps[4 * x + d][...], blocks[d][x * rows:(x + 1) * rows, :], preferred_element_type=jnp.float32)
            acc = term if acc is None else acc + term
    done = acc.astype(jnp.bfloat16)
    out_ref[...] = done
    mine_ref[...] = done


def class_call(core, ps, blocks, width, part, before):
    labels = ps[0].shape[0]
    steps = labels // CLASS
    start, each = sum(SPLIT[:part]), SPLIT[part]
    rows = ps[0].shape[1]
    whole = lambda i, c: (0, 0)
    kept = () if before is None else (before,)
    return pl.pallas_call(
        class_kernel,
        out_shape=(jax.ShapeDtypeStruct((2 * labels, width), jnp.bfloat16), pltpu.HBM((each * CLASS, width), jnp.bfloat16)),
        grid_spec=pltpu.PrefetchScalarGridSpec(
            num_scalar_prefetch=1,
            grid=(each,),
            in_specs=[pl.BlockSpec((CLASS, rows), lambda i, c: (start + i, 0))] * 8
            + [pl.BlockSpec(blocks[0].shape, whole)] * 4
            + [HBM] * len(kept),
            out_specs=(
                pl.BlockSpec((CLASS, width), lambda i, c: (c[0] * steps + start + i, 0)),
                pl.BlockSpec((CLASS, width), lambda i, c: (i, 0)),
            ),
        ),
        input_output_aliases={13: 0} if kept else {},
        compiler_params=pltpu.CompilerParams(vmem_limit_bytes=24 * 2**20),
        cost_estimate=pl.CostEstimate(flops=16 * rows * each * CLASS * width, bytes_accessed=2**23, transcendentals=0),
        name="class_part",
    )(core, *in_hbm(ps), *blocks, *kept)


def place_kernel(core_ref, *refs):
    parts, out_ref, sem = refs[:PARTS], refs[-2], refs[-1]
    first = (1 - core_ref[0]) * (out_ref.shape[0] // 2)
    copies = [
        pltpu.make_async_copy(p, out_ref.at[pl.ds(pl.multiple_of(first + sum(SPLIT[:j]) * CLASS, CLASS), p.shape[0]), :], sem.at[j])
        for j, p in enumerate(parts)
    ]
    for copy in copies:
        copy.start()
    for copy in copies:
        copy.wait()


def place_call(core, parts, into):
    return pl.pallas_call(
        place_kernel,
        out_shape=jax.ShapeDtypeStruct(into.shape, into.dtype),
        in_specs=[SMEM] + [VMEM] * PARTS + [HBM],
        out_specs=HBM,
        scratch_shapes=[pltpu.SemaphoreType.DMA((PARTS,))],
        input_output_aliases={1 + PARTS: 0},
        compiler_params=pltpu.CompilerParams(vmem_limit_bytes=8 * 2**20),
        cost_estimate=pl.CostEstimate(flops=1000, bytes_accessed=1000, transcendentals=0),
        name="place",
    )(core, *parts, into)


def pack_kernel(counts_ref, emb_ref, pos_ref, out_ref):
    q_dev = emb_ref.shape[0]
    row = lax.broadcasted_iota(jnp.int32, (q_dev, EXTRA), 0)
    lane = lax.broadcasted_iota(jnp.int32, (q_dev, EXTRA), 1)
    extra = jnp.zeros((q_dev, EXTRA), jnp.int32)
    for j in range(POS):
        ids = pos_ref[:, j:j + 1]
        for first, digit in ((LO, ids & 127), (MID, (ids >> 7) & 127), (HI, ids >> 14)):
            extra = jnp.where(lane == first + j, digit, extra)
    for i in range(q_dev):
        extra = jnp.where((row == i) & (lane == CNT), counts_ref[i], extra)
    one = jnp.concatenate([emb_ref[...].astype(jnp.float32), extra.astype(jnp.float32)], 1)
    two = jnp.concatenate([one, one], 0).astype(jnp.bfloat16)
    for i in range(out_ref.shape[0] // two.shape[0]):
        out_ref[i * two.shape[0]:(i + 1) * two.shape[0], :] = two


def pack_call(embeddings, positives, counts):
    q_dev, width = embeddings.shape
    return pl.pallas_call(
        pack_kernel,
        out_shape=jax.ShapeDtypeStruct((SIZES["z"] * q_dev, width + EXTRA), jnp.bfloat16),
        in_specs=[SMEM, VMEM, VMEM],
        out_specs=VMEM,
        name="pack",
    )(counts, embeddings, positives)


def take_kernel(core_ref, all_ref, out_ref, sem):
    rows = out_ref.shape[0]
    part = rows // 4
    first = core_ref[0] * rows
    copies = [
        pltpu.make_async_copy(all_ref.at[pl.ds(pl.multiple_of(first + i * part, part), part), :], out_ref.at[pl.ds(i * part, part), :], sem.at[i])
        for i in range(4)
    ]
    for copy in copies:
        copy.start()
    for copy in copies:
        copy.wait()


def take_call(core, everything):
    rows, width = everything.shape
    return pl.pallas_call(
        take_kernel,
        out_shape=jax.ShapeDtypeStruct((rows // 2, width), everything.dtype),
        in_specs=[SMEM, HBM],
        out_specs=VMEM,
        scratch_shapes=[pltpu.SemaphoreType.DMA((4,))],
        compiler_params=pltpu.CompilerParams(vmem_limit_bytes=8 * 2**20),
        cost_estimate=pl.CostEstimate(flops=1000, bytes_accessed=1000, transcendentals=0),
        name="take",
    )(core, *in_hbm([everything]))


def close_kernel(got_ref, grad_ref, tail_ref):
    q_dev, width = grad_ref.shape
    step = 2 * q_dev
    total = got_ref[:step, :].astype(jnp.float32)
    for i in range(1, got_ref.shape[0] // step):
        total = total + got_ref[i * step:(i + 1) * step, :].astype(jnp.float32)
    total = total[:q_dev] + total[q_dev:]
    grad_ref[...] = total[:, :width].astype(jnp.bfloat16)
    tail_ref[...] = total[:, width:]


def close_call(got, q_dev, width):
    return pl.pallas_call(
        close_kernel,
        out_shape=(jax.ShapeDtypeStruct((q_dev, width), jnp.bfloat16), jax.ShapeDtypeStruct((q_dev, EXTRA), jnp.float32)),
        in_specs=[VMEM],
        out_specs=(VMEM, VMEM),
        name="close",
    )(got)


def lse_of(parts, axis=None):
    if axis is None:
        top = functools.reduce(jnp.maximum, parts)
        return top + jnp.log(functools.reduce(jnp.add, [jnp.exp(p - top) for p in parts]))
    top = jnp.max(parts, axis)
    return top + jnp.log(jnp.sum(jnp.exp(parts - jnp.expand_dims(top, axis)), axis))


def body(embeddings, classifier, positives, counts):
    q_dev, width = embeddings.shape
    labels = classifier.shape[0] // 2
    xh, core, xl, z, y = (lax.axis_index(a) for a in AXES)
    rank = (xl * 8 + z) * 4 + y
    base = (rank * 2 + core) * labels

    spread = lambda x, n: jnp.broadcast_to(x[None], (n,) + x.shape).reshape((n * x.shape[0],) + x.shape[1:])
    column = lax.all_to_all(pack_call(embeddings, positives, counts), "z", 0, 0, tiled=True)
    mine = lax.all_to_all(spread(column, 4), ("xh", "xl"), 0, 0, tiled=True)
    own = [mine, shift(mine, "y", -1), None, shift(mine, "y", 1)]
    relay = [(c * 4 + i, c * 4 + (i + 2 * c - 1) % 4) for c in range(2) for i in range(4)]
    own[2] = lax.ppermute(jnp.where(core == 0, own[1], own[3]), ("core", "y"), relay)
    w = take_call(core[None], classifier)
    rows = mine.shape[0]

    oth, parts = [None] * 4, [None] * 4
    for d in (0, 1, 3, 2):
        if d:
            done = (parts[1][1], parts[3][1]) if d == 2 else (hits[0][0],)
            own[d] = lax.optimization_barrier((own[d],) + done)[0]
        oth[d] = shift(own[d], "core", 1)
        parts[d] = scores_call(xh[None], own[d], oth[d], w)
        if d == 0:
            first = lax.optimization_barrier((own[0], parts[0][1]))[0]
            hits = [hits_call(jnp.stack([base, xh]), (first, oth[0]), w)]
    es, ms, ls, kept = zip(*parts)
    blocks = [b for pair in zip(own, oth) for b in pair]
    hits.append(hits_call(jnp.stack([base, xh]), blocks[2:4] + blocks[6:], w))
    m = jnp.concatenate(ms, 0)
    stat = jnp.concatenate(ls, 0)
    their, n = shift(stat, "core", 1), rows // 2
    their = jnp.concatenate([their[:, n:2 * n], their[:, :n], their[:, 3 * n:], their[:, 2 * n:3 * n]], 1)
    stat = lse_of([stat, their])
    at, stat = lax.optimization_barrier((jnp.stack([base, xh]), stat))
    hits.append(hits_call(at, blocks[4:6], w))
    others = lax.optimization_barrier((hits[2][0],) + tuple(shift(stat, "y", -d) for d in range(1, 4)))[1:]
    stat = lse_of([stat] + [jnp.roll(o, d, 0) for d, o in enumerate(others, 1)])
    stat = stat.reshape(8, rows)
    lse = lse_of(lax.all_to_all(jnp.broadcast_to(stat[None], (16, 8, rows)), ("xl", "z"), 0, 0, tiled=True), 0)

    lines = lse.reshape(4, 2 * rows)
    ps, (u_own, u_oth) = grad_call(0, y[None], hits, lines, m, es, w)
    f32 = lambda a: a.astype(jnp.float32)
    u = (f32(u_own) + f32(shift(u_oth, "core", 1))).astype(jnp.bfloat16)
    lines, u = lax.optimization_barrier((lines, u))
    ps += grad_call(1, y[None], hits, lines, m, es)[0]
    by_y = lax.all_to_all(u, "y", 0, 0, tiled=True)
    v = jnp.sum(f32(by_y).reshape((4, -1) + by_y.shape[1:]), 0).astype(jnp.bfloat16)
    class_grad, one = class_call(core[None], ps, kept, width, 0, None)
    second, v, one = lax.optimization_barrier((ps[0], v, one))
    got = lax.all_to_all(v, ("xl", "z"), 0, 0, tiled=True)
    class_grad, two = class_call(core[None], (second,) + tuple(ps[1:]), in_hbm(kept), width, 1, class_grad)
    two, got = lax.optimization_barrier((two, got))
    sent_parts = [shift(one, "core", 1), shift(two, "core", 1)]
    class_grad = place_call(core[None], sent_parts, class_grad)

    query_grad, tail = close_call(got, q_dev, width)
    pos_mean = jnp.sum(tail, 1)
    at = (xl * 8 + z) * q_dev
    loss = lax.dynamic_slice(lse, (0, at), (1, q_dev))[0] - pos_mean
    return loss, query_grad, class_grad


def solution(mesh):
    fine = Mesh(mesh.devices.reshape(tuple(SIZES[a] for a in AXES)), AXES)
    split = P(AXES, None)
    lab = P(("xl", "z", "y"), None)
    return jax.shard_map(
        body,
        mesh=fine,
        in_specs=(split, lab, split, P(AXES)),
        out_specs=(P(AXES), split, lab),
        check_vma=False,
    )
```

```python
import functools

import jax
import jax.numpy as jnp
from jax import lax
from jax.experimental import pallas as pl
from jax.experimental.pallas import tpu as pltpu
from jax.sharding import Mesh, PartitionSpec as P

AXES = ("xh", "core", "xl", "z", "y")
SIZES = {"xh": 2, "core": 2, "xl": 2, "z": 8, "y": 4}
EXTRA = 128
POS = 5
LO, MID, HI, CNT = 0, 8, 16, 24
VMEM = pl.BlockSpec(memory_space=pltpu.VMEM)
SMEM = pl.BlockSpec(memory_space=pltpu.SMEM)
ANY = pl.BlockSpec(memory_space=pl.ANY)
HBM = pl.BlockSpec(memory_space=pltpu.HBM)
NT = (((1,), (1,)), ((), ()))
TN = (((0,), (0,)), ((), ()))
LCH = 256
PROD = 1024
EXPO = 128
SPLIT = (3, 1)
PARTS = len(SPLIT)
EARLY = 2
CLASS = 512


def shift(x, axis, step):
    n = SIZES[axis]
    return lax.ppermute(x, axis, [(i, (i + step) % n) for i in range(n)])


def in_hbm(arrays):
    return [pltpu.with_memory_space_constraint(a, pltpu.HBM) for a in arrays]


def scores_kernel(xh_ref, own_ref, oth_ref, w_ref, e_ref, m_ref, l_ref, kept_ref, q_ref, s_ref, qt_ref, held_ref, sem, keep_sem):
    labels, width = w_ref.shape
    rows = own_ref.shape[0]
    both = 2 * rows
    copies = [pltpu.make_async_copy(a, q_ref.at[k], sem.at[k]) for k, a in enumerate((own_ref, oth_ref))]
    for copy in copies:
        copy.start()
    half = rows // 2
    keep = []
    for k, copy in enumerate(copies):
        copy.wait()
        for x in range(2):
            rowsx = pl.ds(pl.multiple_of((xh_ref[0] ^ x) * half, half), half)
            at = x * rows + k * half
            keep.append(pltpu.make_async_copy(q_ref.at[k, rowsx, pl.ds(0, width)], kept_ref.at[pl.ds(at, half), :], keep_sem.at[2 * k + x]))
            keep[-1].start()
            qt_ref[:, at:at + half] = q_ref[k, rowsx, :width].T

    def product(i, top):
        at = pl.multiple_of(i * PROD, PROD)
        s = jnp.dot(w_ref[pl.ds(at, PROD), :], qt_ref[...], preferred_element_type=jnp.float32)
        s_ref[pl.ds(at, PROD), :] = s
        return jnp.maximum(top, jnp.max(s.reshape(PROD // 16, 16, both), 0))

    top = lax.fori_loop(0, labels // PROD, product, jnp.full((16, both), -1e30, jnp.float32))
    top = jnp.max(top, 0, keepdims=True)

    def leave(i):
        part = pl.ds(pl.multiple_of(i * EXPO, EXPO), EXPO)
        return pltpu.make_async_copy(held_ref.at[part, :], e_ref.at[part, :], sem.at[i])

    def expo(i, total):
        at = pl.multiple_of(i * EXPO, EXPO)
        e = jnp.exp(s_ref[pl.ds(at, EXPO), :] - top)
        held_ref[pl.ds(at, EXPO), :] = e.astype(jnp.bfloat16)
        leave(i).start()
        return total + jnp.sum(e.reshape(EXPO // 16, 16, both), 0)

    total = lax.fori_loop(0, labels // EXPO, expo, jnp.zeros((16, both), jnp.float32))
    m_ref[...] = top
    l_ref[...] = top + jnp.log(jnp.sum(total, 0, keepdims=True))

    def gone(i, carry):
        leave(i).wait()
        return carry

    lax.fori_loop(0, labels // EXPO, gone, 0)
    for copy in keep:
        copy.wait()


def scores_call(xh, own, oth, w):
    rows = own.shape[0]
    labels, width = w.shape
    line = jax.ShapeDtypeStruct((1, 2 * rows), jnp.float32)
    return pl.pallas_call(
        scores_kernel,
        out_shape=(pltpu.HBM((labels, 2 * rows), jnp.bfloat16), line, line, pltpu.HBM((2 * rows, width), jnp.bfloat16)),
        in_specs=[SMEM, ANY, ANY, VMEM],
        out_specs=(HBM, VMEM, VMEM, HBM),
        scratch_shapes=[
            pltpu.VMEM((2,) + own.shape, jnp.bfloat16),
            pltpu.VMEM((labels, 2 * rows), jnp.float32),
            pltpu.VMEM((width, 2 * rows), jnp.bfloat16),
            pltpu.VMEM((labels, 2 * rows), jnp.bfloat16),
            pltpu.SemaphoreType.DMA((labels // EXPO,)),
            pltpu.SemaphoreType.DMA((4,)),
        ],
        compiler_params=pltpu.CompilerParams(vmem_limit_bytes=18 * 2**20),
        cost_estimate=pl.CostEstimate(flops=1000, bytes_accessed=1000, transcendentals=0),
        name="scores",
    )(xh, own, oth, w)


def hits_kernel(base_ref, *refs):
    count = len(refs) - 7
    sources = refs[:count]
    w_ref, n_ref, key_ref, s_ref, t_ref, blocks, sem = refs[count:]
    copies = [pltpu.make_async_copy(q, blocks.at[b], sem.at[b]) for b, q in enumerate(sources)]
    for copy in copies:
        copy.start()
    labels, width = w_ref.shape
    base = base_ref[0].astype(jnp.float32)
    half = sources[0].shape[0] // 2
    starts = [pl.multiple_of((base_ref[1] ^ x) * half, half) for x in range(2)]
    row = lax.broadcasted_iota(jnp.int32, (8, EXTRA), 0)
    col = lax.broadcasted_iota(jnp.int32, (8, EXTRA), 1)
    digits = jnp.where(col == row + LO, 1.0, jnp.where(col == row + MID, 128.0, jnp.where(col == row + HI, 16384.0, 0.0)))
    digits = jnp.where(row < POS, digits, 0.0).astype(jnp.bfloat16)
    counting = jnp.where(col == CNT, 1.0, 0.0).astype(jnp.bfloat16)
    big = 1e9
    rows = half
    slot = lax.broadcasted_iota(jnp.int32, (8, rows), 0)
    lane = lax.broadcasted_iota(jnp.int32, (8, rows), 1)
    keys, weights, most = [], [], jnp.int32(0)
    for part in range(2 * count):
        b = part // 2
        if part % 2 == 0:
            copies[b].wait()
        extra = blocks[b, pl.ds(starts[part % 2], half), width:]
        ids = lax.dot_general(digits, extra, NT, preferred_element_type=jnp.float32)
        cnt = lax.dot_general(counting, extra, NT, preferred_element_type=jnp.float32)
        valid = (slot.astype(jnp.float32) < cnt) & (slot < POS)
        ids = jnp.where(valid, ids, -1.0)
        same = jnp.zeros((8, rows), jnp.float32)
        again = jnp.zeros((8, rows), jnp.float32)
        for j in range(POS):
            eq = jnp.where(ids == ids[j:j + 1, :], 1.0, 0.0)
            same = same + eq
            again = again + jnp.where(slot > j, eq, 0.0)
        local = ids - base
        hit = valid & (local >= 0.0) & (local < float(labels)) & (again == 0.0)
        weights.append(same / cnt)
        keys.append(jnp.where(hit, (lane * 8 + slot).astype(jnp.float32) * float(labels) + local, big))
        n = jnp.sum(jnp.where(hit, 1.0, 0.0)).astype(jnp.int32)
        n_ref[part] = n
        most = jnp.maximum(most, n)
    r16 = lax.broadcasted_iota(jnp.int32, (16, width), 0)

    def step(i, keys):
        least = [jnp.min(k) for k in keys]
        found = [jnp.where(k < big, k, 0.0).astype(jnp.int32) for k in least]
        same = [k == kf for k, kf in zip(keys, least)]
        score, weight = [], []
        for part, k in enumerate(found):
            b = part // 2
            label = k & (labels - 1)
            query = lax.div(k, 8 * labels)
            qat = pl.multiple_of((query >> 4) << 4, 16)
            brow = pl.multiple_of(starts[part % 2] + qat, 16)
            lat = pl.multiple_of((label >> 4) << 4, 16)
            row_q = jnp.where(r16 == query - qat, blocks[b, pl.ds(brow, 16), :width].astype(jnp.float32), 0.0)
            row_w = jnp.where(r16 == label - lat, w_ref[pl.ds(lat, 16), :].astype(jnp.float32), 0.0)
            score.append(jnp.sum(row_w * jnp.sum(row_q, 0, keepdims=True)))
            weight.append(jnp.sum(jnp.where(same[part], weights[part], 0.0)))
        for part in range(2 * count):
            at = part * rows * POS + i
            key_ref[at] = found[part]
            s_ref[at] = score[part]
            t_ref[at] = weight[part]
        return tuple(jnp.where(t, big, k) for t, k in zip(same, keys))

    lax.fori_loop(0, most, step, tuple(keys))


def hits_call(base, blocks, w):
    count = len(blocks)
    total = count * blocks[0].shape[0] * POS
    return pl.pallas_call(
        hits_kernel,
        out_shape=(
            jax.ShapeDtypeStruct((2 * count,), jnp.int32),
            jax.ShapeDtypeStruct((total,), jnp.int32),
            jax.ShapeDtypeStruct((total,), jnp.float32),
            jax.ShapeDtypeStruct((total,), jnp.float32),
        ),
        in_specs=[SMEM] + [HBM] * count + [VMEM],
        out_specs=(SMEM,) * 4,
        scratch_shapes=[pltpu.VMEM((count,) + blocks[0].shape, jnp.bfloat16), pltpu.SemaphoreType.DMA((count,))],
        compiler_params=pltpu.CompilerParams(vmem_limit_bytes=16 * 2**20),
        cost_estimate=pl.CostEstimate(flops=1000, bytes_accessed=1000, transcendentals=0),
        name="hits",
    )(base, *in_hbm(blocks), w)


def grad_kernel(x, at_ref, na, ka, sa, ta, nb, kb, sb, tb, lse_ref, m_ref, e0, e1, e2, e3, *refs):
    labels, rows = e0.shape[0], e0.shape[1] // 2
    half = rows // 2
    if x == 0:
        w_ref, outs = refs[0], refs[1:5]
        own_ref, oth_ref, pos_ref = refs[5:8]
        width = w_ref.shape[1]
        pos_ref[...] = jnp.zeros_like(pos_ref)
    else:
        outs = refs[:4]
    held, sem = refs[-2:]
    lanes = slice(x * rows, (x + 1) * rows)
    ps = [held.at[d] for d in range(4)]
    copies = [pltpu.make_async_copy(e.at[:, lanes], p, sem.at[d]) for d, (e, p) in enumerate(zip((e0, e1, e2, e3), ps))]
    for copy in copies:
        copy.start()
    for d, p_ref in enumerate(ps):
        copies[d].wait()
        scale = jnp.exp(m_ref[d:d + 1, lanes] - lse_ref[d:d + 1, lanes])

        def scaled(i, carry):
            at = pl.multiple_of(i * 128, 128)
            p_ref[pl.ds(at, 128), :] = (p_ref[pl.ds(at, 128), :].astype(jnp.float32) * scale).astype(jnp.bfloat16)
            return carry

        lax.fori_loop(0, labels // 128, scaled, 0)

    r = lax.broadcasted_iota(jnp.int32, (16, half), 0)
    c = lax.broadcasted_iota(jnp.int32, (16, half), 1)
    c1 = lax.broadcasted_iota(jnp.int32, (1, EXTRA), 1)
    lists = []
    for b in range(8):
        group, spot = ((na, ka, sa, ta), b) if b < EARLY else ((nb, kb, sb, tb), b - EARLY)
        lists.append(group + (2 * spot + x,))
    most = jnp.int32(0)
    for n_ref, _, _, _, part in lists:
        most = jnp.maximum(most, n_ref[part])

    def patch(i, carry):
        todo = []
        for b, (n_ref, key_ref, s_ref, t_ref, part) in enumerate(lists):
            d, k = b // 2, b % 2
            at = part * half * POS + i
            live = i < n_ref[part]
            key, s, weight = jnp.where(live, key_ref[at], 0), s_ref[at], t_ref[at]
            label = key & (labels - 1)
            rest = lax.div(key, labels)
            slot = rest & 7
            query = rest >> 3
            lat = pl.multiple_of((label >> 4) << 4, 16)
            spot = (pl.ds(lat, 16), slice(k * half, (k + 1) * half))
            first = x * rows + k * half
            value = jnp.exp(s - lse_ref[d:d + 1, first:first + half]) - weight
            row = jnp.where(live, label - lat, -1)
            old = ps[d][spot].astype(jnp.float32)
            new = jnp.where((r == row) & (c == query), value, old).astype(jnp.bfloat16)
            into = pos = None
            if x == 0:
                full = jnp.full((1, EXTRA), s * weight, jnp.float32)
                high = full.astype(jnp.bfloat16).astype(jnp.float32)
                mid = (full - high).astype(jnp.bfloat16).astype(jnp.float32)
                low = full - high - mid
                put = jnp.where(c1 == slot, high, jnp.where(c1 == slot + 8, mid, jnp.where(c1 == slot + 16, low, 0.0)))
                into = (k, pl.ds(d * half + query, 1), slice(None))
                pos = pos_ref[into] + jnp.where(live, put, 0.0)
            todo.append((d, spot, new, into, pos))
        for d, spot, new, into, pos in todo:
            ps[d][spot] = new
            if x == 0:
                pos_ref[into] = pos
        return carry

    lax.fori_loop(0, most, patch, 0)
    copies = [pltpu.make_async_copy(p, out, sem.at[d]) for d, (p, out) in enumerate(zip(ps, outs))]
    for copy in copies:
        copy.start()
    if x == 0:
        for d, p_ref in enumerate(ps):
            u = lax.dot_general(p_ref[...], w_ref[...], TN, preferred_element_type=jnp.float32)
            to = pl.ds(pl.multiple_of(((at_ref[0] + d) & 3) * half, half), half)
            for k, out in enumerate((own_ref, oth_ref)):
                out[to, :width] = u[k * half:(k + 1) * half].astype(jnp.bfloat16)
                out[to, width:] = pos_ref[k, d * half:(d + 1) * half, :].astype(jnp.bfloat16)
    for copy in copies:
        copy.wait()


def grad_call(x, at, hits, lse, m, es, w=None):
    labels, rows = es[0].shape[0], es[0].shape[1] // 2
    p = (pltpu.HBM((labels, rows), jnp.bfloat16),) * 4
    held = [pltpu.VMEM((4, labels, rows), jnp.bfloat16), pltpu.SemaphoreType.DMA((4,))]
    more, specs, u, pos = (), [], (), []
    if x == 0:
        more, specs = (w,), [VMEM]
        u = (jax.ShapeDtypeStruct((2 * rows, w.shape[1] + EXTRA), jnp.bfloat16),) * 2
        pos = [pltpu.VMEM((2, 2 * rows, EXTRA), jnp.float32)]
    res = pl.pallas_call(
        functools.partial(grad_kernel, x),
        out_shape=p + u,
        in_specs=[SMEM] * 9 + [VMEM] * 2 + [HBM] * 4 + specs,
        out_specs=(HBM,) * 4 + (VMEM,) * len(u),
        scratch_shapes=pos + held,
        compiler_params=pltpu.CompilerParams(vmem_limit_bytes=20 * 2**20),
        cost_estimate=pl.CostEstimate(flops=4 * labels * rows * 4096 if x == 0 else 1000, bytes_accessed=2**23, transcendentals=0),
        name="rest_part" if x else "query_part",
    )(at, *hits[0], *hits[1], lse, m, *in_hbm(es), *more)
    return res[:4], res[4:]


def class_kernel(core_ref, *refs):
    ps, blocks = refs[:8], refs[8:12]
    out_ref, mine_ref = refs[-2:]
    rows = ps[0].shape[1]
    width = out_ref.shape[1]
    acc = None
    for d in range(4):
        for x in range(2):
            term = jnp.dot(ps[4 * x + d][...], blocks[d][x * rows:(x + 1) * rows, :], preferred_element_type=jnp.float32)
            acc = term if acc is None else acc + term
    done = acc.astype(jnp.bfloat16)
    out_ref[...] = done
    mine_ref[...] = done


def class_call(core, ps, blocks, width, part, before):
    labels = ps[0].shape[0]
    steps = labels // CLASS
    start, each = sum(SPLIT[:part]), SPLIT[part]
    rows = ps[0].shape[1]
    whole = lambda i, c: (0, 0)
    kept = () if before is None else (before,)
    return pl.pallas_call(
        class_kernel,
        out_shape=(jax.ShapeDtypeStruct((2 * labels, width), jnp.bfloat16), pltpu.HBM((each * CLASS, width), jnp.bfloat16)),
        grid_spec=pltpu.PrefetchScalarGridSpec(
            num_scalar_prefetch=1,
            grid=(each,),
            in_specs=[pl.BlockSpec((CLASS, rows), lambda i, c: (start + i, 0))] * 8
            + [pl.BlockSpec(blocks[0].shape, whole)] * 4
            + [HBM] * len(kept),
            out_specs=(
                pl.BlockSpec((CLASS, width), lambda i, c: (c[0] * steps + start + i, 0)),
                pl.BlockSpec((CLASS, width), lambda i, c: (i, 0)),
            ),
        ),
        input_output_aliases={13: 0} if kept else {},
        compiler_params=pltpu.CompilerParams(vmem_limit_bytes=24 * 2**20),
        cost_estimate=pl.CostEstimate(flops=16 * rows * each * CLASS * width, bytes_accessed=2**23, transcendentals=0),
        name="class_part",
    )(core, *in_hbm(ps), *blocks, *kept)


def place_kernel(core_ref, *refs):
    parts, out_ref, sem = refs[:PARTS], refs[-2], refs[-1]
    first = (1 - core_ref[0]) * (out_ref.shape[0] // 2)
    copies = [
        pltpu.make_async_copy(p, out_ref.at[pl.ds(pl.multiple_of(first + sum(SPLIT[:j]) * CLASS, CLASS), p.shape[0]), :], sem.at[j])
        for j, p in enumerate(parts)
    ]
    for copy in copies:
        copy.start()
    for copy in copies:
        copy.wait()


def place_call(core, parts, into):
    return pl.pallas_call(
        place_kernel,
        out_shape=jax.ShapeDtypeStruct(into.shape, into.dtype),
        in_specs=[SMEM] + [VMEM] * PARTS + [HBM],
        out_specs=HBM,
        scratch_shapes=[pltpu.SemaphoreType.DMA((PARTS,))],
        input_output_aliases={1 + PARTS: 0},
        compiler_params=pltpu.CompilerParams(vmem_limit_bytes=8 * 2**20),
        cost_estimate=pl.CostEstimate(flops=1000, bytes_accessed=1000, transcendentals=0),
        name="place",
    )(core, *parts, into)


def pack_kernel(counts_ref, emb_ref, pos_ref, out_ref):
    q_dev = emb_ref.shape[0]
    row = lax.broadcasted_iota(jnp.int32, (q_dev, EXTRA), 0)
    lane = lax.broadcasted_iota(jnp.int32, (q_dev, EXTRA), 1)
    extra = jnp.zeros((q_dev, EXTRA), jnp.int32)
    for j in range(POS):
        ids = pos_ref[:, j:j + 1]
        for first, digit in ((LO, ids & 127), (MID, (ids >> 7) & 127), (HI, ids >> 14)):
            extra = jnp.where(lane == first + j, digit, extra)
    for i in range(q_dev):
        extra = jnp.where((row == i) & (lane == CNT), counts_ref[i], extra)
    one = jnp.concatenate([emb_ref[...].astype(jnp.float32), extra.astype(jnp.float32)], 1)
    two = jnp.concatenate([one, one], 0).astype(jnp.bfloat16)
    for i in range(out_ref.shape[0] // two.shape[0]):
        out_ref[i * two.shape[0]:(i + 1) * two.shape[0], :] = two


def pack_call(embeddings, positives, counts):
    q_dev, width = embeddings.shape
    return pl.pallas_call(
        pack_kernel,
        out_shape=jax.ShapeDtypeStruct((SIZES["z"] * q_dev, width + EXTRA), jnp.bfloat16),
        in_specs=[SMEM, VMEM, VMEM],
        out_specs=VMEM,
        name="pack",
    )(counts, embeddings, positives)


def take_kernel(core_ref, all_ref, out_ref, sem):
    rows = out_ref.shape[0]
    part = rows // 4
    first = core_ref[0] * rows
    copies = [
        pltpu.make_async_copy(all_ref.at[pl.ds(pl.multiple_of(first + i * part, part), part), :], out_ref.at[pl.ds(i * part, part), :], sem.at[i])
        for i in range(4)
    ]
    for copy in copies:
        copy.start()
    for copy in copies:
        copy.wait()


def take_call(core, everything):
    rows, width = everything.shape
    return pl.pallas_call(
        take_kernel,
        out_shape=jax.ShapeDtypeStruct((rows // 2, width), everything.dtype),
        in_specs=[SMEM, HBM],
        out_specs=VMEM,
        scratch_shapes=[pltpu.SemaphoreType.DMA((4,))],
        compiler_params=pltpu.CompilerParams(vmem_limit_bytes=8 * 2**20),
        cost_estimate=pl.CostEstimate(flops=1000, bytes_accessed=1000, transcendentals=0),
        name="take",
    )(core, *in_hbm([everything]))


def close_kernel(got_ref, grad_ref, tail_ref):
    q_dev, width = grad_ref.shape
    step = 2 * q_dev
    total = got_ref[:step, :].astype(jnp.float32)
    for i in range(1, got_ref.shape[0] // step):
        total = total + got_ref[i * step:(i + 1) * step, :].astype(jnp.float32)
    total = total[:q_dev] + total[q_dev:]
    grad_ref[...] = total[:, :width].astype(jnp.bfloat16)
    tail_ref[...] = total[:, width:]


def close_call(got, q_dev, width):
    return pl.pallas_call(
        close_kernel,
        out_shape=(jax.ShapeDtypeStruct((q_dev, width), jnp.bfloat16), jax.ShapeDtypeStruct((q_dev, EXTRA), jnp.float32)),
        in_specs=[VMEM],
        out_specs=(VMEM, VMEM),
        name="close",
    )(got)


def lse_of(parts, axis=None):
    if axis is None:
        top = functools.reduce(jnp.maximum, parts)
        return top + jnp.log(functools.reduce(jnp.add, [jnp.exp(p - top) for p in parts]))
    top = jnp.max(parts, axis)
    return top + jnp.log(jnp.sum(jnp.exp(parts - jnp.expand_dims(top, axis)), axis))


def body(embeddings, classifier, positives, counts):
    q_dev, width = embeddings.shape
    labels = classifier.shape[0] // 2
    xh, core, xl, z, y = (lax.axis_index(a) for a in AXES)
    rank = (xl * 8 + z) * 4 + y
    base = (rank * 2 + core) * labels

    spread = lambda x, n: jnp.broadcast_to(x[None], (n,) + x.shape).reshape((n * x.shape[0],) + x.shape[1:])
    column = lax.all_to_all(pack_call(embeddings, positives, counts), "z", 0, 0, tiled=True)
    mine = lax.all_to_all(spread(column, 4), ("xh", "xl"), 0, 0, tiled=True)
    own = [mine, shift(mine, "y", -1), None, shift(mine, "y", 1)]
    relay = [(c * 4 + i, c * 4 + (i + 2 * c - 1) % 4) for c in range(2) for i in range(4)]
    own[2] = lax.ppermute(jnp.where(core == 0, own[1], own[3]), ("core", "y"), relay)
    w = take_call(core[None], classifier)
    rows = mine.shape[0]

    oth, parts = [None] * 4, [None] * 4
    for d in (0, 1, 3, 2):
        if d:
            done = (parts[1][1], parts[3][1]) if d == 2 else (hits[0][0],)
            own[d] = lax.optimization_barrier((own[d],) + done)[0]
        oth[d] = shift(own[d], "core", 1)
        parts[d] = scores_call(xh[None], own[d], oth[d], w)
        if d == 0:
            first = lax.optimization_barrier((own[0], parts[0][1]))[0]
            hits = [hits_call(jnp.stack([base, xh]), (first, oth[0]), w)]
    es, ms, ls, kept = zip(*parts)
    blocks = [b for pair in zip(own, oth) for b in pair]
    hits.append(hits_call(jnp.stack([base, xh]), blocks[EARLY:], w))
    m = jnp.concatenate(ms, 0)
    stat = jnp.concatenate(ls, 0)
    their, n = shift(stat, "core", 1), rows // 2
    their = jnp.concatenate([their[:, n:2 * n], their[:, :n], their[:, 3 * n:], their[:, 2 * n:3 * n]], 1)
    stat = lse_of([stat, their])
    stat = lse_of([stat] + [jnp.roll(shift(stat, "y", -d), d, 0) for d in range(1, 4)])
    stat = stat.reshape(8, rows)
    lse = lse_of(lax.all_to_all(jnp.broadcast_to(stat[None], (16, 8, rows)), ("xl", "z"), 0, 0, tiled=True), 0)

    lines = lse.reshape(4, 2 * rows)
    ps, (u_own, u_oth) = grad_call(0, y[None], hits, lines, m, es, w)
    f32 = lambda a: a.astype(jnp.float32)
    u = (f32(u_own) + f32(shift(u_oth, "core", 1))).astype(jnp.bfloat16)
    lines, u = lax.optimization_barrier((lines, u))
    ps += grad_call(1, y[None], hits, lines, m, es)[0]
    by_y = lax.all_to_all(u, "y", 0, 0, tiled=True)
    v = jnp.sum(f32(by_y).reshape((4, -1) + by_y.shape[1:]), 0).astype(jnp.bfloat16)
    class_grad, one = class_call(core[None], ps, kept, width, 0, None)
    second, v, one = lax.optimization_barrier((ps[0], v, one))
    got = lax.all_to_all(v, ("xl", "z"), 0, 0, tiled=True)
    class_grad, two = class_call(core[None], (second,) + tuple(ps[1:]), in_hbm(kept), width, 1, class_grad)
    two, got = lax.optimization_barrier((two, got))
    sent_parts = [shift(one, "core", 1), shift(two, "core", 1)]
    class_grad = place_call(core[None], sent_parts, class_grad)

    query_grad, tail = close_call(got, q_dev, width)
    pos_mean = jnp.sum(tail, 1)
    at = (xl * 8 + z) * q_dev
    loss = lax.dynamic_slice(lse, (0, at), (1, q_dev))[0] - pos_mean
    return loss, query_grad, class_grad


def solution(mesh):
    fine = Mesh(mesh.devices.reshape(tuple(SIZES[a] for a in AXES)), AXES)
    split = P(AXES, None)
    lab = P(("xl", "z", "y"), None)
    return jax.shard_map(
        body,
        mesh=fine,
        in_specs=(split, lab, split, P(AXES)),
        out_specs=(P(AXES), split, lab),
        check_vma=False,
    )
```
